256 devices in a mesh: fsdp: 64 (over y_hi, x, z), tp: 4 (over y_lo, core).
Axes of the slice: x: 4, y: 4 (y_hi: 2, y_lo: 2; y = y_hi * 2 + y_lo), z: 8, core: 2. Of those that a mesh axis runs over, the one named last changes fastest.
Arguments:
- tokens: bfloat16 [8192, 8192], P('fsdp', 'tp'), may hold values from -32 to 32
- gain: bfloat16 [8192], P('tp'), may hold values from 0.25 to 1.75
- w_query: bfloat16 [8192, 512], P('fsdp', 'tp'), may hold values from -0.055242717 to 0.055242717
- w_key: bfloat16 [8192, 128], P('fsdp'), may hold values from -1.2153398 to 1.2153398
- w_value: bfloat16 [8192, 128], P('fsdp'), may hold values from -0.0625 to 0.0625
- w_out: bfloat16 [512, 8192], P('tp', 'fsdp'), may hold values from -0.0625 to 0.0625
- cotangent: bfloat16 [8192, 8192], P('fsdp', 'tp'), may hold values from -6 to 6
Outputs:
- grad_input: float32 [8192, 8192], P('fsdp', 'tp')
- grad_gain: float32 [8192], P('tp')
- grad_query: float32 [8192, 512], P('fsdp', 'tp')
- grad_key: float32 [8192, 128], P('fsdp')
- grad_value: float32 [8192, 128], P('fsdp')
- grad_out: float32 [512, 8192], P('tp', 'fsdp')
The draws below stay inside these ranges and needn't reach their ends.
All inputs are finite; a program needn't handle non-finite values.
Results may differ from the reference program's by a relative error of at most 0.024.
Values may be sent and summed in bfloat16 or wider, within the bound.
No kernel may reach another device: no remote copies, remote signals or barrier semaphores. Data moves between devices by JAX's collectives and lax.ppermute only.
A program may use at most 128 MiB of HBM per device.

```python
import math
import jax
import jax.numpy as jnp
from jax import lax

D = 8192
HD = 128
TOK = 128
HEADS = 4
TOKENS = 8192
N_FSDP = 64


def draw_w_query(key, part):
    key = jax.random.fold_in(key, 11)
    own = jax.random.truncated_normal(key, -3.0, 3.0, (D, HEADS * HD), jnp.float32)
    return (own * D ** (-0.5)).astype(jnp.bfloat16)


def draw_w_key(key, part):
    key = jax.random.fold_in(key, 12)
    own = jax.random.truncated_normal(key, -3.0, 3.0, (D, HD), jnp.float32)
    return (own * D ** (-0.5)).astype(jnp.bfloat16)


def draw_tokens(key, part):
    key = jax.random.fold_in(key, 13)
    keys = jax.random.split(key, 3)
    base = jax.random.truncated_normal(keys[0], -3.0, 3.0, (TOKENS, D), jnp.float32)
    ramp = jnp.arange(D, dtype=jnp.float32) / D - 0.5
    column = jax.random.uniform(keys[1], (D,), jnp.float32, -0.5, 0.5)
    colscale = jnp.exp(column + ramp * math.log(3.0))
    rowscale = jnp.exp(jax.random.uniform(keys[2], (TOKENS, 1), jnp.float32, -0.5, 0.5))
    return (base * colscale * rowscale).astype(jnp.bfloat16)


def block_levels(rng, shape, pieces, least, top_value):
    def one(axis_at, parts):
        draws = jax.random.uniform(jax.random.fold_in(jax.random.fold_in(rng, 6), axis_at), (parts,), jnp.float32, least / len(pieces), top_value / len(pieces))
        return jnp.repeat(jnp.exp(draws), shape[axis_at] // parts).reshape((-1,) + (1,) * (len(shape) - axis_at - 1))

    loudness = one(*pieces[0])
    for cut in pieces[1:]:
        loudness = loudness * one(*cut)
    return loudness


def scatter_about(stream_key, extent, scale, limit, pieces=(), kind=jnp.bfloat16):
    factor_of = block_levels(stream_key, extent, pieces, -0.22, 0.18) if pieces else 1.0
    values = jax.random.normal(stream_key, extent, jnp.float32) * scale * factor_of
    return jnp.minimum(jnp.maximum(values, -limit), limit).astype(kind)


def setup_inputs(seed: int = 0) -> dict:
    splits = jax.random.split(jax.random.key(seed), 8)
    return {
        "tokens": draw_tokens(jax.random.fold_in(splits[7], 71), 0),
        "gain": jnp.clip(1.0 + 0.15 * jax.random.normal(splits[1], (D,), jnp.float32), 0.25, 1.75).astype(jnp.bfloat16),
        "w_query": draw_w_query(jax.random.fold_in(splits[7], 71), 0),
        "w_key": draw_w_key(jax.random.fold_in(splits[7], 71), 0),
        "w_value": scatter_about(splits[4], (D, HD), D ** -0.5, 0.0625, ((0, 64),)),
        "w_out": scatter_about(splits[5], (HEADS * HD, D), D ** -0.5, 0.0625, ((0, 4), (1, 64))),
        "cotangent": scatter_about(splits[6], (TOKENS, D), 1.0, 6.0, ((0, 64), (1, 4))),
    }


def attend(query, key_rows, value_rows, attn_grad):
    row_count = query.shape[0]
    heads = query.shape[1] // HD
    query_h = query.astype(jnp.float32).reshape(row_count, heads, HD)
    key_f = key_rows.astype(jnp.float32)
    value_f = value_rows.astype(jnp.float32)
    grad_h = attn_grad.astype(jnp.float32).reshape(row_count, heads, HD)
    scores = jnp.einsum('thd,sd->hts', query_h, key_f) * HD ** (-0.5)
    causal = jnp.arange(row_count)[:, None] >= jnp.arange(row_count)[None, :]
    scores = jnp.where(causal[None], scores, jnp.float32(-1e+30))
    row_peak = lax.optimization_barrier(jnp.max(scores, axis=-1, keepdims=True))
    shifted = jnp.exp(scores - row_peak)
    softmax_out = shifted / lax.optimization_barrier(jnp.sum(shifted, axis=-1, keepdims=True))
    rounded = softmax_out.astype(jnp.bfloat16).astype(jnp.float32)
    attended = jnp.einsum('hts,sd->thd', rounded, value_f).astype(jnp.bfloat16)
    dprob = jnp.einsum('thd,sd->hts', grad_h, value_f)
    dscore = softmax_out * (dprob - lax.optimization_barrier(jnp.sum(dprob * softmax_out, axis=-1, keepdims=True))) * HD ** (-0.5)
    dscore = dscore.astype(jnp.bfloat16).astype(jnp.float32)
    d_query = jnp.einsum('hts,sd->thd', dscore, key_f).astype(jnp.bfloat16)
    d_key = jnp.einsum('hts,thd->shd', dscore, query_h).astype(jnp.bfloat16)
    d_value = jnp.einsum('hts,thd->shd', rounded, grad_h).astype(jnp.bfloat16)
    width_all = heads * HD
    return (attended.reshape(row_count, width_all), d_query.reshape(row_count, width_all), d_key.reshape(row_count, width_all), d_value.reshape(row_count, width_all))

def group_step(pack):
    return attend(pack[0], pack[1], pack[2], pack[3])

def reference(tokens, gain, w_query, w_key, w_value, w_out, cotangent):
    values_f = tokens.astype(jnp.float32)
    inv_rms = lax.rsqrt(lax.optimization_barrier(jnp.mean(values_f * values_f, axis=-1, keepdims=True)) + 1e-05)
    unit_rows = values_f * inv_rms
    normed = (unit_rows * gain.astype(jnp.float32)).astype(jnp.bfloat16)
    query = jnp.dot(normed, w_query, preferred_element_type=jnp.float32).astype(jnp.bfloat16)
    key_rows = jnp.dot(normed, w_key, preferred_element_type=jnp.float32).astype(jnp.bfloat16)
    value_rows = jnp.dot(normed, w_value, preferred_element_type=jnp.float32).astype(jnp.bfloat16)
    attn_grad = jnp.dot(cotangent, w_out.T, preferred_element_type=jnp.float32).astype(jnp.bfloat16)
    shape_groups = (N_FSDP, TOK, HEADS * HD)
    shape_shared = (N_FSDP, TOK, HD)
    packed = (query.reshape(shape_groups), key_rows.reshape(shape_shared), value_rows.reshape(shape_shared), attn_grad.reshape(shape_groups))
    attended, d_query, d_key, d_value = lax.map(group_step, packed)
    attended = attended.reshape(TOKENS, HEADS * HD)
    d_query = d_query.reshape(TOKENS, HEADS * HD)
    d_key = d_key.reshape(TOKENS, HEADS * HD)
    d_value = d_value.reshape(TOKENS, HEADS * HD)
    summed = jnp.zeros((TOKENS, D), jnp.float32)
    for head in range(HEADS):
        begin = head * HD
        finish = begin + HD
        term = jnp.dot(d_query[:, begin:finish], w_query[:, begin:finish].T, preferred_element_type=jnp.float32)
        term = term + jnp.dot(d_key[:, begin:finish], w_key.T, preferred_element_type=jnp.float32)
        term = term + jnp.dot(d_value[:, begin:finish], w_value.T, preferred_element_type=jnp.float32)
        summed = summed + lax.optimization_barrier(term.astype(jnp.bfloat16)).astype(jnp.float32)
    scaled = summed * gain.astype(jnp.float32)
    row_mean = lax.optimization_barrier(jnp.mean(scaled * unit_rows, axis=-1, keepdims=True))
    grad_input = inv_rms * (scaled - unit_rows * row_mean)
    loss_scale = 1.0 / math.sqrt(TOKENS)
    grad_gain = lax.optimization_barrier(jnp.sum(summed * unit_rows, axis=0)) * loss_scale
    grad_query = jnp.dot(normed.T, d_query, preferred_element_type=jnp.float32) * loss_scale
    key_terms = jnp.dot(normed.T, d_key, preferred_element_type=jnp.float32)
    grad_key = lax.optimization_barrier(jnp.sum(key_terms.reshape(D, HEADS, HD), axis=1)) * loss_scale
    value_terms = jnp.dot(normed.T, d_value, preferred_element_type=jnp.float32)
    grad_value = lax.optimization_barrier(jnp.sum(value_terms.reshape(D, HEADS, HD), axis=1)) * loss_scale
    grad_out = jnp.dot(attended.T, cotangent, preferred_element_type=jnp.float32) * loss_scale
    return (grad_input, grad_gain, grad_query, grad_key, grad_value, grad_out)
```

```python
import math

import jax
import jax.numpy as jnp
from jax import lax
from jax.sharding import Mesh, PartitionSpec as P

HD = 128
NX = 4
NZ = 8
AXES = ("yh", "x", "z", "yl", "c")
FSDP = ("yh", "x", "z")
TP = ("yl", "c")
F32 = jnp.float32
BF16 = jnp.bfloat16


def flat(yh, x, z, yl, c):
    return (((yh * NX + x) * NZ + z) * 2 + yl) * 2 + c


def owner_perm(flip):
    pairs = []
    for yh in range(2):
        for x in range(NX):
            for z in range(NZ):
                for yl in range(2):
                    for c in range(2):
                        dest_x = (x % 2) * 2 + z // 4
                        dest_z = c * 4 + z % 4
                        pairs.append((flat(yh, x, z, yl, c), flat(yl ^ flip, dest_x, dest_z, yh, x // 2)))
    return pairs


def inverse(pairs):
    return [(d, s) for s, d in pairs]


def shift_x(value, by):
    return lax.ppermute(value, "x", [(i, (i + by) % NX) for i in range(NX)])


def swap(value, axis):
    return lax.ppermute(value, axis, [(0, 1), (1, 0)])


def dot(a, b, ca, cb):
    return lax.dot_general(a, b, (((ca,), (cb,)), ((), ())), preferred_element_type=F32)


def attend(query, key_rows, value_rows, attn_grad):
    rows = query.shape[0]
    scores = dot(query, key_rows, 1, 1) * HD ** (-0.5)
    causal = jnp.arange(rows)[:, None] >= jnp.arange(rows)[None, :]
    scores = jnp.where(causal, scores, jnp.float32(-1e30))
    peak = jnp.max(scores, axis=-1, keepdims=True)
    shifted = jnp.exp(scores - peak)
    softmax_out = shifted / jnp.sum(shifted, axis=-1, keepdims=True)
    rounded = softmax_out.astype(BF16)
    attended = dot(rounded, value_rows, 1, 0).astype(BF16)
    dprob = dot(attn_grad, value_rows, 1, 1)
    dscore = softmax_out * (dprob - jnp.sum(dprob * softmax_out, axis=-1, keepdims=True)) * HD ** (-0.5)
    dscore = dscore.astype(BF16)
    d_query = dot(dscore, key_rows, 1, 0).astype(BF16)
    d_key = dot(dscore, query, 0, 0)
    d_value = dot(rounded, attn_grad, 0, 0)
    return attended, d_query, d_key.astype(BF16), d_value.astype(BF16)


def local(tokens, gain, w_query, w_key, w_value, w_out, cotangent):
    rows, quarter = tokens.shape
    sub = quarter // NX
    width = quarter * 4
    yh, x, yl, c = (lax.axis_index(a) for a in ("yh", "x", "yl", "c"))
    head = yl * 2 + c
    loss_scale = 1.0 / math.sqrt(rows * 64)

    piece = rows // 4
    pack = jnp.concatenate(
        [
            w_query,
            w_out,
            lax.dynamic_slice_in_dim(w_key, head * piece, piece, 0),
            lax.dynamic_slice_in_dim(w_value, head * piece, piece, 0),
        ],
        axis=0,
    )
    same = lax.ppermute(pack, AXES, owner_perm(0))
    other = lax.ppermute(pack, AXES, owner_perm(1))
    first = jnp.where(yh == 0, same, other)
    second = jnp.where(yh == 0, other, same)
    both = jnp.stack([first, second])
    gathered = lax.all_gather(both, "z")
    gathered = gathered.reshape(2, 4, 2, *pack.shape)

    values_f = tokens.astype(F32)
    square_sum = jnp.sum(values_f * values_f, axis=-1, keepdims=True)
    inv_rms = lax.rsqrt(lax.psum(square_sum, TP) / width + 1e-05)
    unit_rows = values_f * inv_rms
    gain_f = gain.astype(F32)
    normed = (unit_rows * gain_f).astype(BF16)

    def spread(value):
        parts = [lax.dynamic_slice_in_dim(value, ((x + s) % NX) * sub, sub, 1) for s in range(NX)]
        return jnp.concatenate([parts[0]] + [shift_x(parts[s], s) for s in range(1, NX)], axis=0)

    cot_sw = spread(cotangent)
    normed_sw = spread(normed)

    def columns(side):
        block = gathered[side]
        w_q = jnp.transpose(block[:, :, :HD], (0, 2, 1, 3)).reshape(sub, 2 * HD)
        w_o = jnp.transpose(block[:, :, HD : 2 * HD], (1, 2, 0, 3)).reshape(2 * HD, sub)
        return w_q, w_o

    def shared(start):
        block = gathered[:, :, :, start : start + piece]
        return jnp.transpose(block, (1, 2, 0, 3, 4)).reshape(sub, HD)

    w_k, w_v = shared(2 * HD), shared(2 * HD + piece)
    w_mine = jnp.where(c == 0, w_k, w_v)
    w_theirs = jnp.where(c == 0, w_v, w_k)

    def partial(side, w_shared):
        w_q, w_o = columns(side)
        left = dot(normed_sw, jnp.concatenate([w_q, w_shared], axis=1), 1, 0)
        return jnp.concatenate([left, dot(cot_sw, w_o, 1, 1)], axis=1)

    theirs = partial(1 - c, w_theirs)
    mine = partial(c, w_mine)
    total = mine + swap(theirs, "c")
    total = total.reshape(NX, rows, 5 * HD)
    own = total[0]
    for s in range(1, NX):
        own = own + shift_x(total[s], -s)
    q01, kv, a01 = own[:, : 2 * HD], own[:, 2 * HD : 3 * HD], own[:, 3 * HD :]
    keep = jnp.where(yl == 0, jnp.concatenate([q01[:, :HD], a01[:, :HD]], 1), jnp.concatenate([q01[:, HD:], a01[:, HD:]], 1))
    give = jnp.where(yl == 0, jnp.concatenate([q01[:, HD:], a01[:, HD:]], 1), jnp.concatenate([q01[:, :HD], a01[:, :HD]], 1))
    got = swap(jnp.concatenate([give, kv], 1), "yl")
    final = (jnp.concatenate([keep, kv], 1) + got).astype(BF16)
    query, attn_grad, kv_mine = final[:, :HD], final[:, HD : 2 * HD], final[:, 2 * HD :]
    kv_theirs = swap(kv_mine, "c")
    key_rows = jnp.where(c == 0, kv_mine, kv_theirs)
    value_rows = jnp.where(c == 0, kv_theirs, kv_mine)

    attended, d_query, d_key, d_value = attend(query, key_rows, value_rows, attn_grad)

    sum_mine = jnp.where(c == 0, d_key, d_value).astype(F32)
    sum_mine = (sum_mine + swap(jnp.where(c == 0, d_value, d_key), "c").astype(F32)).astype(BF16)
    heads_own = jnp.concatenate([d_query, attended, sum_mine], axis=1)
    heads_x = jnp.concatenate([heads_own] + [shift_x(heads_own, s) for s in range(1, NX)], axis=0)
    heads_yl = swap(heads_x, "yl")
    lower = jnp.where(yl == 0, heads_x, heads_yl)
    upper = jnp.where(yl == 0, heads_yl, heads_x)
    shared_sum = (heads_x[:, 2 * HD :].astype(F32) + heads_yl[:, 2 * HD :].astype(F32)).astype(BF16)
    side_mine = jnp.concatenate([lower[:, :HD], upper[:, :HD], lower[:, HD : 2 * HD], upper[:, HD : 2 * HD], shared_sum], 1)
    side_theirs = swap(side_mine, "c")
    even = jnp.where(c == 0, side_mine, side_theirs)
    odd = jnp.where(c == 0, side_theirs, side_mine)
    d_heads = jnp.concatenate([even[:, : 2 * HD], odd[:, : 2 * HD], even[:, 4 * HD :], odd[:, 4 * HD :]], 1)
    attended_all = jnp.concatenate([even[:, 2 * HD : 4 * HD], odd[:, 2 * HD : 4 * HD]], 1)

    grads = dot(normed_sw, d_heads, 0, 0).astype(BF16)
    grad_o = dot(attended_all, cot_sw, 0, 0).astype(BF16)
    g_q = grads[:, : 4 * HD].reshape(4, HD, 2, 2, HD).transpose(2, 0, 3, 1, 4)
    g_o = grad_o.reshape(2, 2, HD, 4, HD).transpose(0, 3, 1, 2, 4)
    g_k = grads[:, 4 * HD : 5 * HD].reshape(4, 2, 2, piece, HD).transpose(2, 0, 1, 3, 4)
    g_v = grads[:, 5 * HD :].reshape(4, 2, 2, piece, HD).transpose(2, 0, 1, 3, 4)
    terms = jnp.concatenate([g_q, g_o, g_k, g_v], axis=3).reshape(NZ, 2, 2 * HD + 2 * piece, HD)
    scattered = lax.psum_scatter(terms, "z", scatter_dimension=0)
    to_same = jnp.where(yh == 0, scattered[0], scattered[1])
    to_other = jnp.where(yh == 0, scattered[1], scattered[0])
    summed_grads = lax.ppermute(to_same, AXES, inverse(owner_perm(0))).astype(F32)
    summed_grads = (summed_grads + lax.ppermute(to_other, AXES, inverse(owner_perm(1))).astype(F32)) * loss_scale
    grad_query = summed_grads[:HD]
    grad_out = summed_grads[HD : 2 * HD]
    shared_grads = lax.all_gather(summed_grads[2 * HD :].reshape(2, piece, HD), TP)
    grad_key = shared_grads[:, 0].reshape(rows, HD)
    grad_value = shared_grads[:, 1].reshape(rows, HD)

    w_even, o_even = columns(0)
    w_odd, o_odd = columns(1)
    w_all = jnp.concatenate([w_even, w_odd, w_k, w_v], axis=1)
    back = dot(d_heads, w_all, 1, 1).astype(BF16).reshape(NX, rows, sub)
    pieces = [back[0]] + [shift_x(back[s], -s) for s in range(1, NX)]
    summed = jnp.zeros((rows, quarter), BF16)
    for s in range(NX):
        summed = lax.dynamic_update_slice_in_dim(summed, pieces[s], ((x + s) % NX) * sub, 1)
    summed = summed.astype(F32)
    scaled = summed * gain_f
    row_mean = lax.psum(jnp.sum(scaled * unit_rows, axis=-1, keepdims=True), TP) / width
    grad_input = inv_rms * (scaled - unit_rows * row_mean)
    gain_term = jnp.sum(summed * unit_rows, axis=0)
    gain_terms = lax.all_to_all(jnp.broadcast_to(gain_term.reshape(1, 16, 128), (64, 16, 128)), FSDP, 0, 0)
    grad_gain = jnp.sum(gain_terms, axis=0).reshape(quarter) * loss_scale
    return (grad_input, grad_gain, grad_query, grad_key, grad_value, grad_out)


def solution(mesh):
    fine = Mesh(mesh.devices.reshape(2, NX, NZ, 2, 2), AXES)
    in_specs = (P(FSDP, TP), P(TP), P(FSDP, TP), P(FSDP, None), P(FSDP, None), P(TP, FSDP), P(FSDP, TP))
    out_specs = (P(FSDP, TP), P(TP), P(FSDP, TP), P(FSDP, None), P(FSDP, None), P(TP, FSDP))
    return jax.shard_map(local, mesh=fine, in_specs=in_specs, out_specs=out_specs, check_vma=False)
```

```python
import functools
import math

import jax
import jax.numpy as jnp
from jax import lax
from jax.experimental import pallas as pl
from jax.experimental.pallas import tpu as pltpu
from jax.sharding import Mesh, PartitionSpec as P

HD = 128
NX = 4
NZ = 8
AXES = ("yh", "x", "z", "yl", "c")
FSDP = ("yh", "x", "z")
TP = ("yl", "c")
F32 = jnp.float32
BF16 = jnp.bfloat16
PIECE = 32
BLOCK = 2 * HD + 2 * PIECE
GROWS = 16
VMEM = pl.BlockSpec(memory_space=pltpu.VMEM)
SMEM = pl.BlockSpec(memory_space=pltpu.SMEM)


def flat(yh, x, z, yl, c):
    return (((yh * NX + x) * NZ + z) * 2 + yl) * 2 + c


def owner_perm(flip):
    pairs = []
    for yh in range(2):
        for x in range(NX):
            for z in range(NZ):
                for yl in range(2):
                    for c in range(2):
                        dest_x = (x % 2) * 2 + z // 4
                        dest_z = c * 4 + z % 4
                        pairs.append((flat(yh, x, z, yl, c), flat(yl ^ flip, dest_x, dest_z, yh, x // 2)))
    return pairs


def inverse(pairs):
    return [(d, s) for s, d in pairs]


def shift_x(value, by):
    return lax.ppermute(value, "x", [(i, (i + by) % NX) for i in range(NX)])


def shift_z(value, by):
    return lax.ppermute(value, "z", [(i, (i + by) % NZ) for i in range(NZ)])


def shift_x_flip(value, by):
    return lax.ppermute(
        value, ("x", "yl"), [(2 * i + l, 2 * ((i + by) % NX) + 1 - l) for i in range(NX) for l in range(2)]
    )


def swap(value, axis):
    return lax.ppermute(value, axis, [(0, 1), (1, 0)])


def dot(a, b, ca, cb):
    return lax.dot_general(a, b, (((ca,), (cb,)), ((), ())), preferred_element_type=F32)


def lanes(start, size=HD):
    return pl.ds(pl.multiple_of(start, HD), size)


def call(body, outs, scratch, ids, *args):
    return pl.pallas_call(
        body,
        out_shape=[jax.ShapeDtypeStruct(s, d) for s, d in outs],
        in_specs=[SMEM] + [VMEM] * len(args),
        out_specs=[VMEM] * len(outs),
        scratch_shapes=[pltpu.VMEM(s, d) for s, d in scratch],
        compiler_params=pltpu.CompilerParams(vmem_limit_bytes=40 * 2**20),
    )(ids, *args)


def forward_kernel(ids, *refs):
    pieces, (normed, cot, mine, theirs, w_all, w_out) = refs[:9], refs[9:]
    z, yl, c = ids[0], ids[1], ids[2]

    def place(ref, base, zt, half):
        side, j = zt // 4, zt % 4
        rows = pl.ds(pl.multiple_of(j * HD, HD), HD)
        w_all[rows, lanes(side * 2 * HD + half * HD)] = ref[base : base + HD]
        w_out[side, half * HD : (half + 1) * HD, lanes(j * HD)] = ref[base + HD : base + 2 * HD]
        part = pl.ds(pl.multiple_of(j * HD + (2 * half + side) * PIECE, PIECE), PIECE)
        w_all[part, 4 * HD : 5 * HD] = ref[base + 2 * HD : base + 2 * HD + PIECE]
        w_all[part, 5 * HD : 6 * HD] = ref[base + 2 * HD + PIECE : base + BLOCK]

    for index, d in enumerate((0, -1, 1, -2, 2, -3, 3)):
        zt = (z + d + NZ) % NZ
        place(pieces[index], 0, zt, 0)
        place(pieces[index], BLOCK, zt, 1)
    far = (z + 4) % NZ
    place(pieces[7], 0, far, 0)
    place(pieces[8], 0, far, 1)

    for out, side in ((theirs, 1 - c), (mine, c)):
        w_q = w_all[:, lanes(side * 2 * HD, 2 * HD)]
        w_kv = w_all[:, lanes((4 + side) * HD)]
        w_o = w_out[side]
        for r in range(0, 512, 256):
            rows = slice(r, r + 256)
            q = dot(normed[rows], w_q, 1, 0)
            out[rows, lanes(yl * 3 * HD)] = q[:, :HD]
            out[rows, lanes((1 - yl) * 3 * HD)] = q[:, HD:]
            out[rows, 2 * HD : 3 * HD] = dot(normed[rows], w_kv, 1, 0)
            a = dot(cot[rows], w_o, 1, 1)
            out[rows, lanes((1 + yl * 3) * HD)] = a[:, :HD]
            out[rows, lanes((4 - yl * 3) * HD)] = a[:, HD:]


def chunk_kernel(ids, mine, got, *outs):
    for s in range(NX):
        rows = slice(s * HD, (s + 1) * HD)
        total = mine[rows] + got[rows]
        outs[s][...] = total[:, : 3 * HD]
        outs[NX + s][...] = total[:, 2 * HD :]


def side_kernel(ids, *refs):
    pieces, out = refs[:8], refs[8]
    yl = ids[1]
    for s in range(NX):
        rows = slice(s * HD, (s + 1) * HD)
        same, flip = pieces[s], pieces[NX + s]
        out[rows, lanes(yl * HD)] = same[:, :HD]
        out[rows, lanes((1 - yl) * HD)] = flip[:, :HD]
        out[rows, lanes((2 + yl) * HD)] = same[:, HD : 2 * HD]
        out[rows, lanes((3 - yl) * HD)] = flip[:, HD : 2 * HD]
        shared = same[:, 2 * HD :].astype(F32) + flip[:, 2 * HD :].astype(F32)
        out[rows, 4 * HD :] = shared.astype(BF16)


def gradient_kernel(ids, mine, theirs, normed, cot, tokens, inv, w_all, *refs):
    (t0, t1, m1, t2, m2, t3, m3, t4a, t4b, back, heads, attended, shared) = refs
    z, c = ids[0], ids[2]
    for ref, side in ((mine, c), (theirs, 1 - c)):
        heads[:, lanes(side * 2 * HD, 2 * HD)] = ref[:, : 2 * HD]
        attended[:, lanes(side * 2 * HD, 2 * HD)] = ref[:, 2 * HD : 4 * HD]
        heads[:, lanes((4 + side) * HD)] = ref[:, 4 * HD :]

    gain_sum = jnp.zeros((1, 4 * HD), F32)
    for s in range(NX):
        rows = slice(s * HD, (s + 1) * HD)
        term = dot(heads[rows], w_all[...], 1, 1)
        back[rows] = term.astype(BF16)
        unit = tokens[rows].astype(F32) * inv[rows]
        gain_sum = gain_sum + jnp.sum(term * unit, axis=0, keepdims=True)
    gain_rows = jnp.concatenate([gain_sum[:, j * HD : (j + 1) * HD] for j in range(4)], axis=0)
    high = gain_rows.astype(BF16).astype(F32)
    gain_rows = jnp.concatenate([high, gain_rows - high, jnp.zeros((8, HD), F32)], axis=0).astype(BF16)

    shared[...] = dot(normed[...], heads[:, 4 * HD :], 0, 0)
    for d, outs in ((0, (t0,)), (1, (t1,)), (-1, (m1,)), (3, (t3,)), (-3, (m3,)), (2, (t2,)), (-2, (m2,)), (4, (t4a, t4b))):
        zt = (z + d + NZ) % NZ
        side, j = zt // 4, zt % 4
        g_q = dot(normed[:, lanes(j * HD)], heads[:, lanes(side * 2 * HD, 2 * HD)], 0, 0).astype(BF16)
        g_o = dot(attended[:, lanes(side * 2 * HD, 2 * HD)], cot[:, lanes(j * HD)], 0, 0).astype(BF16)
        for half in range(2):
            if len(outs) == 1:
                out, base = outs[0], GROWS + half * BLOCK
            else:
                out, base = outs[half], GROWS * (1 - half)
            out[base : base + HD] = g_q[:, half * HD : (half + 1) * HD]
            out[base + HD : base + 2 * HD] = g_o[half * HD : (half + 1) * HD]
            part = shared[pl.ds(pl.multiple_of(j * HD + (2 * half + side) * PIECE, PIECE), PIECE), :].astype(BF16)
            out[base + 2 * HD : base + 2 * HD + PIECE] = part[:, :HD]
            out[base + 2 * HD + PIECE : base + BLOCK] = part[:, HD:]
        if len(outs) == 1:
            outs[0][:GROWS] = gain_rows
            outs[0][GROWS + 2 * BLOCK :] = gain_rows
        else:
            t4a[:GROWS] = gain_rows
            t4b[BLOCK:] = gain_rows


def relay_kernel(ids, t2, m2, a, b, c, d, e, f, up, down):
    g, n = GROWS, BLOCK
    up[:g] = e[:g]
    up[g : 2 * g] = c[:g]
    down[:g] = f[:g]
    down[g : 2 * g] = d[n:]
    total = t2[g : g + 2 * n].astype(F32) + a[g : g + 2 * n].astype(F32)
    up[2 * g : 2 * g + n] = (total[:n] + c[g:].astype(F32)).astype(BF16)
    up[2 * g + n :] = total[n:].astype(BF16)
    total = m2[g : g + 2 * n].astype(F32) + b[g : g + 2 * n].astype(F32)
    down[2 * g : 2 * g + n] = total[:n].astype(BF16)
    down[2 * g + n :] = (total[n:] + d[:n].astype(F32)).astype(BF16)


def finish_kernel(ids, t0, e, f, up, down, c, d, halves, gain_out):
    g, n = GROWS, BLOCK
    yh = ids[3]
    for half in range(2):
        mid = slice(g + half * n, g + (half + 1) * n)
        far = slice(2 * g + half * n, 2 * g + (half + 1) * n)
        total = t0[mid].astype(F32) + e[mid].astype(F32) + f[mid].astype(F32)
        total = total + up[far].astype(F32) + down[far].astype(F32)
        halves[(half + yh) % 2] = total.astype(BF16)
    rows = t0[:g].astype(F32) + e[:g].astype(F32) + f[:g].astype(F32) + c[:g].astype(F32) + d[n:].astype(F32)
    rows = rows + up[:g].astype(F32) + up[g : 2 * g].astype(F32) + down[:g].astype(F32)
    gain_out[...] = rows[:4] + rows[4:8]


def attend(query, key_rows, value_rows, attn_grad):
    rows = query.shape[0]
    scores = dot(query, key_rows, 1, 1) * HD ** (-0.5)
    causal = jnp.arange(rows)[:, None] >= jnp.arange(rows)[None, :]
    scores = jnp.where(causal, scores, jnp.float32(-1e30))
    peak = jnp.max(scores, axis=-1, keepdims=True)
    shifted = jnp.exp(scores - peak)
    softmax_out = shifted / jnp.sum(shifted, axis=-1, keepdims=True)
    rounded = softmax_out.astype(BF16)
    attended = dot(rounded, value_rows, 1, 0).astype(BF16)
    dprob = dot(attn_grad, value_rows, 1, 1)
    dscore = softmax_out * (dprob - jnp.sum(dprob * softmax_out, axis=-1, keepdims=True)) * HD ** (-0.5)
    dscore = dscore.astype(BF16)
    d_query = dot(dscore, key_rows, 1, 0).astype(BF16)
    d_key = dot(dscore, query, 0, 0)
    d_value = dot(rounded, attn_grad, 0, 0)
    return attended, d_query, d_key.astype(BF16), d_value.astype(BF16)


def local(tokens, gain, w_query, w_key, w_value, w_out, cotangent):
    rows, quarter = tokens.shape
    sub = quarter // NX
    width = quarter * 4
    yh, x, z, yl, c = (lax.axis_index(a) for a in AXES)
    ids = jnp.stack([z, yl, c, yh]).astype(jnp.int32)
    head = yl * 2 + c
    loss_scale = 1.0 / math.sqrt(rows * 64)

    pack = jnp.concatenate(
        [
            w_query,
            w_out,
            lax.dynamic_slice_in_dim(w_key, head * PIECE, PIECE, 0),
            lax.dynamic_slice_in_dim(w_value, head * PIECE, PIECE, 0),
        ],
        axis=0,
    )
    same = lax.ppermute(pack, AXES, owner_perm(0))
    other = lax.ppermute(pack, AXES, owner_perm(1))
    both = jnp.where(yh == 0, jnp.concatenate([same, other]), jnp.concatenate([other, same]))
    prev1, next1 = shift_z(both, 1), shift_z(both, -1)
    prev2, next2 = shift_z(both, 2), shift_z(both, -2)
    prev3, next3 = shift_z(prev2, 1), shift_z(next2, -1)
    far_a, far_b = shift_z(prev2[:BLOCK], 2), shift_z(next2[BLOCK:], -2)
    weights = (both, prev1, next1, prev2, next2, prev3, next3, far_a, far_b)

    own = jnp.concatenate([tokens, cotangent], axis=0)
    parts = [lax.dynamic_slice_in_dim(own, ((x + s) % NX) * sub, sub, 1) for s in range(NX)]
    parts = [parts[0]] + [shift_x(parts[s], s) for s in range(1, NX)]
    tokens_sw = jnp.concatenate([p[:rows] for p in parts], axis=0)
    cot_sw = jnp.concatenate([p[rows:] for p in parts], axis=0)

    values_f = tokens.astype(F32)
    square_sum = jnp.sum(values_f * values_f, axis=-1)
    square_sum = square_sum + swap(square_sum, "c")
    square_sum = square_sum + swap(square_sum, "yl")
    inv_flat = lax.rsqrt(square_sum / width + 1e-05)
    inv_sw = jnp.concatenate([inv_flat] + [shift_x(inv_flat, s) for s in range(1, NX)])[:, None]
    gain_f = gain.astype(F32)
    gain_sub = lax.dynamic_slice_in_dim(gain_f, x * sub, sub, 0)
    normed_sw = (tokens_sw.astype(F32) * inv_sw * gain_sub).astype(BF16)

    mine, theirs, w_all, _ = call(
        forward_kernel,
        [((512, 5 * HD), F32), ((512, 5 * HD), F32), ((sub, 6 * HD), BF16), ((2, 2 * HD, sub), BF16)],
        [],
        ids,
        *weights,
        normed_sw,
        cot_sw,
    )
    chunks = call(chunk_kernel, [((rows, 3 * HD), F32)] * 8, [], ids, mine, swap(theirs, "c"))
    keep = chunks[0]
    for s in range(1, NX):
        keep = keep + shift_x(chunks[s], -s)
    give = shift_x_flip(chunks[NX], 0)
    for s in range(1, NX):
        give = give + shift_x_flip(chunks[NX + s], -s)
    query = (keep[:, :HD] + give[:, HD : 2 * HD]).astype(BF16)
    attn_grad = (keep[:, HD : 2 * HD] + give[:, 2 * HD :]).astype(BF16)
    kv_mine = (keep[:, 2 * HD :] + give[:, :HD]).astype(BF16)
    kv_theirs = swap(kv_mine, "c")
    key_rows = jnp.where(c == 0, kv_mine, kv_theirs)
    value_rows = jnp.where(c == 0, kv_theirs, kv_mine)

    attended, d_query, d_key, d_value = attend(query, key_rows, value_rows, attn_grad)

    sum_mine = jnp.where(c == 0, d_key, d_value).astype(F32)
    sum_mine = (sum_mine + swap(jnp.where(c == 0, d_value, d_key), "c").astype(F32)).astype(BF16)
    heads_own = jnp.concatenate([d_query, attended, sum_mine], axis=1)
    heads_same = [heads_own] + [shift_x(heads_own, s) for s in range(1, NX)]
    heads_flip = [shift_x_flip(heads_own, s) for s in range(NX)]
    (side,) = call(side_kernel, [((512, 5 * HD), BF16)], [], ids, *heads_same, *heads_flip)

    long, short = (2 * GROWS + 2 * BLOCK, HD), (GROWS + BLOCK, HD)
    t0, t1, m1, t2, m2, t3, m3, t4a, t4b, back = call(
        gradient_kernel,
        [(long, BF16)] * 7 + [(short, BF16)] * 2 + [((512, sub), BF16)],
        [((512, 6 * HD), BF16), ((512, 4 * HD), BF16), ((sub, 2 * HD), F32)],
        ids,
        side,
        swap(side, "c"),
        normed_sw,
        cot_sw,
        tokens_sw,
        inv_sw,
        w_all,
    )
    a, b = shift_z(t3, 1), shift_z(m3, -1)
    c4, d4 = shift_z(t4a, 2), shift_z(t4b, -2)
    e, f = shift_z(t1, 1), shift_z(m1, -1)
    up, down = call(relay_kernel, [(long, BF16)] * 2, [], ids, t2, m2, a, b, c4, d4, e, f)
    up, down = shift_z(up, 2), shift_z(down, -2)
    halves, gain_z = call(
        finish_kernel, [((2, BLOCK, HD), BF16), ((4, HD), F32)], [], ids, t0, e, f, up, down, c4, d4
    )
    summed_grads = lax.ppermute(halves[0], AXES, inverse(owner_perm(0))).astype(F32)
    summed_grads = (summed_grads + lax.ppermute(halves[1], AXES, inverse(owner_perm(1))).astype(F32)) * loss_scale
    grad_query = summed_grads[:HD]
    grad_out = summed_grads[HD : 2 * HD]
    shared_grads = lax.all_gather(summed_grads[2 * HD :].reshape(2, PIECE, HD), TP)
    grad_key = shared_grads[:, 0].reshape(rows, HD)
    grad_value = shared_grads[:, 1].reshape(rows, HD)

    gain_z = (gain_z + swap(gain_z, "yh")).reshape(sub) * loss_scale
    grad_gain = jnp.zeros((quarter,), F32)
    for s in range(NX):
        part = shift_x(gain_z, s) if s else gain_z
        grad_gain = lax.dynamic_update_slice_in_dim(grad_gain, part, ((x - s) % NX) * sub, 0)

    pieces = [back[:rows]] + [shift_x(back[s * rows : (s + 1) * rows], -s) for s in range(1, NX)]
    summed = jnp.zeros((rows, quarter), BF16)
    for s in range(NX):
        summed = lax.dynamic_update_slice_in_dim(summed, pieces[s], ((x + s) % NX) * sub, 1)
    inv_rms = inv_flat[:, None]
    unit_rows = values_f * inv_rms
    scaled = summed.astype(F32) * gain_f
    row_sum = jnp.sum(scaled * unit_rows, axis=-1)
    row_sum = row_sum + swap(row_sum, "c")
    row_sum = row_sum + swap(row_sum, "yl")
    grad_input = inv_rms * (scaled - unit_rows * (row_sum[:, None] / width))
    return (grad_input, grad_gain, grad_query, grad_key, grad_value, grad_out)


def solution(mesh):
    fine = Mesh(mesh.devices.reshape(2, NX, NZ, 2, 2), AXES)
    in_specs = (P(FSDP, TP), P(TP), P(FSDP, TP), P(FSDP, None), P(FSDP, None), P(TP, FSDP), P(FSDP, TP))
    out_specs = (P(FSDP, TP), P(TP), P(FSDP, TP), P(FSDP, None), P(FSDP, None), P(TP, FSDP))
    return jax.shard_map(local, mesh=fine, in_specs=in_specs, out_specs=out_specs, check_vma=False)
```

```python
import functools
import math

import jax
import jax.numpy as jnp
from jax import lax
from jax.experimental import pallas as pl
from jax.experimental.pallas import tpu as pltpu
from jax.sharding import Mesh, PartitionSpec as P

HD = 128
NX = 4
NZ = 8
AXES = ("yh", "x", "z", "yl", "c")
FSDP = ("yh", "x", "z")
TP = ("yl", "c")
F32 = jnp.float32
BF16 = jnp.bfloat16
PIECE = 32
BLOCK = 2 * HD + 2 * PIECE
GROWS = 16
VMEM = pl.BlockSpec(memory_space=pltpu.VMEM)
SMEM = pl.BlockSpec(memory_space=pltpu.SMEM)


def flat(yh, x, z, yl, c):
    return (((yh * NX + x) * NZ + z) * 2 + yl) * 2 + c


def owner_perm(flip):
    pairs = []
    for yh in range(2):
        for x in range(NX):
            for z in range(NZ):
                for yl in range(2):
                    for c in range(2):
                        dest_x = (x % 2) * 2 + z // 4
                        dest_z = c * 4 + z % 4
                        pairs.append((flat(yh, x, z, yl, c), flat(yl ^ flip, dest_x, dest_z, yh, x // 2)))
    return pairs


def inverse(pairs):
    return [(d, s) for s, d in pairs]


def shift_x(value, by):
    return lax.ppermute(value, "x", [(i, (i + by) % NX) for i in range(NX)])


def shift_z(value, by):
    return lax.ppermute(value, "z", [(i, (i + by) % NZ) for i in range(NZ)])


def swap(value, axis):
    return lax.ppermute(value, axis, [(0, 1), (1, 0)])


def dot(a, b, ca, cb):
    return lax.dot_general(a, b, (((ca,), (cb,)), ((), ())), preferred_element_type=F32)


def lanes(start, size=HD):
    return pl.ds(pl.multiple_of(start, HD), size)


def call(body, outs, scratch, ids, *args):
    return pl.pallas_call(
        body,
        out_shape=[jax.ShapeDtypeStruct(s, d) for s, d in outs],
        in_specs=[SMEM] + [VMEM] * len(args),
        out_specs=[VMEM] * len(outs),
        scratch_shapes=[pltpu.VMEM(s, d) for s, d in scratch],
        compiler_params=pltpu.CompilerParams(vmem_limit_bytes=16 * 2**20),
    )(ids, *args)


def spread_kernel(ids, tokens, cot, extra, *outs):
    x = ids[4]
    rows = tokens.shape[0]
    for s in range(NX):
        block = lanes(((x + s) % NX) * 4 * HD, 4 * HD)
        outs[s][:rows] = tokens[:, block]
        outs[s][rows : 2 * rows] = cot[:, block]
        outs[s][2 * rows :] = extra[...]


def normalize_kernel(width, ids, *refs):
    parts, (gain, unit, normed, cot) = refs[:4], refs[4:]
    for s in range(NX):
        rows = slice(s * HD, (s + 1) * HD)
        terms = parts[s][2 * HD :, :HD].astype(F32)
        total = (terms[2:3] + terms[1:2]) + terms[0:1]
        column = jnp.transpose(jnp.broadcast_to(total, (HD, HD)))
        inv = lax.rsqrt(column / width + 1e-05)
        for j in range(4):
            cols = slice(j * HD, (j + 1) * HD)
            value = parts[s][:HD, cols].astype(F32) * inv
            unit[rows, cols] = value
            normed[rows, cols] = (value * gain[:, cols]).astype(BF16)
        cot[rows] = parts[s][HD : 2 * HD]


def forward_kernel(ids, *refs):
    pieces, (normed, cot, mine, theirs, w_all, w_out) = refs[:9], refs[9:]
    z, c = ids[0], ids[2]

    def place(ref, base, zt, half):
        side, j = zt // 4, zt % 4
        rows = pl.ds(pl.multiple_of(j * HD, HD), HD)
        w_all[rows, lanes(side * 2 * HD + half * HD)] = ref[base : base + HD]
        w_out[side, half * HD : (half + 1) * HD, lanes(j * HD)] = ref[base + HD : base + 2 * HD]
        part = pl.ds(pl.multiple_of(j * HD + (2 * half + side) * PIECE, PIECE), PIECE)
        w_all[part, 4 * HD : 5 * HD] = ref[base + 2 * HD : base + 2 * HD + PIECE]
        w_all[part, 5 * HD : 6 * HD] = ref[base + 2 * HD + PIECE : base + BLOCK]

    for index, d in enumerate((0, -1, 1, -2, 2, -3, 3)):
        zt = (z + d + NZ) % NZ
        place(pieces[index], 0, zt, 0)
        place(pieces[index], BLOCK, zt, 1)
    far = (z + 4) % NZ
    place(pieces[7], 0, far, 0)
    place(pieces[8], 0, far, 1)

    for out, side in ((theirs, 1 - c), (mine, c)):
        w_q = w_all[:, lanes(side * 2 * HD, 2 * HD)]
        w_kv = w_all[:, lanes((4 + side) * HD)]
        w_o = w_out[side]
        for r in range(0, 512, 256):
            rows = slice(r, r + 256)
            out[rows, : 2 * HD] = dot(normed[rows], w_q, 1, 0)
            out[rows, 2 * HD : 4 * HD] = dot(cot[rows], w_o, 1, 1)
            out[rows, 4 * HD :] = dot(normed[rows], w_kv, 1, 0)


def split_store(ref, total):
    for start, size, at in ((0, 2 * HD, 0), (4 * HD, HD, 6 * HD)):
        value = total[:, start : start + size]
        high = value.astype(BF16)
        ref[:, at : at + size] = high
        ref[:, at + size : at + 2 * size] = (value - high.astype(F32)).astype(BF16)
    ref[:, 4 * HD : 6 * HD] = total[:, 2 * HD : 4 * HD].astype(BF16)


def joined(ref):
    value = ref[...].astype(F32)
    return jnp.concatenate(
        [
            value[:, : 2 * HD] + value[:, 2 * HD : 4 * HD],
            value[:, 4 * HD : 6 * HD],
            value[:, 6 * HD : 7 * HD] + value[:, 7 * HD :],
        ],
        axis=1,
    )


def chunk_kernel(ids, mine, got, own, *outs):
    own[...] = mine[:HD] + got[:HD]
    for s in range(1, NX):
        rows = slice(s * HD, (s + 1) * HD)
        split_store(outs[s - 1], mine[rows] + got[rows])


def sum_kernel(ids, own, a, b, c, out):
    split_store(out, own[...] + joined(a) + joined(b) + joined(c))


def final_kernel(ids, mine, got, qa, kv):
    total = (joined(mine) + joined(got)).astype(BF16)
    qa[...] = total[:, : 4 * HD]
    kv[...] = total[:, 4 * HD :]


def attend_kernel(ids, qa, kv_mine, kv_theirs, out):
    first = ids[2] == 0
    mine, theirs = kv_mine[...].astype(F32), kv_theirs[...].astype(F32)
    key_rows = jnp.where(first, mine, theirs).astype(BF16)
    value_rows = jnp.where(first, theirs, mine).astype(BF16)
    causal = lax.broadcasted_iota(jnp.int32, (HD, HD), 0) >= lax.broadcasted_iota(jnp.int32, (HD, HD), 1)
    keys = jnp.zeros((HD, HD), F32)
    values = jnp.zeros((HD, HD), F32)
    for h in range(2):
        query = qa[:, h * HD : (h + 1) * HD]
        attn_grad = qa[:, (2 + h) * HD : (3 + h) * HD]
        scores = dot(query, key_rows, 1, 1) * HD ** (-0.5)
        scores = jnp.where(causal, scores, jnp.float32(-1e30))
        shifted = jnp.exp(scores - jnp.max(scores, axis=-1, keepdims=True))
        softmax_out = shifted / jnp.sum(shifted, axis=-1, keepdims=True)
        rounded = softmax_out.astype(BF16)
        dprob = dot(attn_grad, value_rows, 1, 1)
        dscore = softmax_out * (dprob - jnp.sum(dprob * softmax_out, axis=-1, keepdims=True)) * HD ** (-0.5)
        dscore = dscore.astype(BF16)
        out[:, h * HD : (h + 1) * HD] = dot(dscore, key_rows, 1, 0).astype(BF16)
        out[:, (2 + h) * HD : (3 + h) * HD] = dot(rounded, value_rows, 1, 0).astype(BF16)
        keys = keys + dot(dscore, query, 0, 0).astype(BF16).astype(F32)
        values = values + dot(rounded, attn_grad, 0, 0).astype(BF16).astype(F32)
    out[:, 4 * HD : 5 * HD] = keys.astype(BF16)
    out[:, 5 * HD :] = values.astype(BF16)


def gradient_kernel(ids, *refs):
    mine, theirs, (normed, cot, unit, w_all) = refs[:4], refs[4:8], refs[8:12]
    (t0, t1, m1, t2, m2, t3, m3, t4a, t4b, back, heads, attended, shared) = refs[12:]
    z, c = ids[0], ids[2]
    for s in range(NX):
        rows = slice(s * HD, (s + 1) * HD)
        for ref, side in ((mine[s], c), (theirs[s], 1 - c)):
            heads[rows, lanes(side * 2 * HD, 2 * HD)] = ref[:, : 2 * HD]
            attended[rows, lanes(side * 2 * HD, 2 * HD)] = ref[:, 2 * HD : 4 * HD]
        total = mine[s][:, 4 * HD :].astype(F32) + theirs[s][:, 4 * HD :].astype(F32)
        heads[rows, 4 * HD :] = total.astype(BF16)

    gain_sum = jnp.zeros((1, 4 * HD), F32)
    for s in range(NX):
        rows = slice(s * HD, (s + 1) * HD)
        term = dot(heads[rows], w_all[...], 1, 1)
        back[rows] = term.astype(BF16)
        gain_sum = gain_sum + jnp.sum(term * unit[rows], axis=0, keepdims=True)
    gain_rows = jnp.concatenate([gain_sum[:, j * HD : (j + 1) * HD] for j in range(4)], axis=0)
    high = gain_rows.astype(BF16).astype(F32)
    gain_rows = jnp.concatenate([high, gain_rows - high, jnp.zeros((8, HD), F32)], axis=0).astype(BF16)

    shared[...] = dot(normed[...], heads[:, 4 * HD :], 0, 0)
    for d, outs in ((0, (t0,)), (1, (t1,)), (-1, (m1,)), (3, (t3,)), (-3, (m3,)), (2, (t2,)), (-2, (m2,)), (4, (t4a, t4b))):
        zt = (z + d + NZ) % NZ
        side, j = zt // 4, zt % 4
        g_q = dot(normed[:, lanes(j * HD)], heads[:, lanes(side * 2 * HD, 2 * HD)], 0, 0).astype(BF16)
        g_o = dot(attended[:, lanes(side * 2 * HD, 2 * HD)], cot[:, lanes(j * HD)], 0, 0).astype(BF16)
        for half in range(2):
            if len(outs) == 1:
                out, base = outs[0], GROWS + half * BLOCK
            else:
                out, base = outs[half], GROWS * (1 - half)
            out[base : base + HD] = g_q[:, half * HD : (half + 1) * HD]
            out[base + HD : base + 2 * HD] = g_o[half * HD : (half + 1) * HD]
            part = shared[pl.ds(pl.multiple_of(j * HD + (2 * half + side) * PIECE, PIECE), PIECE), :].astype(BF16)
            out[base + 2 * HD : base + 2 * HD + PIECE] = part[:, :HD]
            out[base + 2 * HD + PIECE : base + BLOCK] = part[:, HD:]
        if len(outs) == 1:
            outs[0][:GROWS] = gain_rows
        else:
            t4a[:GROWS] = gain_rows
            t4b[BLOCK:] = gain_rows


def relay_kernel(ids, t2, m2, a, b, c, d, up, down):
    g, n = GROWS, BLOCK
    up[:g] = a[:g]
    up[g : 2 * g] = c[:g]
    down[:g] = b[:g]
    down[g : 2 * g] = d[n:]
    total = t2[g:].astype(F32) + a[g:].astype(F32)
    up[2 * g : 2 * g + n] = (total[:n] + c[g:].astype(F32)).astype(BF16)
    up[2 * g + n :] = total[n:].astype(BF16)
    total = m2[g:].astype(F32) + b[g:].astype(F32)
    down[2 * g : 2 * g + n] = total[:n].astype(BF16)
    down[2 * g + n :] = (total[n:] + d[:n].astype(F32)).astype(BF16)


def finish_kernel(ids, t0, e, f, up, down, c, d, same, other, gain_out):
    g, n = GROWS, BLOCK
    flip = ids[3]
    total = t0[g:].astype(F32) + e[g:].astype(F32) + f[g:].astype(F32)
    total = total + up[2 * g :].astype(F32) + down[2 * g :].astype(F32)
    same[...] = jnp.where(flip == 0, total[:n], total[n:]).astype(BF16)
    other[...] = jnp.where(flip == 0, total[n:], total[:n]).astype(BF16)
    rows = t0[:g].astype(F32) + e[:g].astype(F32) + f[:g].astype(F32) + c[:g].astype(F32) + d[n:].astype(F32)
    rows = rows + up[:g].astype(F32) + up[g : 2 * g].astype(F32) + down[:g].astype(F32)
    gain_out[...] = rows[:4] + rows[4:8]


def local(tokens, gain, w_query, w_key, w_value, w_out, cotangent):
    rows, quarter = tokens.shape
    sub = quarter // NX
    width = quarter * 4
    yh, x, z, yl, c = (lax.axis_index(a) for a in AXES)
    ids = jnp.stack([z, yl, c, yh, x]).astype(jnp.int32)
    head = yl * 2 + c
    loss_scale = 1.0 / math.sqrt(rows * 64)

    pack = jnp.concatenate(
        [
            w_query,
            w_out,
            lax.dynamic_slice_in_dim(w_key, head * PIECE, PIECE, 0),
            lax.dynamic_slice_in_dim(w_value, head * PIECE, PIECE, 0),
        ],
        axis=0,
    )
    same = lax.ppermute(pack, AXES, owner_perm(0))
    other = lax.ppermute(pack, AXES, owner_perm(1))
    both = jnp.where(yh == 0, jnp.concatenate([same, other]), jnp.concatenate([other, same]))
    prev2, next2 = shift_z(both, 2), shift_z(both, -2)
    prev1, next1 = shift_z(both, 1), shift_z(both, -1)
    prev3, next3 = shift_z(prev2, 1), shift_z(next2, -1)
    far_a, far_b = shift_z(prev2[:BLOCK], 2), shift_z(next2[BLOCK:], -2)
    weights = (both, prev1, next1, prev2, next2, prev3, next3, far_a, far_b)

    values_f = tokens.astype(F32)
    square_sum = jnp.sum(values_f * values_f, axis=-1)
    square_sum = square_sum + swap(square_sum, "c")
    square_sum = square_sum + swap(square_sum, "yl")
    high = lax.reduce_precision(square_sum, 8, 7)
    middle = lax.reduce_precision(square_sum - high, 8, 7)
    extra = jnp.stack([high, middle, square_sum - high - middle]).astype(BF16)
    extra = jnp.pad(extra, ((0, GROWS - 3), (0, sub - HD)))
    part_shape = ((2 * rows + GROWS, sub), BF16)
    parts = call(spread_kernel, [part_shape] * 4, [], ids, tokens, cotangent, extra)
    *parts, _ = lax.optimization_barrier((*parts, prev1))
    parts = [parts[0]] + [shift_x(parts[s], s) for s in range(1, NX)]
    gain_f = gain.astype(F32)
    gain_sub = lax.dynamic_slice_in_dim(gain_f, x * sub, sub, 0).reshape(1, sub)
    unit_sw, normed_sw, cot_sw = call(
        functools.partial(normalize_kernel, width),
        [((512, sub), F32), ((512, sub), BF16), ((512, sub), BF16)],
        [],
        ids,
        *parts,
        gain_sub,
    )

    mine, theirs, w_all, _ = call(
        forward_kernel,
        [((512, 5 * HD), F32), ((512, 5 * HD), F32), ((sub, 6 * HD), BF16), ((2, 2 * HD, sub), BF16)],
        [],
        ids,
        *weights,
        normed_sw,
        cot_sw,
    )
    split = ((rows, 8 * HD), BF16)
    own, *chunks = call(chunk_kernel, [((rows, 5 * HD), F32)] + [split] * 3, [], ids, mine, swap(theirs, "c"))
    chunks = [shift_x(chunks[s - 1], -s) for s in range(1, NX)]
    (partial,) = call(sum_kernel, [split], [], ids, own, *chunks)
    qa, kv = call(final_kernel, [((rows, 4 * HD), BF16), ((rows, HD), BF16)], [], ids, partial, swap(partial, "yl"))
    (heads,) = call(attend_kernel, [((rows, 6 * HD), BF16)], [], ids, qa, kv, swap(kv, "c"))
    heads = [heads] + [shift_x(heads, s) for s in range(1, NX)]

    long, short = (GROWS + 2 * BLOCK, HD), (GROWS + BLOCK, HD)
    t0, t1, m1, t2, m2, t3, m3, t4a, t4b, back = call(
        gradient_kernel,
        [(long, BF16)] * 7 + [(short, BF16)] * 2 + [((512, sub), BF16)],
        [((512, 6 * HD), BF16), ((512, 4 * HD), BF16), ((sub, 2 * HD), F32)],
        ids,
        *heads,
        *[swap(h, "c") for h in heads],
        normed_sw,
        cot_sw,
        unit_sw,
        w_all,
    )
    a, b = shift_z(t3, 1), shift_z(m3, -1)
    c4, d4 = shift_z(t4a, 2), shift_z(t4b, -2)
    e, f = shift_z(t1, 1), shift_z(m1, -1)
    up, down = call(relay_kernel, [((2 * GROWS + 2 * BLOCK, HD), BF16)] * 2, [], ids, t2, m2, a, b, c4, d4)
    up, down = shift_z(up, 2), shift_z(down, -2)
    to_same, to_other, gain_z = call(
        finish_kernel, [((BLOCK, HD), BF16)] * 2 + [((4, HD), F32)], [], ids, t0, e, f, up, down, c4, d4
    )
    summed_grads = lax.ppermute(to_same, AXES, inverse(owner_perm(0))).astype(F32)
    summed_grads = (summed_grads + lax.ppermute(to_other, AXES, inverse(owner_perm(1))).astype(F32)) * loss_scale
    grad_query = summed_grads[:HD]
    grad_out = summed_grads[HD : 2 * HD]
    shared_own = summed_grads[2 * HD :].reshape(1, 2, PIECE, HD)
    shared_c = swap(shared_own, "c")
    shared_own = jnp.where(c == 0, jnp.concatenate([shared_own, shared_c]), jnp.concatenate([shared_c, shared_own]))
    shared_yl = swap(shared_own, "yl")
    shared_own = jnp.where(yl == 0, jnp.concatenate([shared_own, shared_yl]), jnp.concatenate([shared_yl, shared_own]))
    grad_key = shared_own[:, 0].reshape(rows, HD)
    grad_value = shared_own[:, 1].reshape(rows, HD)

    gain_z = (gain_z + swap(gain_z, "yh")).reshape(sub) * loss_scale
    grad_gain = jnp.zeros((quarter,), F32)
    for s in range(NX):
        part = shift_x(gain_z, s) if s else gain_z
        grad_gain = lax.dynamic_update_slice_in_dim(grad_gain, part, ((x - s) % NX) * sub, 0)

    back, _ = lax.optimization_barrier((back, e))
    pieces = [back[:rows]] + [shift_x(back[s * rows : (s + 1) * rows], -s) for s in range(1, NX)]
    summed = jnp.zeros((rows, quarter), BF16)
    for s in range(NX):
        summed = lax.dynamic_update_slice_in_dim(summed, pieces[s], ((x + s) % NX) * sub, 1)
    inv_rms = lax.rsqrt(square_sum / width + 1e-05)[:, None]
    unit_rows = values_f * inv_rms
    scaled = summed.astype(F32) * gain_f
    row_sum = jnp.sum(scaled * unit_rows, axis=-1)
    row_sum = row_sum + swap(row_sum, "c")
    row_sum = row_sum + swap(row_sum, "yl")
    grad_input = inv_rms * (scaled - unit_rows * (row_sum[:, None] / width))
    return (grad_input, grad_gain, grad_query, grad_key, grad_value, grad_out)


def solution(mesh):
    fine = Mesh(mesh.devices.reshape(2, NX, NZ, 2, 2), AXES)
    in_specs = (P(FSDP, TP), P(TP), P(FSDP, TP), P(FSDP, None), P(FSDP, None), P(TP, FSDP), P(FSDP, TP))
    out_specs = (P(FSDP, TP), P(TP), P(FSDP, TP), P(FSDP, None), P(FSDP, None), P(TP, FSDP))
    return jax.shard_map(local, mesh=fine, in_specs=in_specs, out_specs=out_specs, check_vma=False)
```

```python
import functools
import math

import jax
import jax.numpy as jnp
from jax import lax
from jax.experimental import pallas as pl
from jax.experimental.pallas import tpu as pltpu
from jax.sharding import Mesh, PartitionSpec as P

HD = 128
NX = 4
NZ = 8
AXES = ("yh", "x", "z", "yl", "c")
FSDP = ("yh", "x", "z")
TP = ("yl", "c")
F32 = jnp.float32
BF16 = jnp.bfloat16
PIECE = 32
BLOCK = 2 * HD + 2 * PIECE
GROWS = 16
VMEM = pl.BlockSpec(memory_space=pltpu.VMEM)
SMEM = pl.BlockSpec(memory_space=pltpu.SMEM)


def flat(yh, x, z, yl, c):
    return (((yh * NX + x) * NZ + z) * 2 + yl) * 2 + c


def owner_perm():
    pairs = []
    for yh in range(2):
        for x in range(NX):
            for z in range(NZ):
                for yl in range(2):
                    for c in range(2):
                        dest_x = (x % 2) * 2 + z // 4
                        dest_z = c * 4 + z % 4
                        pairs.append((flat(yh, x, z, yl, c), flat(yl, dest_x, dest_z, yh, x // 2)))
    return pairs


def inverse(pairs):
    return [(d, s) for s, d in pairs]


def shift_x(value, by):
    return lax.ppermute(value, "x", [(i, (i + by) % NX) for i in range(NX)])


def swap(value, axis):
    return lax.ppermute(value, axis, [(0, 1), (1, 0)])


def dot(a, b, ca, cb):
    return lax.dot_general(a, b, (((ca,), (cb,)), ((), ())), preferred_element_type=F32)


def lanes(start, size=HD):
    return pl.ds(pl.multiple_of(start, HD), size)


def call(body, outs, scratch, ids, *args):
    return pl.pallas_call(
        body,
        out_shape=[jax.ShapeDtypeStruct(s, d) for s, d in outs],
        in_specs=[SMEM] + [VMEM] * len(args),
        out_specs=[VMEM] * len(outs),
        scratch_shapes=[pltpu.VMEM(s, d) for s, d in scratch],
        compiler_params=pltpu.CompilerParams(vmem_limit_bytes=16 * 2**20),
    )(ids, *args)


def spread_kernel(ids, tokens, cot, extra, *outs):
    x = ids[4]
    rows = tokens.shape[0]
    for s in range(NX):
        block = lanes(((x + s) % NX) * 4 * HD, 4 * HD)
        outs[s][:rows] = tokens[:, block]
        outs[s][rows : 2 * rows] = cot[:, block]
        outs[s][2 * rows :] = extra[...]


def normalize_kernel(width, ids, *refs):
    parts, (gain, unit, normed, cot) = refs[:4], refs[4:]
    for s in range(NX):
        rows = slice(s * HD, (s + 1) * HD)
        terms = parts[s][2 * HD :, :HD].astype(F32)
        total = (terms[2:3] + terms[1:2]) + terms[0:1]
        column = jnp.transpose(jnp.broadcast_to(total, (HD, HD)))
        inv = lax.rsqrt(column / width + 1e-05)
        for j in range(4):
            cols = slice(j * HD, (j + 1) * HD)
            value = parts[s][:HD, cols].astype(F32) * inv
            unit[rows, cols] = value
            normed[rows, cols] = (value * gain[:, cols]).astype(BF16)
        cot[rows] = parts[s][HD : 2 * HD]


def forward_kernel(ids, pieces, normed, cot, mine, theirs, w_all, w_out):
    c = ids[2]
    for index in range(16):
        half, side, j = index // 8, index // 4 % 2, index % 4
        rows = slice(j * HD, (j + 1) * HD)
        col = (side * 2 + half) * HD
        w_all[rows, col : col + HD] = pieces[index, :HD]
        w_out[side, half * HD : (half + 1) * HD, rows] = pieces[index, HD : 2 * HD]
        at = j * HD + (2 * half + side) * PIECE
        w_all[at : at + PIECE, 4 * HD : 5 * HD] = pieces[index, 2 * HD : 2 * HD + PIECE]
        w_all[at : at + PIECE, 5 * HD : 6 * HD] = pieces[index, 2 * HD + PIECE :]

    for out, side in ((theirs, 1 - c), (mine, c)):
        w_q = w_all[:, lanes(side * 2 * HD, 2 * HD)]
        w_kv = w_all[:, lanes((4 + side) * HD)]
        w_o = w_out[side]
        for r in range(0, 512, 256):
            rows = slice(r, r + 256)
            out[rows, : 2 * HD] = dot(normed[rows], w_q, 1, 0)
            out[rows, 2 * HD : 4 * HD] = dot(cot[rows], w_o, 1, 1)
            out[rows, 4 * HD :] = dot(normed[rows], w_kv, 1, 0)


def split_store(ref, total):
    for start, size, at in ((0, 2 * HD, 0), (4 * HD, HD, 6 * HD)):
        value = total[:, start : start + size]
        high = value.astype(BF16)
        ref[:, at : at + size] = high
        ref[:, at + size : at + 2 * size] = (value - high.astype(F32)).astype(BF16)
    ref[:, 4 * HD : 6 * HD] = total[:, 2 * HD : 4 * HD].astype(BF16)


def joined(ref):
    value = ref[...].astype(F32)
    return jnp.concatenate(
        [
            value[:, : 2 * HD] + value[:, 2 * HD : 4 * HD],
            value[:, 4 * HD : 6 * HD],
            value[:, 6 * HD : 7 * HD] + value[:, 7 * HD :],
        ],
        axis=1,
    )


def chunk_kernel(ids, mine, got, own, *outs):
    own[...] = mine[:HD] + got[:HD]
    for s in range(1, NX):
        rows = slice(s * HD, (s + 1) * HD)
        split_store(outs[s - 1], mine[rows] + got[rows])


def sum_kernel(ids, own, a, b, c, out):
    split_store(out, own[...] + joined(a) + joined(b) + joined(c))


def final_kernel(ids, mine, got, qa, kv):
    total = (joined(mine) + joined(got)).astype(BF16)
    qa[...] = total[:, : 4 * HD]
    kv[...] = total[:, 4 * HD :]


def attend_kernel(ids, qa, kv_mine, kv_theirs, out):
    first = ids[2] == 0
    mine, theirs = kv_mine[...].astype(F32), kv_theirs[...].astype(F32)
    key_rows = jnp.where(first, mine, theirs).astype(BF16)
    value_rows = jnp.where(first, theirs, mine).astype(BF16)
    causal = lax.broadcasted_iota(jnp.int32, (HD, HD), 0) >= lax.broadcasted_iota(jnp.int32, (HD, HD), 1)
    keys = jnp.zeros((HD, HD), F32)
    values = jnp.zeros((HD, HD), F32)
    for h in range(2):
        query = qa[:, h * HD : (h + 1) * HD]
        attn_grad = qa[:, (2 + h) * HD : (3 + h) * HD]
        scores = dot(query, key_rows, 1, 1) * HD ** (-0.5)
        scores = jnp.where(causal, scores, jnp.float32(-1e30))
        shifted = jnp.exp(scores - jnp.max(scores, axis=-1, keepdims=True))
        softmax_out = shifted / jnp.sum(shifted, axis=-1, keepdims=True)
        rounded = softmax_out.astype(BF16)
        dprob = dot(attn_grad, value_rows, 1, 1)
        dscore = softmax_out * (dprob - jnp.sum(dprob * softmax_out, axis=-1, keepdims=True)) * HD ** (-0.5)
        dscore = dscore.astype(BF16)
        out[:, h * HD : (h + 1) * HD] = dot(dscore, key_rows, 1, 0).astype(BF16)
        out[:, (2 + h) * HD : (3 + h) * HD] = dot(rounded, value_rows, 1, 0).astype(BF16)
        keys = keys + dot(dscore, query, 0, 0).astype(BF16).astype(F32)
        values = values + dot(rounded, attn_grad, 0, 0).astype(BF16).astype(F32)
    out[:, 4 * HD : 5 * HD] = keys.astype(BF16)
    out[:, 5 * HD :] = values.astype(BF16)


def gradient_kernel(ids, *refs):
    mine, theirs, (normed, cot, unit, w_all) = refs[:4], refs[4:8], refs[8:12]
    back, (terms, heads, attended, shared) = refs[12:16], refs[16:]
    c = ids[2]
    for s in range(NX):
        rows = slice(s * HD, (s + 1) * HD)
        for ref, side in ((mine[s], c), (theirs[s], 1 - c)):
            heads[rows, lanes(side * 2 * HD, 2 * HD)] = ref[:, : 2 * HD]
            attended[rows, lanes(side * 2 * HD, 2 * HD)] = ref[:, 2 * HD : 4 * HD]
        total = mine[s][:, 4 * HD :].astype(F32) + theirs[s][:, 4 * HD :].astype(F32)
        heads[rows, 4 * HD :] = total.astype(BF16)

    gain_sum = jnp.zeros((1, 4 * HD), F32)
    for s in range(NX):
        rows = slice(s * HD, (s + 1) * HD)
        term = dot(heads[rows], w_all[...], 1, 1)
        back[s][...] = term.astype(BF16)
        gain_sum = gain_sum + jnp.sum(term * unit[rows], axis=0, keepdims=True)
    gain_rows = jnp.concatenate([gain_sum[:, j * HD : (j + 1) * HD] for j in range(4)], axis=0)
    high = gain_rows.astype(BF16).astype(F32)
    gain_rows = jnp.concatenate([high, gain_rows - high, jnp.zeros((8, HD), F32)], axis=0).astype(BF16)

    shared[...] = dot(normed[...], heads[:, 4 * HD :], 0, 0)
    for side in range(2):
        cols = slice(side * 2 * HD, (side + 1) * 2 * HD)
        for j in range(4):
            block = slice(j * HD, (j + 1) * HD)
            g_q = dot(normed[:, block], heads[:, cols], 0, 0).astype(BF16)
            g_o = dot(attended[:, cols], cot[:, block], 0, 0).astype(BF16)
            for half in range(2):
                out = terms.at[half * 8 + side * 4 + j]
                out[:HD] = g_q[:, half * HD : (half + 1) * HD]
                out[HD : 2 * HD] = g_o[half * HD : (half + 1) * HD]
                at = j * HD + (2 * half + side) * PIECE
                part = shared[at : at + PIECE].astype(BF16)
                out[2 * HD : 2 * HD + PIECE] = part[:, :HD]
                out[2 * HD + PIECE : BLOCK] = part[:, HD:]
                out[BLOCK:] = gain_rows


def finish_kernel(ids, terms, sums, gain_out):
    total = terms[0].astype(F32)
    for index in range(1, 16):
        total = total + terms[index].astype(F32)
    sums[...] = total[:BLOCK].astype(BF16)
    gain_out[...] = total[BLOCK : BLOCK + 4] + total[BLOCK + 4 : BLOCK + 8]


def local(tokens, gain, w_query, w_key, w_value, w_out, cotangent):
    rows, quarter = tokens.shape
    sub = quarter // NX
    width = quarter * 4
    yh, x, z, yl, c = (lax.axis_index(a) for a in AXES)
    ids = jnp.stack([z, yl, c, yh, x]).astype(jnp.int32)
    head = yl * 2 + c
    loss_scale = 1.0 / math.sqrt(rows * 64)

    pack = jnp.concatenate(
        [
            w_query,
            w_out,
            lax.dynamic_slice_in_dim(w_key, head * PIECE, PIECE, 0),
            lax.dynamic_slice_in_dim(w_value, head * PIECE, PIECE, 0),
        ],
        axis=0,
    )
    pack = lax.ppermute(pack, AXES, owner_perm())
    weights = lax.all_to_all(jnp.broadcast_to(pack, (16, *pack.shape)), ("yh", "z"), 0, 0)

    values_f = tokens.astype(F32)
    square_sum = jnp.sum(values_f * values_f, axis=-1)
    square_sum = square_sum + swap(square_sum, "c")
    square_sum = square_sum + swap(square_sum, "yl")
    high = lax.reduce_precision(square_sum, 8, 7)
    middle = lax.reduce_precision(square_sum - high, 8, 7)
    extra = jnp.stack([high, middle, square_sum - high - middle]).astype(BF16)
    extra = jnp.pad(extra, ((0, GROWS - 3), (0, sub - HD)))
    part_shape = ((2 * rows + GROWS, sub), BF16)
    parts = call(spread_kernel, [part_shape] * 4, [], ids, tokens, cotangent, extra)
    parts = [parts[0]] + [shift_x(parts[s], s) for s in range(1, NX)]
    gain_f = gain.astype(F32)
    gain_sub = lax.dynamic_slice_in_dim(gain_f, x * sub, sub, 0).reshape(1, sub)
    unit_sw, normed_sw, cot_sw = call(
        functools.partial(normalize_kernel, width),
        [((512, sub), F32), ((512, sub), BF16), ((512, sub), BF16)],
        [],
        ids,
        *parts,
        gain_sub,
    )

    mine, theirs, w_all, _ = call(
        forward_kernel,
        [((512, 5 * HD), F32), ((512, 5 * HD), F32), ((sub, 6 * HD), BF16), ((2, 2 * HD, sub), BF16)],
        [],
        ids,
        weights,
        normed_sw,
        cot_sw,
    )
    split = ((rows, 8 * HD), BF16)
    own, *chunks = call(chunk_kernel, [((rows, 5 * HD), F32)] + [split] * 3, [], ids, mine, swap(theirs, "c"))
    chunks = [shift_x(chunks[s - 1], -s) for s in range(1, NX)]
    (partial,) = call(sum_kernel, [split], [], ids, own, *chunks)
    qa, kv = call(final_kernel, [((rows, 4 * HD), BF16), ((rows, HD), BF16)], [], ids, partial, swap(partial, "yl"))
    (heads,) = call(attend_kernel, [((rows, 6 * HD), BF16)], [], ids, qa, kv, swap(kv, "c"))
    heads = [heads] + [shift_x(heads, s) for s in range(1, NX)]

    block = (16, BLOCK + GROWS, HD)
    *back, terms = call(
        gradient_kernel,
        [((rows, sub), BF16)] * 4 + [(block, BF16)],
        [((512, 6 * HD), BF16), ((512, 4 * HD), BF16), ((sub, 2 * HD), F32)],
        ids,
        *heads,
        *[swap(h, "c") for h in heads],
        normed_sw,
        cot_sw,
        unit_sw,
        w_all,
    )
    terms = lax.all_to_all(terms, ("yh", "z"), 0, 0)
    sums, gain_z = call(finish_kernel, [((BLOCK, HD), BF16), ((4, HD), F32)], [], ids, terms)
    summed_grads = lax.ppermute(sums, AXES, inverse(owner_perm())).astype(F32) * loss_scale
    grad_query = summed_grads[:HD]
    grad_out = summed_grads[HD : 2 * HD]
    shared_own = summed_grads[2 * HD :].reshape(1, 2, PIECE, HD)
    shared_c = swap(shared_own, "c")
    shared_own = jnp.where(c == 0, jnp.concatenate([shared_own, shared_c]), jnp.concatenate([shared_c, shared_own]))
    shared_yl = swap(shared_own, "yl")
    shared_own = jnp.where(yl == 0, jnp.concatenate([shared_own, shared_yl]), jnp.concatenate([shared_yl, shared_own]))
    grad_key = shared_own[:, 0].reshape(rows, HD)
    grad_value = shared_own[:, 1].reshape(rows, HD)

    gain_z = gain_z.reshape(sub) * loss_scale
    grad_gain = jnp.zeros((quarter,), F32)
    for s in range(NX):
        part = shift_x(gain_z, s) if s else gain_z
        grad_gain = lax.dynamic_update_slice_in_dim(grad_gain, part, ((x - s) % NX) * sub, 0)

    pieces = [back[0]] + [shift_x(back[s], -s) for s in range(1, NX)]
    summed = jnp.zeros((rows, quarter), BF16)
    for s in range(NX):
        summed = lax.dynamic_update_slice_in_dim(summed, pieces[s], ((x + s) % NX) * sub, 1)
    inv_rms = lax.rsqrt(square_sum / width + 1e-05)[:, None]
    unit_rows = values_f * inv_rms
    scaled = summed.astype(F32) * gain_f
    row_sum = jnp.sum(scaled * unit_rows, axis=-1)
    row_sum = row_sum + swap(row_sum, "c")
    row_sum = row_sum + swap(row_sum, "yl")
    grad_input = inv_rms * (scaled - unit_rows * (row_sum[:, None] / width))
    return (grad_input, grad_gain, grad_query, grad_key, grad_value, grad_out)


def solution(mesh):
    fine = Mesh(mesh.devices.reshape(2, NX, NZ, 2, 2), AXES)
    in_specs = (P(FSDP, TP), P(TP), P(FSDP, TP), P(FSDP, None), P(FSDP, None), P(TP, FSDP), P(FSDP, TP))
    out_specs = (P(FSDP, TP), P(TP), P(FSDP, TP), P(FSDP, None), P(FSDP, None), P(TP, FSDP))
    return jax.shard_map(local, mesh=fine, in_specs=in_specs, out_specs=out_specs, check_vma=False)
```

```python
import functools
import math

import jax
import jax.numpy as jnp
from jax import lax
from jax.experimental import pallas as pl
from jax.experimental.pallas import tpu as pltpu
from jax.sharding import Mesh, PartitionSpec as P

HD = 128
NX = 4
NZ = 8
AXES = ("yh", "x", "z", "yl", "c")
FSDP = ("yh", "x", "z")
TP = ("yl", "c")
F32 = jnp.float32
BF16 = jnp.bfloat16
PIECE = 32
BLOCK = 2 * HD + 2 * PIECE
GROWS = 16
VMEM = pl.BlockSpec(memory_space=pltpu.VMEM)
SMEM = pl.BlockSpec(memory_space=pltpu.SMEM)


def flat(yh, x, z, yl, c):
    return (((yh * NX + x) * NZ + z) * 2 + yl) * 2 + c


def owner_perm(flip):
    pairs = []
    for yh in range(2):
        for x in range(NX):
            for z in range(NZ):
                for yl in range(2):
                    for c in range(2):
                        dest_x = (x % 2) * 2 + z // 4
                        dest_z = c * 4 + z % 4
                        pairs.append((flat(yh, x, z, yl, c), flat(yl ^ flip, dest_x, dest_z, yh, x // 2)))
    return pairs


def inverse(pairs):
    return [(d, s) for s, d in pairs]


def shift_x(value, by):
    return lax.ppermute(value, "x", [(i, (i + by) % NX) for i in range(NX)])


def shift_z(value, by):
    return lax.ppermute(value, "z", [(i, (i + by) % NZ) for i in range(NZ)])


def swap(value, axis):
    return lax.ppermute(value, axis, [(0, 1), (1, 0)])


def dot(a, b, ca, cb):
    return lax.dot_general(a, b, (((ca,), (cb,)), ((), ())), preferred_element_type=F32)


def lanes(start, size=HD):
    return pl.ds(pl.multiple_of(start, HD), size)


def call(body, outs, scratch, ids, *args, static=None):
    body = body if static is None else functools.partial(body, static)
    return pl.pallas_call(
        body,
        out_shape=[jax.ShapeDtypeStruct(s, d) for s, d in outs],
        in_specs=[SMEM] + [VMEM] * len(args),
        out_specs=[VMEM] * len(outs),
        scratch_shapes=[pltpu.VMEM(s, d) for s, d in scratch],
        compiler_params=pltpu.CompilerParams(vmem_limit_bytes=16 * 2**20),
    )(ids, *args)


def spread_kernel(ids, tokens, cot, *outs):
    x = ids[4]
    rows = tokens.shape[0]
    squares = jnp.zeros((rows, HD), F32)
    for at in range(0, tokens.shape[1], HD):
        value = tokens[:, at : at + HD].astype(F32)
        squares = squares + value * value
    total = jnp.sum(jnp.transpose(squares), axis=0, keepdims=True)
    high = total.astype(BF16).astype(F32)
    middle = (total - high).astype(BF16).astype(F32)
    extra = jnp.concatenate([high, middle, total - high - middle, jnp.zeros((GROWS - 3, HD), F32)], axis=0)
    for s in range(NX):
        block = lanes(((x + s) % NX) * 4 * HD, 4 * HD)
        outs[s][:rows] = tokens[:, block]
        outs[s][rows : 2 * rows] = cot[:, block]
        outs[s][2 * rows :, :HD] = extra.astype(BF16)
        outs[s][2 * rows :, HD:] = jnp.zeros((GROWS, 3 * HD), BF16)


def squares_kernel(ids, a, b, c, d, out):
    for s, ref in enumerate((a, b, c, d)):
        terms = ref[2 * HD :, :HD].astype(F32)
        out[s : s + 1] = (terms[2:3] + terms[1:2]) + terms[0:1]


def normalize_kernel(width, ids, *refs):
    parts, (totals, gain, unit, normed, cot) = refs[:4], refs[4:]
    for s in range(NX):
        rows = slice(s * HD, (s + 1) * HD)
        column = jnp.transpose(jnp.broadcast_to(totals[s : s + 1], (HD, HD)))
        inv = lax.rsqrt(column / width + 1e-05)
        for j in range(4):
            cols = slice(j * HD, (j + 1) * HD)
            value = parts[s][:HD, cols].astype(F32) * inv
            unit[rows, cols] = value
            normed[rows, cols] = (value * gain[:, cols]).astype(BF16)
        cot[rows] = parts[s][HD : 2 * HD]


def forward_pack_kernel(ids, both, prev, after, up, down, far_first, far_second):
    for out, ref in ((up, prev), (down, after)):
        out[: 2 * BLOCK] = both[...]
        out[2 * BLOCK :] = ref[...]
    far_first[...] = prev[:BLOCK]
    far_second[...] = after[BLOCK:]


def product(out, side, normed, cot, w_all, w_out):
    w_q = w_all[:, lanes(side * 2 * HD, 2 * HD)]
    w_kv = w_all[:, lanes((4 + side) * HD)]
    w_o = w_out[side]
    for r in range(0, 512, 256):
        rows = slice(r, r + 256)
        out[rows, : 2 * HD] = dot(normed[rows], w_q, 1, 0)
        out[rows, 2 * HD : 4 * HD] = dot(cot[rows], w_o, 1, 1)
        out[rows, 4 * HD :] = dot(normed[rows], w_kv, 1, 0)


def theirs_kernel(ids, both, prev1, next1, prev2, next2, far_first, far_second, normed, cot, out, w_all, w_out):
    z, c = ids[0], ids[2]

    def place(ref, base, d, half):
        zt = (z + d + NZ) % NZ
        side, j = zt // 4, zt % 4
        rows = pl.ds(pl.multiple_of(j * HD, HD), HD)
        w_all[rows, lanes(side * 2 * HD + half * HD)] = ref[base : base + HD]
        w_out[side, half * HD : (half + 1) * HD, lanes(j * HD)] = ref[base + HD : base + 2 * HD]
        part = pl.ds(pl.multiple_of(j * HD + (2 * half + side) * PIECE, PIECE), PIECE)
        w_all[part, 4 * HD : 5 * HD] = ref[base + 2 * HD : base + 2 * HD + PIECE]
        w_all[part, 5 * HD : 6 * HD] = ref[base + 2 * HD + PIECE : base + BLOCK]

    for ref, base, d in (
        (both, 0, 0),
        (prev1, 0, -1),
        (prev1, 2 * BLOCK, -3),
        (next1, 0, 1),
        (next1, 2 * BLOCK, 3),
        (prev2, 0, -2),
        (next2, 0, 2),
    ):
        place(ref, base, d, 0)
        place(ref, base + BLOCK, d, 1)
    place(far_first, 0, 4, 0)
    place(far_second, 0, 4, 1)
    product(out, 1 - c, normed, cot, w_all, w_out)


def mine_kernel(ids, normed, cot, w_all, w_out, out):
    product(out, ids[2], normed, cot, w_all, w_out)


def split_store(ref, total):
    for start, size, at in ((0, 2 * HD, 0), (4 * HD, HD, 6 * HD)):
        value = total[:, start : start + size]
        high = value.astype(BF16)
        ref[:, at : at + size] = high
        ref[:, at + size : at + 2 * size] = (value - high.astype(F32)).astype(BF16)
    ref[:, 4 * HD : 6 * HD] = total[:, 2 * HD : 4 * HD].astype(BF16)


def joined(ref):
    value = ref[...].astype(F32)
    return jnp.concatenate(
        [
            value[:, : 2 * HD] + value[:, 2 * HD : 4 * HD],
            value[:, 4 * HD : 6 * HD],
            value[:, 6 * HD : 7 * HD] + value[:, 7 * HD :],
        ],
        axis=1,
    )


def chunk_kernel(ids, mine, got, own, *outs):
    own[...] = mine[:HD] + got[:HD]
    for s in range(1, NX):
        rows = slice(s * HD, (s + 1) * HD)
        split_store(outs[s - 1], mine[rows] + got[rows])


def sum_kernel(ids, own, a, b, c, out):
    split_store(out, own[...] + joined(a) + joined(b) + joined(c))


def final_kernel(ids, mine, got, qa, kv):
    total = (joined(mine) + joined(got)).astype(BF16)
    qa[...] = total[:, : 4 * HD]
    kv[...] = total[:, 4 * HD :]


def attend_kernel(ids, qa, kv_mine, kv_theirs, out):
    first = ids[2] == 0
    mine, theirs = kv_mine[...].astype(F32), kv_theirs[...].astype(F32)
    key_rows = jnp.where(first, mine, theirs).astype(BF16)
    value_rows = jnp.where(first, theirs, mine).astype(BF16)
    causal = lax.broadcasted_iota(jnp.int32, (HD, HD), 0) >= lax.broadcasted_iota(jnp.int32, (HD, HD), 1)
    keys = jnp.zeros((HD, HD), F32)
    values = jnp.zeros((HD, HD), F32)
    for h in range(2):
        query = qa[:, h * HD : (h + 1) * HD]
        attn_grad = qa[:, (2 + h) * HD : (3 + h) * HD]
        scores = dot(query, key_rows, 1, 1) * HD ** (-0.5)
        scores = jnp.where(causal, scores, jnp.float32(-1e30))
        shifted = jnp.exp(scores - jnp.max(scores, axis=-1, keepdims=True))
        softmax_out = shifted / jnp.sum(shifted, axis=-1, keepdims=True)
        rounded = softmax_out.astype(BF16)
        dprob = dot(attn_grad, value_rows, 1, 1)
        dscore = softmax_out * (dprob - jnp.sum(dprob * softmax_out, axis=-1, keepdims=True)) * HD ** (-0.5)
        dscore = dscore.astype(BF16)
        out[:, h * HD : (h + 1) * HD] = dot(dscore, key_rows, 1, 0).astype(BF16)
        out[:, (2 + h) * HD : (3 + h) * HD] = dot(rounded, value_rows, 1, 0).astype(BF16)
        keys = keys + dot(dscore, query, 0, 0).astype(BF16).astype(F32)
        values = values + dot(rounded, attn_grad, 0, 0).astype(BF16).astype(F32)
    out[:, 4 * HD : 5 * HD] = keys.astype(BF16)
    out[:, 5 * HD :] = values.astype(BF16)


def gradient_kernel(ids, *refs):
    mine, theirs, (normed, cot, unit, w_all) = refs[:4], refs[4:8], refs[8:12]
    (t0, up, down, t2, m2, t4a, t4b), back = refs[12:19], refs[19:23]
    heads, attended, shared = refs[23:]
    z, c = ids[0], ids[2]
    for s in range(NX):
        rows = slice(s * HD, (s + 1) * HD)
        for ref, side in ((mine[s], c), (theirs[s], 1 - c)):
            heads[rows, lanes(side * 2 * HD, 2 * HD)] = ref[:, : 2 * HD]
            attended[rows, lanes(side * 2 * HD, 2 * HD)] = ref[:, 2 * HD : 4 * HD]
        total = mine[s][:, 4 * HD :].astype(F32) + theirs[s][:, 4 * HD :].astype(F32)
        heads[rows, 4 * HD :] = total.astype(BF16)

    gain_sum = jnp.zeros((1, 4 * HD), F32)
    for s in range(NX):
        rows = slice(s * HD, (s + 1) * HD)
        term = dot(heads[rows], w_all[...], 1, 1)
        back[s][...] = term.astype(BF16)
        gain_sum = gain_sum + jnp.sum(term * unit[rows], axis=0, keepdims=True)
    gain_rows = jnp.concatenate([gain_sum[:, j * HD : (j + 1) * HD] for j in range(4)], axis=0)
    high = gain_rows.astype(BF16).astype(F32)
    gain_rows = jnp.concatenate([high, gain_rows - high, jnp.zeros((8, HD), F32)], axis=0).astype(BF16)

    shared[...] = dot(normed[...], heads[:, 4 * HD :], 0, 0)
    g, n = GROWS, BLOCK
    for ref in (t0, up, down, t4a, t4b):
        ref[:g] = gain_rows
    for d, out_first, out_second in (
        (0, t0.at[g : g + n], t0.at[g + n :]),
        (1, up.at[g : g + n], up.at[g + n : g + 2 * n]),
        (3, up.at[g + 2 * n : g + 3 * n], up.at[g + 3 * n :]),
        (-1, down.at[g : g + n], down.at[g + n : g + 2 * n]),
        (-3, down.at[g + 2 * n : g + 3 * n], down.at[g + 3 * n :]),
        (2, t2.at[:n], t2.at[n:]),
        (-2, m2.at[:n], m2.at[n:]),
        (4, t4a.at[g:], t4b.at[g:]),
    ):
        zt = (z + d + NZ) % NZ
        side, j = zt // 4, zt % 4
        g_q = dot(normed[:, lanes(j * HD)], heads[:, lanes(side * 2 * HD, 2 * HD)], 0, 0).astype(BF16)
        g_o = dot(attended[:, lanes(side * 2 * HD, 2 * HD)], cot[:, lanes(j * HD)], 0, 0).astype(BF16)
        for half, out in enumerate((out_first, out_second)):
            out[:HD] = g_q[:, half * HD : (half + 1) * HD]
            out[HD : 2 * HD] = g_o[half * HD : (half + 1) * HD]
            part = shared[pl.ds(pl.multiple_of(j * HD + (2 * half + side) * PIECE, PIECE), PIECE), :].astype(BF16)
            out[2 * HD : 2 * HD + PIECE] = part[:, :HD]
            out[2 * HD + PIECE :] = part[:, HD:]


def relay_kernel(ids, t2, m2, a, b, c, d, up, down):
    g, n = GROWS, BLOCK
    up[:g] = a[:g]
    up[g : 2 * g] = c[:g]
    down[:g] = b[:g]
    down[g : 2 * g] = d[:g]
    total = t2[...].astype(F32) + a[g + 2 * n :].astype(F32)
    up[2 * g : 2 * g + n] = (total[:n] + c[g:].astype(F32)).astype(BF16)
    up[2 * g + n :] = total[n:].astype(BF16)
    total = m2[...].astype(F32) + b[g + 2 * n :].astype(F32)
    down[2 * g : 2 * g + n] = total[:n].astype(BF16)
    down[2 * g + n :] = (total[n:] + d[g:].astype(F32)).astype(BF16)


def finish_kernel(ids, t0, a, b, up, down, c, d, same, other, gain_out):
    g, n = GROWS, BLOCK
    flip = ids[3]
    near = slice(g, g + 2 * n)
    total = t0[near].astype(F32) + a[near].astype(F32) + b[near].astype(F32)
    total = total + up[2 * g :].astype(F32) + down[2 * g :].astype(F32)
    same[...] = jnp.where(flip == 0, total[:n], total[n:]).astype(BF16)
    other[...] = jnp.where(flip == 0, total[n:], total[:n]).astype(BF16)
    rows = up[g : 2 * g].astype(F32)
    for ref in (t0, a, b, c, d, up, down):
        rows = rows + ref[:g].astype(F32)
    gain_out[...] = rows[:4] + rows[4:8]


def gain_kernel(scale, ids, own, s1, s2, s3, out):
    for s, ref in enumerate((own, s1, s2, s3)):
        out[(ids[4] - s + NX) % NX] = ref[...] * scale


def row_kernel(width, ids, a, b, c, d, tokens, gain, totals, summed, row_sum):
    column = jnp.transpose(jnp.broadcast_to(totals[0:1], (HD, HD)))
    inv = lax.rsqrt(column / width + 1e-05)
    acc = jnp.zeros((HD, HD), F32)
    for s, ref in enumerate((a, b, c, d)):
        at = (ids[4] + s) % NX
        for j in range(4):
            cols = lanes(at * 4 * HD + j * HD)
            value = ref[:, j * HD : (j + 1) * HD]
            summed[:, cols] = value
            acc = acc + (value.astype(F32) * gain[:, cols]) * (tokens[:, cols].astype(F32) * inv)
    row_sum[...] = jnp.sum(jnp.transpose(acc), axis=0, keepdims=True)


def input_kernel(width, ids, summed, tokens, gain, totals, row_own, row_got, out):
    column = jnp.transpose(jnp.broadcast_to(totals[0:1], (HD, HD)))
    inv = lax.rsqrt(column / width + 1e-05)
    row_mean = jnp.transpose(jnp.broadcast_to(row_own[...] + row_got[...], (HD, HD))) / width
    for at in range(0, summed.shape[1], HD):
        cols = slice(at, at + HD)
        unit = tokens[:, cols].astype(F32) * inv
        out[:, cols] = inv * (summed[:, cols].astype(F32) * gain[:, cols] - unit * row_mean)


def owner_kernel(scale, ids, a, b, grad_query, grad_out, shared):
    total = a[...].astype(F32) + b[...].astype(F32)
    grad_query[...] = total[:HD] * scale
    grad_out[...] = total[HD : 2 * HD] * scale
    shared[...] = total[2 * HD :].astype(BF16)


def shared_kernel(scale, ids, own, by_c, by_yl, by_both, grad_key, grad_value):
    yl, c = ids[1], ids[2]
    for ref, at in ((own, 2 * yl + c), (by_c, 2 * yl + 1 - c), (by_yl, 2 - 2 * yl + c), (by_both, 3 - 2 * yl - c)):
        rows = pl.ds(pl.multiple_of(at * PIECE, PIECE), PIECE)
        grad_key[rows] = ref[:PIECE].astype(F32) * scale
        grad_value[rows] = ref[PIECE:].astype(F32) * scale


def local(tokens, gain, w_query, w_key, w_value, w_out, cotangent):
    rows, quarter = tokens.shape
    sub = quarter // NX
    width = quarter * 4
    yh, x, z, yl, c = (lax.axis_index(a) for a in AXES)
    ids = jnp.stack([z, yl, c, yh, x]).astype(jnp.int32)
    head = yl * 2 + c
    loss_scale = 1.0 / math.sqrt(rows * 64)

    pack = jnp.concatenate(
        [
            w_query,
            w_out,
            lax.dynamic_slice_in_dim(w_key, head * PIECE, PIECE, 0),
            lax.dynamic_slice_in_dim(w_value, head * PIECE, PIECE, 0),
        ],
        axis=0,
    )
    same = lax.ppermute(pack, AXES, owner_perm(0))
    other = lax.ppermute(pack, AXES, owner_perm(1))
    part_shape = ((2 * rows + GROWS, sub), BF16)
    parts = call(spread_kernel, [part_shape] * 4, [], ids, tokens, cotangent)
    same, other, *parts = lax.optimization_barrier((same, other, *parts))
    both = jnp.where(yh == 0, jnp.concatenate([same, other]), jnp.concatenate([other, same]))
    prev2, next2 = shift_z(both, 2), shift_z(both, -2)
    double, half_shape = ((4 * BLOCK, HD), BF16), ((BLOCK, HD), BF16)
    relays = call(forward_pack_kernel, [double] * 2 + [half_shape] * 2, [], ids, both, prev2, next2)
    prev1, next1 = shift_z(relays[0], 1), shift_z(relays[1], -1)
    far_first, far_second = shift_z(relays[2], 2), shift_z(relays[3], -2)
    weights = (both, prev1, next1, prev2, next2, far_first, far_second)

    parts = [parts[0]] + [shift_x(parts[s], s) for s in range(1, NX)]
    (totals,) = call(squares_kernel, [((NX, HD), F32)], [], ids, *parts)
    totals, *_ = lax.optimization_barrier((totals, relays[0]))
    totals = totals + swap(totals, "c")
    totals = totals + swap(totals, "yl")
    gain_f = gain.astype(F32)
    gain_sub = lax.dynamic_slice_in_dim(gain_f, x * sub, sub, 0).reshape(1, sub)
    unit_sw, normed_sw, cot_sw = call(
        normalize_kernel,
        [((512, sub), F32), ((512, sub), BF16), ((512, sub), BF16)],
        [],
        ids,
        *parts,
        totals,
        gain_sub,
        static=width,
    )

    theirs, w_all, w_heads = call(
        theirs_kernel,
        [((512, 5 * HD), F32), ((sub, 6 * HD), BF16), ((2, 2 * HD, sub), BF16)],
        [],
        ids,
        *weights,
        normed_sw,
        cot_sw,
    )
    (mine,) = call(mine_kernel, [((512, 5 * HD), F32)], [], ids, normed_sw, cot_sw, w_all, w_heads)
    split = ((rows, 8 * HD), BF16)
    own, *chunks = call(chunk_kernel, [((rows, 5 * HD), F32)] + [split] * 3, [], ids, mine, swap(theirs, "c"))
    chunks = [shift_x(chunks[s - 1], -s) for s in range(1, NX)]
    (partial,) = call(sum_kernel, [split], [], ids, own, *chunks)
    qa, kv = call(final_kernel, [((rows, 4 * HD), BF16), ((rows, HD), BF16)], [], ids, partial, swap(partial, "yl"))
    (heads,) = call(attend_kernel, [((rows, 6 * HD), BF16)], [], ids, qa, kv, swap(kv, "c"))
    heads = [heads] + [shift_x(heads, s) for s in range(1, NX)]

    g, n = GROWS, BLOCK
    t0, up, down, t2, m2, t4a, t4b, *back = call(
        gradient_kernel,
        [
            ((g + 2 * n, HD), BF16),
            ((g + 4 * n, HD), BF16),
            ((g + 4 * n, HD), BF16),
            ((2 * n, HD), BF16),
            ((2 * n, HD), BF16),
            ((g + n, HD), BF16),
            ((g + n, HD), BF16),
        ]
        + [((rows, sub), BF16)] * 4,
        [((512, 6 * HD), BF16), ((512, 4 * HD), BF16), ((sub, 2 * HD), F32)],
        ids,
        *heads,
        *[swap(h, "c") for h in heads],
        normed_sw,
        cot_sw,
        unit_sw,
        w_all,
    )
    c4, d4 = shift_z(t4a, 2), shift_z(t4b, -2)
    a, b = shift_z(up, 1), shift_z(down, -1)
    up, down = call(relay_kernel, [((2 * g + 2 * n, HD), BF16)] * 2, [], ids, t2, m2, a, b, c4, d4)
    *back, _ = lax.optimization_barrier((*back, swap(up[:g], "c")))
    up, down = shift_z(up, 2), shift_z(down, -2)
    to_same, to_other, gain_z = call(
        finish_kernel, [((n, HD), BF16)] * 2 + [((4, HD), F32)], [], ids, t0, a, b, up, down, c4, d4
    )
    gain_z, _ = lax.optimization_barrier((gain_z, swap(to_same[:g], "c")))
    arrived = (lax.ppermute(to_same, AXES, inverse(owner_perm(0))), lax.ppermute(to_other, AXES, inverse(owner_perm(1))))
    *sums, shared_own = call(
        owner_kernel,
        [((HD, HD), F32)] * 2 + [((2 * PIECE, HD), BF16)],
        [],
        ids,
        *arrived,
        static=loss_scale,
    )
    grad_query, grad_out = sums
    both_flip = lax.ppermute(shared_own, TP, [(i, 3 - i) for i in range(4)])
    grad_key, grad_value = call(
        shared_kernel,
        [((rows, HD), F32)] * 2,
        [],
        ids,
        shared_own,
        swap(shared_own, "c"),
        swap(shared_own, "yl"),
        both_flip,
        static=loss_scale,
    )

    gain_z = gain_z + swap(gain_z, "yh")
    (grad_gain,) = call(
        gain_kernel,
        [((NX, 4, HD), F32)],
        [],
        ids,
        gain_z,
        *[shift_x(gain_z, s) for s in range(1, NX)],
        static=loss_scale,
    )
    grad_gain = grad_gain.reshape(quarter)

    pieces = [back[0]] + [shift_x(back[s], -s) for s in range(1, NX)]
    gain_f = gain_f.reshape(1, quarter)
    summed, row_sum = call(
        row_kernel,
        [((rows, quarter), BF16), ((1, rows), F32)],
        [],
        ids,
        *pieces,
        tokens,
        gain_f,
        totals,
        static=width,
    )
    row_sum = row_sum + swap(row_sum, "c")
    (grad_input,) = call(
        input_kernel,
        [((rows, quarter), F32)],
        [],
        ids,
        summed,
        tokens,
        gain_f,
        totals,
        row_sum,
        swap(row_sum, "yl"),
        static=width,
    )
    return (grad_input, grad_gain, grad_query, grad_key, grad_value, grad_out)


def solution(mesh):
    fine = Mesh(mesh.devices.reshape(2, NX, NZ, 2, 2), AXES)
    in_specs = (P(FSDP, TP), P(TP), P(FSDP, TP), P(FSDP, None), P(FSDP, None), P(TP, FSDP), P(FSDP, TP))
    out_specs = (P(FSDP, TP), P(TP), P(FSDP, TP), P(FSDP, None), P(FSDP, None), P(TP, FSDP))
    return jax.shard_map(local, mesh=fine, in_specs=in_specs, out_specs=out_specs, check_vma=False)
```

```python
import functools
import math

import jax
import jax.numpy as jnp
from jax import lax
from jax.experimental import pallas as pl
from jax.experimental.pallas import tpu as pltpu
from jax.sharding import Mesh, PartitionSpec as P

HD = 128
NX = 4
NZ = 8
AXES = ("yh", "x", "z", "yl", "c")
FSDP = ("yh", "x", "z")
TP = ("yl", "c")
F32 = jnp.float32
BF16 = jnp.bfloat16
PIECE = 32
BLOCK = 2 * HD + 2 * PIECE
GROWS = 16
VMEM = pl.BlockSpec(memory_space=pltpu.VMEM)
SMEM = pl.BlockSpec(memory_space=pltpu.SMEM)


def flat(yh, x, z, yl, c):
    return (((yh * NX + x) * NZ + z) * 2 + yl) * 2 + c


def owner_perm(flip):
    pairs = []
    for yh in range(2):
        for x in range(NX):
            for z in range(NZ):
                for yl in range(2):
                    for c in range(2):
                        dest_x = (x % 2) * 2 + z % 2
                        dest_z = (z // 2) * 2 + c
                        pairs.append((flat(yh, x, z, yl, c), flat(yl ^ flip, dest_x, dest_z, yh, x // 2)))
    return pairs


def inverse(pairs):
    return [(d, s) for s, d in pairs]


def shift_x(value, by):
    return lax.ppermute(value, "x", [(i, (i + by) % NX) for i in range(NX)])


def shift_z(value, by):
    return lax.ppermute(value, "z", [(i, (i + by) % NZ) for i in range(NZ)])


def swap(value, axis):
    return lax.ppermute(value, axis, [(0, 1), (1, 0)])


def dot(a, b, ca, cb):
    return lax.dot_general(a, b, (((ca,), (cb,)), ((), ())), preferred_element_type=F32)


def lanes(start, size=HD):
    return pl.ds(pl.multiple_of(start, HD), size)


def feature(at, j):
    return ((at // 2) * 8 + 2 * j + at % 2) * HD


def call(body, outs, scratch, ids, *args, static=None):
    body = body if static is None else functools.partial(body, static)
    return pl.pallas_call(
        body,
        out_shape=[jax.ShapeDtypeStruct(s, d) for s, d in outs],
        in_specs=[SMEM] + [VMEM] * len(args),
        out_specs=[VMEM] * len(outs),
        scratch_shapes=[pltpu.VMEM(s, d) for s, d in scratch],
        compiler_params=pltpu.CompilerParams(vmem_limit_bytes=16 * 2**20),
    )(ids, *args)


def squares_kernel(ids, tokens, out):
    squares = jnp.zeros((tokens.shape[0], HD), F32)
    for at in range(0, tokens.shape[1], HD):
        value = tokens[:, at : at + HD].astype(F32)
        squares = squares + value * value
    out[...] = jnp.sum(jnp.transpose(squares), axis=0, keepdims=True)


def spread_kernel(ids, tokens, cot, total, *outs):
    rows = tokens.shape[0]
    total = total[...]
    high = total.astype(BF16).astype(F32)
    middle = (total - high).astype(BF16).astype(F32)
    extra = jnp.concatenate([high, middle, total - high - middle, jnp.zeros((GROWS - 3, HD), F32)], axis=0)
    for s in range(NX):
        at = (ids[4] + s) % NX
        for j in range(4):
            block, cols = lanes(feature(at, j)), slice(j * HD, (j + 1) * HD)
            outs[s][:rows, cols] = tokens[:, block]
            outs[s][rows : 2 * rows, cols] = cot[:, block]
            outs[s][2 * rows :, cols] = extra.astype(BF16)


def normalize_kernel(width, ids, *refs):
    parts, (gain, unit, normed, cot) = refs[:4], refs[4:]
    for s in range(NX):
        rows = slice(s * HD, (s + 1) * HD)
        terms = parts[s][2 * HD :, :HD].astype(F32)
        total = (terms[2:3] + terms[1:2]) + terms[0:1]
        column = jnp.transpose(jnp.broadcast_to(total, (HD, HD)))
        inv = lax.rsqrt(column / width + 1e-05)
        for j in range(4):
            cols = slice(j * HD, (j + 1) * HD)
            value = parts[s][:HD, cols].astype(F32) * inv
            unit[rows, cols] = value
            normed[rows, cols] = (value * gain[:, lanes(feature(ids[4], j))]).astype(BF16)
        cot[rows] = parts[s][HD : 2 * HD]


def forward_pack_kernel(ids, both, prev, after, up, down, far_first, far_second):
    for out, ref in ((up, prev), (down, after)):
        out[: 2 * BLOCK] = both[...]
        out[2 * BLOCK :] = ref[...]
    far_first[...] = prev[:BLOCK]
    far_second[...] = after[BLOCK:]


def product(out, side, normed, cot, w_all, w_out):
    w_q = w_all[:, lanes(side * 2 * HD, 2 * HD)]
    w_kv = w_all[:, lanes((4 + side) * HD)]
    w_o = w_out[side]
    for r in range(0, 512, 256):
        rows = slice(r, r + 256)
        out[rows, : 2 * HD] = dot(normed[rows], w_q, 1, 0)
        out[rows, 2 * HD : 4 * HD] = dot(cot[rows], w_o, 1, 1)
        out[rows, 4 * HD :] = dot(normed[rows], w_kv, 1, 0)


def theirs_kernel(ids, both, prev1, next1, prev2, next2, far_first, far_second, normed, cot, out, w_all, w_out):
    z, c = ids[0], ids[2]

    def place(ref, base, d, half):
        zt = (z + d + NZ) % NZ
        side, j = zt % 2, zt // 2
        rows = pl.ds(pl.multiple_of(j * HD, HD), HD)
        w_all[rows, lanes(side * 2 * HD + half * HD)] = ref[base : base + HD]
        w_out[side, half * HD : (half + 1) * HD, lanes(j * HD)] = ref[base + HD : base + 2 * HD]
        part = pl.ds(pl.multiple_of(j * HD + (2 * half + side) * PIECE, PIECE), PIECE)
        w_all[part, 4 * HD : 5 * HD] = ref[base + 2 * HD : base + 2 * HD + PIECE]
        w_all[part, 5 * HD : 6 * HD] = ref[base + 2 * HD + PIECE : base + BLOCK]

    for ref, base, d in (
        (both, 0, 0),
        (prev1, 0, -1),
        (prev1, 2 * BLOCK, -3),
        (next1, 0, 1),
        (next1, 2 * BLOCK, 3),
        (prev2, 0, -2),
        (next2, 0, 2),
    ):
        place(ref, base, d, 0)
        place(ref, base + BLOCK, d, 1)
    place(far_first, 0, 4, 0)
    place(far_second, 0, 4, 1)
    product(out, 1 - c, normed, cot, w_all, w_out)


def mine_kernel(ids, normed, cot, w_all, w_out, out):
    product(out, ids[2], normed, cot, w_all, w_out)


def split_store(ref, total):
    for start, size, at in ((0, 2 * HD, 0), (4 * HD, HD, 6 * HD)):
        value = total[:, start : start + size]
        high = value.astype(BF16)
        ref[:, at : at + size] = high
        ref[:, at + size : at + 2 * size] = (value - high.astype(F32)).astype(BF16)
    ref[:, 4 * HD : 6 * HD] = total[:, 2 * HD : 4 * HD].astype(BF16)


def joined(ref):
    value = ref[...].astype(F32)
    return jnp.concatenate(
        [
            value[:, : 2 * HD] + value[:, 2 * HD : 4 * HD],
            value[:, 4 * HD : 6 * HD],
            value[:, 6 * HD : 7 * HD] + value[:, 7 * HD :],
        ],
        axis=1,
    )


def chunk_kernel(ids, mine, got, own, *outs):
    own[...] = mine[:HD] + got[:HD]
    for s in range(1, NX):
        rows = slice(s * HD, (s + 1) * HD)
        split_store(outs[s - 1], mine[rows] + got[rows])


def sum_kernel(ids, own, a, b, c, out):
    split_store(out, own[...] + joined(a) + joined(b) + joined(c))


def final_kernel(ids, mine, got, qa, kv):
    total = (joined(mine) + joined(got)).astype(BF16)
    qa[...] = total[:, : 4 * HD]
    kv[...] = total[:, 4 * HD :]


def attend_kernel(ids, qa, kv_mine, kv_theirs, out):
    first = ids[2] == 0
    mine, theirs = kv_mine[...].astype(F32), kv_theirs[...].astype(F32)
    key_rows = jnp.where(first, mine, theirs).astype(BF16)
    value_rows = jnp.where(first, theirs, mine).astype(BF16)
    causal = lax.broadcasted_iota(jnp.int32, (HD, HD), 0) >= lax.broadcasted_iota(jnp.int32, (HD, HD), 1)
    keys = jnp.zeros((HD, HD), F32)
    values = jnp.zeros((HD, HD), F32)
    for h in range(2):
        query = qa[:, h * HD : (h + 1) * HD]
        attn_grad = qa[:, (2 + h) * HD : (3 + h) * HD]
        scores = dot(query, key_rows, 1, 1) * HD ** (-0.5)
        scores = jnp.where(causal, scores, jnp.float32(-1e30))
        shifted = jnp.exp(scores - jnp.max(scores, axis=-1, keepdims=True))
        softmax_out = shifted / jnp.sum(shifted, axis=-1, keepdims=True)
        rounded = softmax_out.astype(BF16)
        dprob = dot(attn_grad, value_rows, 1, 1)
        dscore = softmax_out * (dprob - jnp.sum(dprob * softmax_out, axis=-1, keepdims=True)) * HD ** (-0.5)
        dscore = dscore.astype(BF16)
        out[:, h * HD : (h + 1) * HD] = dot(dscore, key_rows, 1, 0).astype(BF16)
        out[:, (2 + h) * HD : (3 + h) * HD] = dot(rounded, value_rows, 1, 0).astype(BF16)
        keys = keys + dot(dscore, query, 0, 0).astype(BF16).astype(F32)
        values = values + dot(rounded, attn_grad, 0, 0).astype(BF16).astype(F32)
    out[:, 4 * HD : 5 * HD] = keys.astype(BF16)
    out[:, 5 * HD :] = values.astype(BF16)


def gradient_kernel(ids, *refs):
    mine, theirs, (normed, cot, unit, w_all) = refs[:4], refs[4:8], refs[8:12]
    (t0, up, down, t2, m2, t4a, t4b), back = refs[12:19], refs[19:23]
    heads, attended, shared = refs[23:]
    z, c = ids[0], ids[2]
    for s in range(NX):
        rows = slice(s * HD, (s + 1) * HD)
        for ref, side in ((mine[s], c), (theirs[s], 1 - c)):
            heads[rows, lanes(side * 2 * HD, 2 * HD)] = ref[:, : 2 * HD]
            attended[rows, lanes(side * 2 * HD, 2 * HD)] = ref[:, 2 * HD : 4 * HD]
        total = mine[s][:, 4 * HD :].astype(F32) + theirs[s][:, 4 * HD :].astype(F32)
        heads[rows, 4 * HD :] = total.astype(BF16)

    gain_sum = jnp.zeros((1, 4 * HD), F32)
    for s in range(NX):
        rows = slice(s * HD, (s + 1) * HD)
        term = dot(heads[rows], w_all[...], 1, 1)
        back[s][...] = term.astype(BF16)
        gain_sum = gain_sum + jnp.sum(term * unit[rows], axis=0, keepdims=True)
    gain_rows = jnp.concatenate([gain_sum[:, j * HD : (j + 1) * HD] for j in range(4)], axis=0)
    high = gain_rows.astype(BF16).astype(F32)
    gain_rows = jnp.concatenate([high, gain_rows - high, jnp.zeros((8, HD), F32)], axis=0).astype(BF16)

    shared[...] = dot(normed[...], heads[:, 4 * HD :], 0, 0)
    g, n = GROWS, BLOCK
    for ref in (t0, up, down, t4a, t4b):
        ref[:g] = gain_rows
    for d, out_first, out_second in (
        (0, t0.at[g : g + n], t0.at[g + n :]),
        (1, up.at[g : g + n], up.at[g + n : g + 2 * n]),
        (3, up.at[g + 2 * n : g + 3 * n], up.at[g + 3 * n :]),
        (-1, down.at[g : g + n], down.at[g + n : g + 2 * n]),
        (-3, down.at[g + 2 * n : g + 3 * n], down.at[g + 3 * n :]),
        (2, t2.at[:n], t2.at[n:]),
        (-2, m2.at[:n], m2.at[n:]),
        (4, t4a.at[g:], t4b.at[g:]),
    ):
        zt = (z + d + NZ) % NZ
        side, j = zt % 2, zt // 2
        g_q = dot(normed[:, lanes(j * HD)], heads[:, lanes(side * 2 * HD, 2 * HD)], 0, 0).astype(BF16)
        g_o = dot(attended[:, lanes(side * 2 * HD, 2 * HD)], cot[:, lanes(j * HD)], 0, 0).astype(BF16)
        for half, out in enumerate((out_first, out_second)):
            out[:HD] = g_q[:, half * HD : (half + 1) * HD]
            out[HD : 2 * HD] = g_o[half * HD : (half + 1) * HD]
            part = shared[pl.ds(pl.multiple_of(j * HD + (2 * half + side) * PIECE, PIECE), PIECE), :].astype(BF16)
            out[2 * HD : 2 * HD + PIECE] = part[:, :HD]
            out[2 * HD + PIECE :] = part[:, HD:]


def relay_kernel(ids, t2, m2, a, b, c, d, up, down):
    g, n = GROWS, BLOCK
    up[:g] = a[:g]
    up[g : 2 * g] = c[:g]
    down[:g] = b[:g]
    down[g : 2 * g] = d[:g]
    total = t2[...].astype(F32) + a[g + 2 * n :].astype(F32)
    up[2 * g : 2 * g + n] = (total[:n] + c[g:].astype(F32)).astype(BF16)
    up[2 * g + n :] = total[n:].astype(BF16)
    total = m2[...].astype(F32) + b[g + 2 * n :].astype(F32)
    down[2 * g : 2 * g + n] = total[:n].astype(BF16)
    down[2 * g + n :] = (total[n:] + d[g:].astype(F32)).astype(BF16)


def finish_kernel(ids, t0, a, b, up, down, c, d, same, other, gain_out):
    g, n = GROWS, BLOCK
    flip = ids[3]
    near = slice(g, g + 2 * n)
    total = t0[near].astype(F32) + a[near].astype(F32) + b[near].astype(F32)
    total = total + up[2 * g :].astype(F32) + down[2 * g :].astype(F32)
    same[...] = jnp.where(flip == 0, total[:n], total[n:]).astype(BF16)
    other[...] = jnp.where(flip == 0, total[n:], total[:n]).astype(BF16)
    rows = up[g : 2 * g].astype(F32)
    for ref in (t0, a, b, c, d, up, down):
        rows = rows + ref[:g].astype(F32)
    gain_out[...] = rows[:4] + rows[4:8]


def gain_kernel(scale, ids, own, s1, s2, s3, out):
    for s, ref in enumerate((own, s1, s2, s3)):
        at = (ids[4] - s + NX) % NX
        for j in range(4):
            out[(at // 2) * 8 + 2 * j + at % 2] = ref[j : j + 1] * scale


def row_kernel(width, ids, a, b, c, d, tokens, gain, total, summed, row_sum):
    column = jnp.transpose(jnp.broadcast_to(total[...], (HD, HD)))
    inv = lax.rsqrt(column / width + 1e-05)
    acc = jnp.zeros((HD, HD), F32)
    for s, ref in enumerate((a, b, c, d)):
        at = (ids[4] + s) % NX
        for j in range(4):
            cols = lanes(feature(at, j))
            value = ref[:, j * HD : (j + 1) * HD]
            summed[:, cols] = value
            acc = acc + (value.astype(F32) * gain[:, cols]) * (tokens[:, cols].astype(F32) * inv)
    row_sum[...] = jnp.sum(jnp.transpose(acc), axis=0, keepdims=True)


def input_kernel(width, ids, summed, tokens, gain, total, row_own, row_got, out):
    column = jnp.transpose(jnp.broadcast_to(total[...], (HD, HD)))
    inv = lax.rsqrt(column / width + 1e-05)
    row_mean = jnp.transpose(jnp.broadcast_to(row_own[...] + row_got[...], (HD, HD))) / width
    for at in range(0, summed.shape[1], HD):
        cols = slice(at, at + HD)
        unit = tokens[:, cols].astype(F32) * inv
        out[:, cols] = inv * (summed[:, cols].astype(F32) * gain[:, cols] - unit * row_mean)


def owner_kernel(scale, ids, a, b, grad_query, grad_out):
    for out, rows in ((grad_query, slice(0, HD)), (grad_out, slice(HD, 2 * HD))):
        out[...] = (a[rows].astype(F32) + b[rows].astype(F32)) * scale


def shared_kernel(ids, a, b, shared):
    shared[...] = (a[2 * HD :].astype(F32) + b[2 * HD :].astype(F32)).astype(BF16)


def join_kernel(scale, ids, own, by_c, by_yl, by_both, grad_key, grad_value):
    yl, c = ids[1], ids[2]
    for ref, at in ((own, 2 * yl + c), (by_c, 2 * yl + 1 - c), (by_yl, 2 - 2 * yl + c), (by_both, 3 - 2 * yl - c)):
        rows = pl.ds(pl.multiple_of(at * PIECE, PIECE), PIECE)
        grad_key[rows] = ref[:PIECE].astype(F32) * scale
        grad_value[rows] = ref[PIECE:].astype(F32) * scale


def local(tokens, gain, w_query, w_key, w_value, w_out, cotangent):
    rows, quarter = tokens.shape
    sub = quarter // NX
    width = quarter * 4
    yh, x, z, yl, c = (lax.axis_index(a) for a in AXES)
    ids = jnp.stack([z, yl, c, yh, x]).astype(jnp.int32)
    head = yl * 2 + c
    loss_scale = 1.0 / math.sqrt(rows * 64)

    pack = jnp.concatenate(
        [
            w_query,
            w_out,
            lax.dynamic_slice_in_dim(w_key, head * PIECE, PIECE, 0),
            lax.dynamic_slice_in_dim(w_value, head * PIECE, PIECE, 0),
        ],
        axis=0,
    )
    same = lax.ppermute(pack, AXES, owner_perm(0))
    other = lax.ppermute(pack, AXES, owner_perm(1))
    (total,) = call(squares_kernel, [((1, rows), F32)], [], ids, tokens)
    total = total + swap(total, "c")
    same, other, total = lax.optimization_barrier((same, other, total))
    total = total + swap(total, "yl")
    both = jnp.where(yh == 0, jnp.concatenate([same, other]), jnp.concatenate([other, same]))
    prev2, next2 = shift_z(both, 2), shift_z(both, -2)
    double, half_shape = ((4 * BLOCK, HD), BF16), ((BLOCK, HD), BF16)
    relays = call(forward_pack_kernel, [double] * 2 + [half_shape] * 2, [], ids, both, prev2, next2)
    prev1, next1 = shift_z(relays[0], 1), shift_z(relays[1], -1)
    far_first, far_second = shift_z(relays[2], 2), shift_z(relays[3], -2)
    weights = (both, prev1, next1, prev2, next2, far_first, far_second)

    total, _ = lax.optimization_barrier((total, both))
    part_shape = ((2 * rows + GROWS, sub), BF16)
    parts = call(spread_kernel, [part_shape] * 4, [], ids, tokens, cotangent, total)
    parts = [parts[0]] + [shift_x(parts[s], s) for s in range(1, NX)]
    gain_f = gain.astype(F32).reshape(1, quarter)
    unit_sw, normed_sw, cot_sw = call(
        normalize_kernel,
        [((512, sub), F32), ((512, sub), BF16), ((512, sub), BF16)],
        [],
        ids,
        *parts,
        gain_f,
        static=width,
    )

    theirs, w_all, w_heads = call(
        theirs_kernel,
        [((512, 5 * HD), F32), ((sub, 6 * HD), BF16), ((2, 2 * HD, sub), BF16)],
        [],
        ids,
        *weights,
        normed_sw,
        cot_sw,
    )
    (mine,) = call(mine_kernel, [((512, 5 * HD), F32)], [], ids, normed_sw, cot_sw, w_all, w_heads)
    split = ((rows, 8 * HD), BF16)
    own, *chunks = call(chunk_kernel, [((rows, 5 * HD), F32)] + [split] * 3, [], ids, mine, swap(theirs, "c"))
    chunks = [shift_x(chunks[s - 1], -s) for s in range(1, NX)]
    (partial,) = call(sum_kernel, [split], [], ids, own, *chunks)
    qa, kv = call(final_kernel, [((rows, 4 * HD), BF16), ((rows, HD), BF16)], [], ids, partial, swap(partial, "yl"))
    (heads,) = call(attend_kernel, [((rows, 6 * HD), BF16)], [], ids, qa, kv, swap(kv, "c"))
    heads = [heads] + [shift_x(heads, s) for s in range(1, NX)]

    g, n = GROWS, BLOCK
    t0, up, down, t2, m2, t4a, t4b, *back = call(
        gradient_kernel,
        [
            ((g + 2 * n, HD), BF16),
            ((g + 4 * n, HD), BF16),
            ((g + 4 * n, HD), BF16),
            ((2 * n, HD), BF16),
            ((2 * n, HD), BF16),
            ((g + n, HD), BF16),
            ((g + n, HD), BF16),
        ]
        + [((rows, sub), BF16)] * 4,
        [((512, 6 * HD), BF16), ((512, 4 * HD), BF16), ((sub, 2 * HD), F32)],
        ids,
        *heads,
        *[swap(h, "c") for h in heads],
        normed_sw,
        cot_sw,
        unit_sw,
        w_all,
    )
    c4, d4 = shift_z(t4a, 2), shift_z(t4b, -2)
    a, b = shift_z(up, 1), shift_z(down, -1)
    up, down = call(relay_kernel, [((2 * g + 2 * n, HD), BF16)] * 2, [], ids, t2, m2, a, b, c4, d4)
    up, down = shift_z(up, 2), shift_z(down, -2)

    pieces = [back[0]] + [shift_x(back[s], -s) for s in range(1, NX)]
    summed, row_sum = call(
        row_kernel,
        [((rows, quarter), BF16), ((1, rows), F32)],
        [],
        ids,
        *pieces,
        tokens,
        gain_f,
        total,
        static=width,
    )
    row_sum = row_sum + swap(row_sum, "c")
    up, down, row_sum = lax.optimization_barrier((up, down, row_sum))
    to_same, to_other, gain_z = call(
        finish_kernel, [((n, HD), BF16)] * 2 + [((4, HD), F32)], [], ids, t0, a, b, up, down, c4, d4
    )
    gain_z, _ = lax.optimization_barrier((gain_z, swap(to_same[:g], "c")))
    (grad_input,) = call(
        input_kernel,
        [((rows, quarter), F32)],
        [],
        ids,
        summed,
        tokens,
        gain_f,
        total,
        row_sum,
        swap(row_sum, "yl"),
        static=width,
    )
    arrived = (lax.ppermute(to_same, AXES, inverse(owner_perm(0))), lax.ppermute(to_other, AXES, inverse(owner_perm(1))))
    gain_z = gain_z + swap(gain_z, "yh")
    *arrived, grad_input, gain_z = lax.optimization_barrier((*arrived, grad_input, gain_z))
    (shared_own,) = call(shared_kernel, [((2 * PIECE, HD), BF16)], [], ids, *arrived)
    grad_query, grad_out = call(owner_kernel, [((HD, HD), F32)] * 2, [], ids, *arrived, static=loss_scale)
    shared_yl = swap(shared_own, "yl")
    grad_key, grad_value = call(
        join_kernel,
        [((rows, HD), F32)] * 2,
        [],
        ids,
        shared_own,
        swap(shared_own, "c"),
        shared_yl,
        swap(shared_yl, "c"),
        static=loss_scale,
    )

    (grad_gain,) = call(
        gain_kernel,
        [((4 * NX, 1, HD), F32)],
        [],
        ids,
        gain_z,
        *[shift_x(gain_z, s) for s in range(1, NX)],
        static=loss_scale,
    )
    grad_gain = grad_gain.reshape(quarter)

    return (grad_input, grad_gain, grad_query, grad_key, grad_value, grad_out)


def solution(mesh):
    fine = Mesh(mesh.devices.reshape(2, NX, NZ, 2, 2), AXES)
    in_specs = (P(FSDP, TP), P(TP), P(FSDP, TP), P(FSDP, None), P(FSDP, None), P(TP, FSDP), P(FSDP, TP))
    out_specs = (P(FSDP, TP), P(TP), P(FSDP, TP), P(FSDP, None), P(FSDP, None), P(TP, FSDP))
    return jax.shard_map(local, mesh=fine, in_specs=in_specs, out_specs=out_specs, check_vma=False)
```

```python
import functools
import math

import jax
import jax.numpy as jnp
from jax import lax
from jax.experimental import pallas as pl
from jax.experimental.pallas import tpu as pltpu
from jax.sharding import Mesh, PartitionSpec as P

HD = 128
NX = 4
NZ = 8
AXES = ("yh", "x", "z", "yl", "c")
FSDP = ("yh", "x", "z")
TP = ("yl", "c")
F32 = jnp.float32
BF16 = jnp.bfloat16
PIECE = 32
BLOCK = 2 * HD + 2 * PIECE
GROWS = 16
VMEM = pl.BlockSpec(memory_space=pltpu.VMEM)
SMEM = pl.BlockSpec(memory_space=pltpu.SMEM)


def flat(yh, x, z, yl, c):
    return (((yh * NX + x) * NZ + z) * 2 + yl) * 2 + c


def owner_perm(flip):
    pairs = []
    for yh in range(2):
        for x in range(NX):
            for z in range(NZ):
                for yl in range(2):
                    for c in range(2):
                        dest_x = (x % 2) * 2 + z % 2
                        dest_z = (z // 2) * 2 + c
                        pairs.append((flat(yh, x, z, yl, c), flat(yl ^ flip, dest_x, dest_z, yh, x // 2)))
    return pairs


def inverse(pairs):
    return [(d, s) for s, d in pairs]


def shift_x(value, by):
    return lax.ppermute(value, "x", [(i, (i + by) % NX) for i in range(NX)])


def shift_z(value, by):
    return lax.ppermute(value, "z", [(i, (i + by) % NZ) for i in range(NZ)])


def swap(value, axis):
    return lax.ppermute(value, axis, [(0, 1), (1, 0)])


def dot(a, b, ca, cb):
    return lax.dot_general(a, b, (((ca,), (cb,)), ((), ())), preferred_element_type=F32)


def lanes(start, size=HD):
    return pl.ds(pl.multiple_of(start, HD), size)


def feature(at, j):
    return ((at // 2) * 8 + 2 * j + at % 2) * HD


def call(body, outs, scratch, ids, *args, static=None, aliases={}):
    body = body if static is None else functools.partial(body, static)
    return pl.pallas_call(
        body,
        out_shape=[jax.ShapeDtypeStruct(s, d) for s, d in outs],
        in_specs=[SMEM] + [VMEM] * len(args),
        out_specs=[VMEM] * len(outs),
        input_output_aliases=aliases,
        scratch_shapes=[pltpu.VMEM(s, d) for s, d in scratch],
        compiler_params=pltpu.CompilerParams(vmem_limit_bytes=16 * 2**20),
    )(ids, *args)


def spread_kernel(ids, tokens, cot, total_out, *outs):
    rows = tokens.shape[0]
    squares = jnp.zeros((rows, HD), F32)
    for s in range(NX):
        at = (ids[4] + s) % NX
        for j in range(4):
            block, cols = lanes(feature(at, j)), slice(j * HD, (j + 1) * HD)
            value = tokens[:, block]
            squares = squares + value.astype(F32) * value.astype(F32)
            outs[s][:rows, cols] = value
            outs[s][rows : 2 * rows, cols] = cot[:, block]
    total_out[...] = jnp.sum(jnp.transpose(squares), axis=0, keepdims=True)


def stamp_kernel(ids, total, *refs):
    total = total[...]
    high = total.astype(BF16).astype(F32)
    middle = (total - high).astype(BF16).astype(F32)
    extra = jnp.concatenate([high, middle, total - high - middle, jnp.zeros((GROWS - 3, HD), F32)], axis=0)
    extra = jnp.concatenate([extra] * 4, axis=1).astype(BF16)
    for out in refs[NX:]:
        out[2 * HD :] = extra


def normalize_kernel(width, ids, *refs):
    parts, (gain, unit, normed, cot) = refs[:4], refs[4:]
    for s in range(NX):
        rows = slice(s * HD, (s + 1) * HD)
        terms = parts[s][2 * HD :, :HD].astype(F32)
        total = (terms[2:3] + terms[1:2]) + terms[0:1]
        column = jnp.transpose(jnp.broadcast_to(total, (HD, HD)))
        inv = lax.rsqrt(column / width + 1e-05)
        for j in range(4):
            cols = slice(j * HD, (j + 1) * HD)
            value = parts[s][:HD, cols].astype(F32) * inv
            unit[rows, cols] = value
            normed[rows, cols] = (value * gain[:, lanes(feature(ids[4], j))]).astype(BF16)
        cot[rows] = parts[s][HD : 2 * HD]


def forward_pack_kernel(ids, both, prev, after, up, down, far_first, far_second):
    for out, ref in ((up, prev), (down, after)):
        out[: 2 * BLOCK] = both[...]
        out[2 * BLOCK :] = ref[...]
    far_first[...] = prev[:BLOCK]
    far_second[...] = after[BLOCK:]


def product(out, side, normed, cot, w_all, w_out):
    w_q = w_all[:, lanes(side * 2 * HD, 2 * HD)]
    w_kv = w_all[:, lanes((4 + side) * HD)]
    w_o = w_out[side]
    for r in range(0, 512, 256):
        rows = slice(r, r + 256)
        out[rows, : 2 * HD] = dot(normed[rows], w_q, 1, 0)
        out[rows, 2 * HD : 4 * HD] = dot(cot[rows], w_o, 1, 1)
        out[rows, 4 * HD :] = dot(normed[rows], w_kv, 1, 0)


def theirs_kernel(ids, both, prev1, next1, prev2, next2, far_first, far_second, normed, cot, out, w_all, w_out):
    z, c = ids[0], ids[2]

    def place(ref, base, d, half):
        zt = (z + d + NZ) % NZ
        side, j = zt % 2, zt // 2
        rows = pl.ds(pl.multiple_of(j * HD, HD), HD)
        w_all[rows, lanes(side * 2 * HD + half * HD)] = ref[base : base + HD]
        w_out[side, half * HD : (half + 1) * HD, lanes(j * HD)] = ref[base + HD : base + 2 * HD]
        part = pl.ds(pl.multiple_of(j * HD + (2 * half + side) * PIECE, PIECE), PIECE)
        w_all[part, 4 * HD : 5 * HD] = ref[base + 2 * HD : base + 2 * HD + PIECE]
        w_all[part, 5 * HD : 6 * HD] = ref[base + 2 * HD + PIECE : base + BLOCK]

    for ref, base, d in (
        (both, 0, 0),
        (prev1, 0, -1),
        (prev1, 2 * BLOCK, -3),
        (next1, 0, 1),
        (next1, 2 * BLOCK, 3),
        (prev2, 0, -2),
        (next2, 0, 2),
    ):
        place(ref, base, d, 0)
        place(ref, base + BLOCK, d, 1)
    place(far_first, 0, 4, 0)
    place(far_second, 0, 4, 1)
    product(out, 1 - c, normed, cot, w_all, w_out)


def mine_kernel(ids, normed, cot, w_all, w_out, out):
    product(out, ids[2], normed, cot, w_all, w_out)


def split_store(ref, total):
    for start, size, at in ((0, 2 * HD, 0), (4 * HD, HD, 6 * HD)):
        value = total[:, start : start + size]
        high = value.astype(BF16)
        ref[:, at : at + size] = high
        ref[:, at + size : at + 2 * size] = (value - high.astype(F32)).astype(BF16)
    ref[:, 4 * HD : 6 * HD] = total[:, 2 * HD : 4 * HD].astype(BF16)


def joined(ref):
    value = ref[...].astype(F32)
    return jnp.concatenate(
        [
            value[:, : 2 * HD] + value[:, 2 * HD : 4 * HD],
            value[:, 4 * HD : 6 * HD],
            value[:, 6 * HD : 7 * HD] + value[:, 7 * HD :],
        ],
        axis=1,
    )


def chunk_kernel(ids, mine, got, own, *outs):
    own[...] = mine[:HD] + got[:HD]
    for s in range(1, NX):
        rows = slice(s * HD, (s + 1) * HD)
        split_store(outs[s - 1], mine[rows] + got[rows])


def sum_kernel(ids, own, a, b, c, out):
    split_store(out, own[...] + joined(a) + joined(b) + joined(c))


def final_kernel(ids, mine, got, qa, kv):
    total = (joined(mine) + joined(got)).astype(BF16)
    qa[...] = total[:, : 4 * HD]
    kv[...] = total[:, 4 * HD :]


def attend_kernel(ids, qa, kv_mine, kv_theirs, out, row_out):
    first = ids[2] == 0
    mine, theirs = kv_mine[...].astype(F32), kv_theirs[...].astype(F32)
    key_rows = jnp.where(first, mine, theirs).astype(BF16)
    value_rows = jnp.where(first, theirs, mine).astype(BF16)
    causal = lax.broadcasted_iota(jnp.int32, (HD, HD), 0) >= lax.broadcasted_iota(jnp.int32, (HD, HD), 1)
    keys = jnp.zeros((HD, HD), F32)
    values = jnp.zeros((HD, HD), F32)
    row_terms = jnp.zeros((HD, HD), F32)
    for h in range(2):
        query = qa[:, h * HD : (h + 1) * HD]
        attn_grad = qa[:, (2 + h) * HD : (3 + h) * HD]
        scores = dot(query, key_rows, 1, 1) * HD ** (-0.5)
        scores = jnp.where(causal, scores, jnp.float32(-1e30))
        shifted = jnp.exp(scores - jnp.max(scores, axis=-1, keepdims=True))
        softmax_out = shifted / jnp.sum(shifted, axis=-1, keepdims=True)
        rounded = softmax_out.astype(BF16)
        dprob = dot(attn_grad, value_rows, 1, 1)
        dscore = softmax_out * (dprob - jnp.sum(dprob * softmax_out, axis=-1, keepdims=True)) * HD ** (-0.5)
        dscore = dscore.astype(BF16)
        d_query = dot(dscore, key_rows, 1, 0).astype(BF16)
        out[:, h * HD : (h + 1) * HD] = d_query
        row_terms = row_terms + d_query.astype(F32) * query.astype(F32)
        out[:, (2 + h) * HD : (3 + h) * HD] = dot(rounded, value_rows, 1, 0).astype(BF16)
        keys = keys + dot(dscore, query, 0, 0).astype(BF16).astype(F32)
        values = values + dot(rounded, attn_grad, 0, 0).astype(BF16).astype(F32)
    out[:, 4 * HD : 5 * HD] = keys.astype(BF16)
    out[:, 5 * HD :] = values.astype(BF16)
    row_terms = row_terms + keys * key_rows.astype(F32) + values * value_rows.astype(F32)
    row_out[...] = jnp.sum(jnp.transpose(row_terms), axis=0, keepdims=True)


def gradient_kernel(ids, *refs):
    mine, theirs, (normed, cot, unit, w_all) = refs[:4], refs[4:8], refs[8:12]
    (t0, up, down, t2, m2, t4a, t4b), back = refs[12:19], refs[19:23]
    heads, attended, shared = refs[23:]
    z, c = ids[0], ids[2]
    for s in range(NX):
        rows = slice(s * HD, (s + 1) * HD)
        for ref, side in ((mine[s], c), (theirs[s], 1 - c)):
            heads[rows, lanes(side * 2 * HD, 2 * HD)] = ref[:, : 2 * HD]
            attended[rows, lanes(side * 2 * HD, 2 * HD)] = ref[:, 2 * HD : 4 * HD]
        total = mine[s][:, 4 * HD :].astype(F32) + theirs[s][:, 4 * HD :].astype(F32)
        heads[rows, 4 * HD :] = total.astype(BF16)

    gain_sum = jnp.zeros((1, 4 * HD), F32)
    for s in range(NX):
        rows = slice(s * HD, (s + 1) * HD)
        term = dot(heads[rows], w_all[...], 1, 1)
        back[s][...] = term.astype(BF16)
        gain_sum = gain_sum + jnp.sum(term * unit[rows], axis=0, keepdims=True)
    gain_rows = jnp.concatenate([gain_sum[:, j * HD : (j + 1) * HD] for j in range(4)], axis=0)
    high = gain_rows.astype(BF16).astype(F32)
    gain_rows = jnp.concatenate([high, gain_rows - high, jnp.zeros((8, HD), F32)], axis=0).astype(BF16)

    shared[...] = dot(normed[...], heads[:, 4 * HD :], 0, 0)
    g, n = GROWS, BLOCK
    for ref in (t0, up, down, t4a, t4b):
        ref[:g] = gain_rows
    for d, out_first, out_second in (
        (0, t0.at[g : g + n], t0.at[g + n :]),
        (1, up.at[g : g + n], up.at[g + n : g + 2 * n]),
        (3, up.at[g + 2 * n : g + 3 * n], up.at[g + 3 * n :]),
        (-1, down.at[g : g + n], down.at[g + n : g + 2 * n]),
        (-3, down.at[g + 2 * n : g + 3 * n], down.at[g + 3 * n :]),
        (2, t2.at[:n], t2.at[n:]),
        (-2, m2.at[:n], m2.at[n:]),
        (4, t4a.at[g:], t4b.at[g:]),
    ):
        zt = (z + d + NZ) % NZ
        side, j = zt % 2, zt // 2
        g_q = dot(normed[:, lanes(j * HD)], heads[:, lanes(side * 2 * HD, 2 * HD)], 0, 0).astype(BF16)
        g_o = dot(attended[:, lanes(side * 2 * HD, 2 * HD)], cot[:, lanes(j * HD)], 0, 0).astype(BF16)
        for half, out in enumerate((out_first, out_second)):
            out[:HD] = g_q[:, half * HD : (half + 1) * HD]
            out[HD : 2 * HD] = g_o[half * HD : (half + 1) * HD]
            part = shared[pl.ds(pl.multiple_of(j * HD + (2 * half + side) * PIECE, PIECE), PIECE), :].astype(BF16)
            out[2 * HD : 2 * HD + PIECE] = part[:, :HD]
            out[2 * HD + PIECE :] = part[:, HD:]


def relay_kernel(ids, t2, m2, a, b, c, d, up, down):
    g, n = GROWS, BLOCK
    up[:g] = a[:g]
    up[g : 2 * g] = c[:g]
    down[:g] = b[:g]
    down[g : 2 * g] = d[:g]
    total = t2[...].astype(F32) + a[g + 2 * n :].astype(F32)
    up[2 * g : 2 * g + n] = (total[:n] + c[g:].astype(F32)).astype(BF16)
    up[2 * g + n :] = total[n:].astype(BF16)
    total = m2[...].astype(F32) + b[g + 2 * n :].astype(F32)
    down[2 * g : 2 * g + n] = total[:n].astype(BF16)
    down[2 * g + n :] = (total[n:] + d[g:].astype(F32)).astype(BF16)


def finish_kernel(ids, t0, a, b, up, down, c, d, same, other, gain_out):
    g, n = GROWS, BLOCK
    flip = ids[3]
    near = slice(g, g + 2 * n)
    total = t0[near].astype(F32) + a[near].astype(F32) + b[near].astype(F32)
    total = total + up[2 * g :].astype(F32) + down[2 * g :].astype(F32)
    same[...] = jnp.where(flip == 0, total[:n], total[n:]).astype(BF16)
    other[...] = jnp.where(flip == 0, total[n:], total[:n]).astype(BF16)
    rows = up[g : 2 * g].astype(F32)
    for ref in (t0, a, b, c, d, up, down):
        rows = rows + ref[:g].astype(F32)
    gain_out[...] = rows[:4] + rows[4:8]


def input_kernel(width, ids, a, b, c, d, tokens, gain, total, row_sum, out):
    inv = lax.rsqrt(jnp.transpose(jnp.broadcast_to(total[...], (HD, HD))) / width + 1e-05)
    row_mean = jnp.transpose(jnp.broadcast_to(row_sum[...], (HD, HD))) / width
    for s, ref in enumerate((a, b, c, d)):
        at = (ids[4] + s) % NX
        for j in range(4):
            cols = lanes(feature(at, j))
            unit = tokens[:, cols].astype(F32) * inv
            scaled = ref[:, j * HD : (j + 1) * HD].astype(F32) * gain[:, cols]
            out[:, cols] = inv * (scaled - unit * row_mean)


def owner_kernel(scale, ids, a, b, grad_query, grad_out):
    for out, rows in ((grad_query, slice(0, HD)), (grad_out, slice(HD, 2 * HD))):
        out[...] = (a[rows].astype(F32) + b[rows].astype(F32)) * scale


def shared_kernel(ids, a, b, shared):
    shared[...] = (a[2 * HD :].astype(F32) + b[2 * HD :].astype(F32)).astype(BF16)


def join_kernel(scale, ids, own, by_c, by_yl, by_both, g0, g1, g2, g3, grad_key, grad_value, grad_gain):
    yl, c, x = ids[1], ids[2], ids[4]
    for ref, at in ((own, 2 * yl + c), (by_c, 2 * yl + 1 - c), (by_yl, 2 - 2 * yl + c), (by_both, 3 - 2 * yl - c)):
        rows = pl.ds(pl.multiple_of(at * PIECE, PIECE), PIECE)
        grad_key[rows] = ref[:PIECE].astype(F32) * scale
        grad_value[rows] = ref[PIECE:].astype(F32) * scale
    for s, ref in enumerate((g0, g1, g2, g3)):
        at = (x - s + NX) % NX
        for j in range(4):
            grad_gain[(at // 2) * 8 + 2 * j + at % 2] = ref[j : j + 1] * scale


def local(tokens, gain, w_query, w_key, w_value, w_out, cotangent):
    rows, quarter = tokens.shape
    sub = quarter // NX
    width = quarter * 4
    yh, x, z, yl, c = (lax.axis_index(a) for a in AXES)
    ids = jnp.stack([z, yl, c, yh, x]).astype(jnp.int32)
    head = yl * 2 + c
    loss_scale = 1.0 / math.sqrt(rows * 64)

    pack = jnp.concatenate(
        [
            w_query,
            w_out,
            lax.dynamic_slice_in_dim(w_key, head * PIECE, PIECE, 0),
            lax.dynamic_slice_in_dim(w_value, head * PIECE, PIECE, 0),
        ],
        axis=0,
    )
    same = lax.ppermute(pack, AXES, owner_perm(0))
    other = lax.ppermute(pack, AXES, owner_perm(1))
    part_shape = ((2 * rows + GROWS, sub), BF16)
    total, *parts = call(spread_kernel, [((1, rows), F32)] + [part_shape] * 4, [], ids, tokens, cotangent)
    total = total + swap(total, "c")
    same, other, total = lax.optimization_barrier((same, other, total))
    total = total + swap(total, "yl")
    both = jnp.where(yh == 0, jnp.concatenate([same, other]), jnp.concatenate([other, same]))
    prev2, next2 = shift_z(both, 2), shift_z(both, -2)
    double, half_shape = ((4 * BLOCK, HD), BF16), ((BLOCK, HD), BF16)
    relays = call(forward_pack_kernel, [double] * 2 + [half_shape] * 2, [], ids, both, prev2, next2)
    prev1, next1 = shift_z(relays[0], 1), shift_z(relays[1], -1)
    far_first, far_second = shift_z(relays[2], 2), shift_z(relays[3], -2)
    weights = (both, prev1, next1, prev2, next2, far_first, far_second)

    parts = call(stamp_kernel, [part_shape] * 4, [], ids, total, *parts, aliases={2 + s: s for s in range(4)})
    parts = [parts[0]] + [shift_x(parts[s], s) for s in range(1, NX)]
    gain_f = gain.astype(F32).reshape(1, quarter)
    unit_sw, normed_sw, cot_sw = call(
        normalize_kernel,
        [((512, sub), F32), ((512, sub), BF16), ((512, sub), BF16)],
        [],
        ids,
        *parts,
        gain_f,
        static=width,
    )

    theirs, w_all, w_heads = call(
        theirs_kernel,
        [((512, 5 * HD), F32), ((sub, 6 * HD), BF16), ((2, 2 * HD, sub), BF16)],
        [],
        ids,
        *weights,
        normed_sw,
        cot_sw,
    )
    (mine,) = call(mine_kernel, [((512, 5 * HD), F32)], [], ids, normed_sw, cot_sw, w_all, w_heads)
    split = ((rows, 8 * HD), BF16)
    own, *chunks = call(chunk_kernel, [((rows, 5 * HD), F32)] + [split] * 3, [], ids, mine, swap(theirs, "c"))
    chunks = [shift_x(chunks[s - 1], -s) for s in range(1, NX)]
    (partial,) = call(sum_kernel, [split], [], ids, own, *chunks)
    qa, kv = call(final_kernel, [((rows, 4 * HD), BF16), ((rows, HD), BF16)], [], ids, partial, swap(partial, "yl"))
    heads, row_sum = call(
        attend_kernel, [((rows, 6 * HD), BF16), ((1, rows), F32)], [], ids, qa, kv, swap(kv, "c")
    )
    row_sum = row_sum + swap(row_sum, "c")
    heads = [heads] + [shift_x(heads, s) for s in range(1, NX)]

    g, n = GROWS, BLOCK
    t0, up, down, t2, m2, t4a, t4b, *back = call(
        gradient_kernel,
        [
            ((g + 2 * n, HD), BF16),
            ((g + 4 * n, HD), BF16),
            ((g + 4 * n, HD), BF16),
            ((2 * n, HD), BF16),
            ((2 * n, HD), BF16),
            ((g + n, HD), BF16),
            ((g + n, HD), BF16),
        ]
        + [((rows, sub), BF16)] * 4,
        [((512, 6 * HD), BF16), ((512, 4 * HD), BF16), ((sub, 2 * HD), F32)],
        ids,
        *heads,
        *[swap(h, "c") for h in heads],
        normed_sw,
        cot_sw,
        unit_sw,
        w_all,
    )
    c4, d4 = shift_z(t4a, 2), shift_z(t4b, -2)
    a, b = shift_z(up, 1), shift_z(down, -1)
    up, down = call(relay_kernel, [((2 * g + 2 * n, HD), BF16)] * 2, [], ids, t2, m2, a, b, c4, d4)
    up, down = shift_z(up, 2), shift_z(down, -2)

    pieces = [back[0]] + [shift_x(back[s], -s) for s in range(1, NX)]
    to_same, to_other, gain_z = call(
        finish_kernel, [((n, HD), BF16)] * 2 + [((4, HD), F32)], [], ids, t0, a, b, up, down, c4, d4
    )
    gain_z, _ = lax.optimization_barrier((gain_z, swap(to_same[:g], "c")))
    (grad_input,) = call(
        input_kernel,
        [((rows, quarter), F32)],
        [],
        ids,
        *pieces,
        tokens,
        gain_f,
        total,
        row_sum,
        static=width,
    )
    arrived = (lax.ppermute(to_same, AXES, inverse(owner_perm(0))), lax.ppermute(to_other, AXES, inverse(owner_perm(1))))
    gain_z = gain_z + swap(gain_z, "yh")
    gain_x = [gain_z] + [shift_x(gain_z, s) for s in range(1, NX)]
    *arrived, grad_input, gain_z = lax.optimization_barrier((*arrived, grad_input, gain_z))
    (shared_own,) = call(shared_kernel, [((2 * PIECE, HD), BF16)], [], ids, *arrived)
    grad_query, grad_out = call(owner_kernel, [((HD, HD), F32)] * 2, [], ids, *arrived, static=loss_scale)
    shared_yl = swap(shared_own, "yl")
    grad_key, grad_value, grad_gain = call(
        join_kernel,
        [((rows, HD), F32)] * 2 + [((4 * NX, 1, HD), F32)],
        [],
        ids,
        shared_own,
        swap(shared_own, "c"),
        shared_yl,
        swap(shared_yl, "c"),
        *gain_x,
        static=loss_scale,
    )
    grad_gain = grad_gain.reshape(quarter)
    return (grad_input, grad_gain, grad_query, grad_key, grad_value, grad_out)


def solution(mesh):
    fine = Mesh(mesh.devices.reshape(2, NX, NZ, 2, 2), AXES)
    in_specs = (P(FSDP, TP), P(TP), P(FSDP, TP), P(FSDP, None), P(FSDP, None), P(TP, FSDP), P(FSDP, TP))
    out_specs = (P(FSDP, TP), P(TP), P(FSDP, TP), P(FSDP, None), P(FSDP, None), P(TP, FSDP))
    return jax.shard_map(local, mesh=fine, in_specs=in_specs, out_specs=out_specs, check_vma=False)
```

```python
import functools
import math

import jax
import jax.numpy as jnp
from jax import lax
from jax.experimental import pallas as pl
from jax.experimental.pallas import tpu as pltpu
from jax.sharding import Mesh, PartitionSpec as P

HD = 128
NX = 4
NZ = 8
AXES = ("yh", "x", "z", "yl", "c")
FSDP = ("yh", "x", "z")
TP = ("yl", "c")
F32 = jnp.float32
BF16 = jnp.bfloat16
PIECE = 32
BLOCK = 2 * HD + 2 * PIECE
GROWS = 16
VMEM = pl.BlockSpec(memory_space=pltpu.VMEM)
SMEM = pl.BlockSpec(memory_space=pltpu.SMEM)


def flat(yh, x, z, yl, c):
    return (((yh * NX + x) * NZ + z) * 2 + yl) * 2 + c


def owner_perm(flip, by):
    pairs = []
    for yh in range(2):
        for x in range(NX):
            for z in range(NZ):
                for yl in range(2):
                    for c in range(2):
                        dest_x = (x % 2) * 2 + z % 2
                        dest_z = ((z // 2) * 2 + c + by) % NZ
                        pairs.append((flat(yh, x, z, yl, c), flat(yl ^ flip, dest_x, dest_z, yh, x // 2)))
    return pairs


def inverse(pairs):
    return [(d, s) for s, d in pairs]


def shift_x(value, by):
    return lax.ppermute(value, "x", [(i, (i + by) % NX) for i in range(NX)])


def shift_z(value, by):
    return lax.ppermute(value, "z", [(i, (i + by) % NZ) for i in range(NZ)])


def swap(value, axis):
    return lax.ppermute(value, axis, [(0, 1), (1, 0)])


def dot(a, b, ca, cb):
    return lax.dot_general(a, b, (((ca,), (cb,)), ((), ())), preferred_element_type=F32)


def lanes(start, size=HD):
    return pl.ds(pl.multiple_of(start, HD), size)


def feature(at, j):
    return ((at // 2) * 8 + 2 * j + at % 2) * HD


def call(body, outs, scratch, ids, *args, static=None, aliases={}):
    body = body if static is None else functools.partial(body, static)
    return pl.pallas_call(
        body,
        out_shape=[jax.ShapeDtypeStruct(s, d) for s, d in outs],
        in_specs=[SMEM] + [VMEM] * len(args),
        out_specs=[VMEM] * len(outs),
        input_output_aliases=aliases,
        scratch_shapes=[pltpu.VMEM(s, d) for s, d in scratch],
        compiler_params=pltpu.CompilerParams(vmem_limit_bytes=16 * 2**20),
    )(ids, *args)


def spread_kernel(ids, tokens, cot, total_out, *outs):
    rows = tokens.shape[0]
    squares = jnp.zeros((rows, HD), F32)
    for s in range(NX):
        at = (ids[4] + s) % NX
        for j in range(4):
            block, cols = lanes(feature(at, j)), slice(j * HD, (j + 1) * HD)
            value = tokens[:, block]
            squares = squares + value.astype(F32) * value.astype(F32)
            outs[s][:rows, cols] = value
            outs[s][rows : 2 * rows, cols] = cot[:, block]
    total_out[...] = jnp.sum(jnp.transpose(squares), axis=0, keepdims=True)


def stamp_kernel(ids, total, *refs):
    total = total[...]
    high = total.astype(BF16).astype(F32)
    middle = (total - high).astype(BF16).astype(F32)
    extra = jnp.concatenate([high, middle, total - high - middle, jnp.zeros((GROWS - 3, HD), F32)], axis=0)
    extra = jnp.concatenate([extra] * 4, axis=1).astype(BF16)
    for out in refs[NX:]:
        out[2 * HD :] = extra


def normalize_kernel(width, ids, *refs):
    parts, (gain, unit, normed, cot) = refs[:4], refs[4:]
    for s in range(NX):
        rows = slice(s * HD, (s + 1) * HD)
        terms = parts[s][2 * HD :, :HD].astype(F32)
        total = (terms[2:3] + terms[1:2]) + terms[0:1]
        column = jnp.transpose(jnp.broadcast_to(total, (HD, HD)))
        inv = lax.rsqrt(column / width + 1e-05)
        for j in range(4):
            cols = slice(j * HD, (j + 1) * HD)
            value = parts[s][:HD, cols].astype(F32) * inv
            unit[rows, cols] = value
            normed[rows, cols] = (value * gain[:, lanes(feature(ids[4], j))]).astype(BF16)
        cot[rows] = parts[s][HD : 2 * HD]


def forward_pack_kernel(ids, same, other, same_prev, other_prev, same_next, other_next, up, down):
    n = BLOCK
    first = ids[3] == 0

    def ordered(a, b):
        a, b = a[...].astype(F32), b[...].astype(F32)
        return jnp.where(first, a, b).astype(BF16), jnp.where(first, b, a).astype(BF16)

    low, high = ordered(same, other)
    for out in (up, down):
        out[:n] = low
        out[n : 2 * n] = high
    for out, pair in ((up, (same_prev, other_prev)), (down, (same_next, other_next))):
        low, high = ordered(*pair)
        out[2 * n : 3 * n] = low
        out[3 * n :] = high


def product(out, side, normed, cot, w_all, w_out):
    w_q = w_all[:, lanes(side * 2 * HD, 2 * HD)]
    w_kv = w_all[:, lanes((4 + side) * HD)]
    w_o = w_out[side]
    for r in range(0, 512, 256):
        rows = slice(r, r + 256)
        out[rows, : 2 * HD] = dot(normed[rows], w_q, 1, 0)
        out[rows, 2 * HD : 4 * HD] = dot(cot[rows], w_o, 1, 1)
        out[rows, 4 * HD :] = dot(normed[rows], w_kv, 1, 0)


def theirs_kernel(ids, up, down, prev1, next1, far_same, far_other, normed, cot, out, w_all, w_out):
    z, c = ids[0], ids[2]

    def place(ref, base, d, half):
        zt = (z + d + NZ) % NZ
        side, j = zt % 2, zt // 2
        rows = pl.ds(pl.multiple_of(j * HD, HD), HD)
        w_all[rows, lanes(side * 2 * HD + half * HD)] = ref[base : base + HD]
        w_out[side, pl.ds(pl.multiple_of(half * HD, HD), HD), lanes(j * HD)] = ref[base + HD : base + 2 * HD]
        part = pl.ds(pl.multiple_of(j * HD + (2 * half + side) * PIECE, PIECE), PIECE)
        w_all[part, 4 * HD : 5 * HD] = ref[base + 2 * HD : base + 2 * HD + PIECE]
        w_all[part, 5 * HD : 6 * HD] = ref[base + 2 * HD + PIECE : base + BLOCK]

    for ref, base, d in (
        (up, 0, 0),
        (prev1, 0, -1),
        (prev1, 2 * BLOCK, -3),
        (next1, 0, 1),
        (next1, 2 * BLOCK, 3),
        (up, 2 * BLOCK, -2),
        (down, 2 * BLOCK, 2),
    ):
        place(ref, base, d, 0)
        place(ref, base + BLOCK, d, 1)
    yh = ids[3]
    place(far_same, 0, 4, yh)
    place(far_other, 0, 4, 1 - yh)
    product(out, 1 - c, normed, cot, w_all, w_out)


def mine_kernel(ids, normed, cot, w_all, w_out, out):
    product(out, ids[2], normed, cot, w_all, w_out)


def split_store(ref, total):
    for start, size, at in ((0, 2 * HD, 0), (4 * HD, HD, 6 * HD)):
        value = total[:, start : start + size]
        high = value.astype(BF16)
        ref[:, at : at + size] = high
        ref[:, at + size : at + 2 * size] = (value - high.astype(F32)).astype(BF16)
    ref[:, 4 * HD : 6 * HD] = total[:, 2 * HD : 4 * HD].astype(BF16)


def joined(ref):
    value = ref[...].astype(F32)
    return jnp.concatenate(
        [
            value[:, : 2 * HD] + value[:, 2 * HD : 4 * HD],
            value[:, 4 * HD : 6 * HD],
            value[:, 6 * HD : 7 * HD] + value[:, 7 * HD :],
        ],
        axis=1,
    )


def chunk_kernel(ids, mine, got, own, *outs):
    own[...] = mine[:HD] + got[:HD]
    for s in range(1, NX):
        rows = slice(s * HD, (s + 1) * HD)
        split_store(outs[s - 1], mine[rows] + got[rows])


def sum_kernel(ids, own, a, b, c, out):
    split_store(out, own[...] + joined(a) + joined(b) + joined(c))


def final_kernel(ids, mine, got, qa, kv):
    total = (joined(mine) + joined(got)).astype(BF16)
    qa[...] = total[:, : 4 * HD]
    kv[...] = total[:, 4 * HD :]


def attend_kernel(ids, qa, kv_mine, kv_theirs, out, row_out):
    first = ids[2] == 0
    mine, theirs = kv_mine[...].astype(F32), kv_theirs[...].astype(F32)
    key_rows = jnp.where(first, mine, theirs).astype(BF16)
    value_rows = jnp.where(first, theirs, mine).astype(BF16)
    causal = lax.broadcasted_iota(jnp.int32, (HD, HD), 0) >= lax.broadcasted_iota(jnp.int32, (HD, HD), 1)
    keys = jnp.zeros((HD, HD), F32)
    values = jnp.zeros((HD, HD), F32)
    row_terms = jnp.zeros((HD, HD), F32)
    for h in range(2):
        query = qa[:, h * HD : (h + 1) * HD]
        attn_grad = qa[:, (2 + h) * HD : (3 + h) * HD]
        scores = dot(query, key_rows, 1, 1) * HD ** (-0.5)
        scores = jnp.where(causal, scores, jnp.float32(-1e30))
        shifted = jnp.exp(scores - jnp.max(scores, axis=-1, keepdims=True))
        softmax_out = shifted / jnp.sum(shifted, axis=-1, keepdims=True)
        rounded = softmax_out.astype(BF16)
        dprob = dot(attn_grad, value_rows, 1, 1)
        dscore = softmax_out * (dprob - jnp.sum(dprob * softmax_out, axis=-1, keepdims=True)) * HD ** (-0.5)
        dscore = dscore.astype(BF16)
        d_query = dot(dscore, key_rows, 1, 0).astype(BF16)
        out[:, h * HD : (h + 1) * HD] = d_query
        row_terms = row_terms + d_query.astype(F32) * query.astype(F32)
        out[:, (2 + h) * HD : (3 + h) * HD] = dot(rounded, value_rows, 1, 0).astype(BF16)
        keys = keys + dot(dscore, query, 0, 0).astype(BF16).astype(F32)
        values = values + dot(rounded, attn_grad, 0, 0).astype(BF16).astype(F32)
    out[:, 4 * HD : 5 * HD] = keys.astype(BF16)
    out[:, 5 * HD :] = values.astype(BF16)
    row_terms = row_terms + keys * key_rows.astype(F32) + values * value_rows.astype(F32)
    row_out[...] = jnp.sum(jnp.transpose(row_terms), axis=0, keepdims=True)


def gradient_kernel(ids, *refs):
    mine, theirs, (normed, cot, unit, w_all) = refs[:4], refs[4:8], refs[8:12]
    (t0, up, down, t2, m2, far_same, far_other), back = refs[12:19], refs[19:23]
    heads, attended, shared = refs[23:]
    z, c, yh = ids[0], ids[2], ids[3]
    for s in range(NX):
        rows = slice(s * HD, (s + 1) * HD)
        for ref, side in ((mine[s], c), (theirs[s], 1 - c)):
            heads[rows, lanes(side * 2 * HD, 2 * HD)] = ref[:, : 2 * HD]
            attended[rows, lanes(side * 2 * HD, 2 * HD)] = ref[:, 2 * HD : 4 * HD]
        total = mine[s][:, 4 * HD :].astype(F32) + theirs[s][:, 4 * HD :].astype(F32)
        heads[rows, 4 * HD :] = total.astype(BF16)

    gain_sum = jnp.zeros((1, 4 * HD), F32)
    for s in range(NX):
        rows = slice(s * HD, (s + 1) * HD)
        term = dot(heads[rows], w_all[...], 1, 1)
        back[s][:HD] = term.astype(BF16)
        gain_sum = gain_sum + jnp.sum(term * unit[rows], axis=0, keepdims=True)
    high = gain_sum.astype(BF16).astype(F32)
    gain_rows = jnp.concatenate([high, gain_sum - high, jnp.zeros((GROWS - 2, 4 * HD), F32)], axis=0)
    for ref in back:
        ref[HD:] = gain_rows.astype(BF16)

    shared[...] = dot(normed[...], heads[:, 4 * HD :], 0, 0)
    n = BLOCK
    for d, out_first, out_second in (
        (0, t0.at[:n], t0.at[n:]),
        (1, up.at[:n], up.at[n : 2 * n]),
        (3, up.at[2 * n : 3 * n], up.at[3 * n :]),
        (-1, down.at[:n], down.at[n : 2 * n]),
        (-3, down.at[2 * n : 3 * n], down.at[3 * n :]),
        (2, t2.at[:n], t2.at[n:]),
        (-2, m2.at[:n], m2.at[n:]),
        (4, far_same, far_other),
    ):
        zt = (z + d + NZ) % NZ
        side, j = zt % 2, zt // 2
        g_q = dot(normed[:, lanes(j * HD)], heads[:, lanes(side * 2 * HD, 2 * HD)], 0, 0).astype(BF16)
        g_o = dot(attended[:, lanes(side * 2 * HD, 2 * HD)], cot[:, lanes(j * HD)], 0, 0).astype(BF16)
        for half, out in enumerate((out_first, out_second)):
            if d == 4:
                half = yh if half == 0 else 1 - yh
                low, high = g_q[:, :HD].astype(F32), g_q[:, HD:].astype(F32)
                out[:HD] = jnp.where(half == 0, low, high).astype(BF16)
                low, high = g_o[:HD].astype(F32), g_o[HD:].astype(F32)
                out[HD : 2 * HD] = jnp.where(half == 0, low, high).astype(BF16)
            else:
                out[:HD] = g_q[:, half * HD : (half + 1) * HD]
                out[HD : 2 * HD] = g_o[half * HD : (half + 1) * HD]
            part = shared[pl.ds(pl.multiple_of(j * HD + (2 * half + side) * PIECE, PIECE), PIECE), :].astype(BF16)
            out[2 * HD : 2 * HD + PIECE] = part[:, :HD]
            out[2 * HD + PIECE :] = part[:, HD:]


def relay_kernel(ids, t0, t2, m2, a, b, *refs):
    pieces, outs = refs[:NX], refs[NX:]
    n = BLOCK
    first = ids[3] == 0
    middle = t0[...].astype(F32) + a[: 2 * n].astype(F32) + b[: 2 * n].astype(F32)
    above = t2[...].astype(F32) + a[2 * n :].astype(F32)
    below = m2[...].astype(F32) + b[2 * n :].astype(F32)
    for s, total in enumerate((middle, above, below)):
        outs[2 * s][...] = jnp.where(first, total[:n], total[n:]).astype(BF16)
        outs[2 * s + 1][...] = jnp.where(first, total[n:], total[:n]).astype(BF16)
    for s, ref in enumerate(pieces):
        rows = ref[HD:].astype(F32)
        sums = rows[0:1] + rows[1:2]
        for j in range(4):
            outs[6][4 * s + j : 4 * s + j + 1] = sums[:, j * HD : (j + 1) * HD]


def input_kernel(sizes, ids, a, b, c, d, tokens, gain, total, row_sum, *refs):
    width, scale = sizes
    arrived, (out, grad_query, grad_out) = refs[:8], refs[8:]
    inv = lax.rsqrt(jnp.transpose(jnp.broadcast_to(total[...], (HD, HD))) / width + 1e-05)
    row_mean = jnp.transpose(jnp.broadcast_to(row_sum[...], (HD, HD))) / width
    for s, ref in enumerate((a, b, c, d)):
        at = (ids[4] + s) % NX
        for j in range(4):
            cols = lanes(feature(at, j))
            unit = tokens[:, cols].astype(F32) * inv
            scaled = ref[:HD, j * HD : (j + 1) * HD].astype(F32) * gain[:, cols]
            out[:, cols] = inv * (scaled - unit * row_mean)
    for grad, at in ((grad_query, slice(0, HD)), (grad_out, slice(HD, 2 * HD))):
        sums = arrived[0][at].astype(F32)
        for ref in arrived[1:]:
            sums = sums + ref[at].astype(F32)
        grad[...] = sums * scale


def shared_kernel(ids, *refs):
    total = refs[0][2 * HD :].astype(F32)
    for ref in refs[1:8]:
        total = total + ref[2 * HD :].astype(F32)
    refs[8][...] = total.astype(BF16)


def join_kernel(scale, ids, own, by_c, by_yl, by_both, gains, grad_key, grad_value, grad_gain):
    yl, c, x = ids[1], ids[2], ids[4]
    for ref, at in ((own, 2 * yl + c), (by_c, 2 * yl + 1 - c), (by_yl, 2 - 2 * yl + c), (by_both, 3 - 2 * yl - c)):
        rows = pl.ds(pl.multiple_of(at * PIECE, PIECE), PIECE)
        grad_key[rows] = ref[:PIECE].astype(F32) * scale
        grad_value[rows] = ref[PIECE:].astype(F32) * scale
    for s in range(NX):
        at = (x + s) % NX
        for j in range(4):
            grad_gain[(at // 2) * 8 + 2 * j + at % 2] = gains[4 * s + j : 4 * s + j + 1] * scale


def local(tokens, gain, w_query, w_key, w_value, w_out, cotangent):
    rows, quarter = tokens.shape
    sub = quarter // NX
    width = quarter * 4
    yh, x, z, yl, c = (lax.axis_index(a) for a in AXES)
    ids = jnp.stack([z, yl, c, yh, x]).astype(jnp.int32)
    head = yl * 2 + c
    loss_scale = 1.0 / math.sqrt(rows * 64)

    pack = jnp.concatenate(
        [
            w_query,
            w_out,
            lax.dynamic_slice_in_dim(w_key, head * PIECE, PIECE, 0),
            lax.dynamic_slice_in_dim(w_value, head * PIECE, PIECE, 0),
        ],
        axis=0,
    )
    blocks = [lax.ppermute(pack, AXES, owner_perm(flip, by)) for by in (0, 2, -2) for flip in range(2)]
    far = [lax.ppermute(pack, AXES, owner_perm(flip, 4)) for flip in range(2)]
    part_shape = ((2 * rows + GROWS, sub), BF16)
    total, *parts = call(spread_kernel, [((1, rows), F32)] + [part_shape] * 4, [], ids, tokens, cotangent)
    total = total + swap(total, "c")
    *blocks, total = lax.optimization_barrier((*blocks, total))
    total = total + swap(total, "yl")
    relays = call(forward_pack_kernel, [((4 * BLOCK, HD), BF16)] * 2, [], ids, *blocks)
    prev1, next1 = shift_z(relays[0], 1), shift_z(relays[1], -1)
    weights = (relays[0], relays[1], prev1, next1, *far)

    parts = call(stamp_kernel, [part_shape] * 4, [], ids, total, *parts, aliases={2 + s: s for s in range(4)})
    parts = [parts[0]] + [shift_x(parts[s], s) for s in range(1, NX)]
    gain_f = gain.astype(F32).reshape(1, quarter)
    unit_sw, normed_sw, cot_sw = call(
        normalize_kernel,
        [((512, sub), F32), ((512, sub), BF16), ((512, sub), BF16)],
        [],
        ids,
        *parts,
        gain_f,
        static=width,
    )

    theirs, w_all, w_heads = call(
        theirs_kernel,
        [((512, 5 * HD), F32), ((sub, 6 * HD), BF16), ((2, 2 * HD, sub), BF16)],
        [],
        ids,
        *weights,
        normed_sw,
        cot_sw,
    )
    (mine,) = call(mine_kernel, [((512, 5 * HD), F32)], [], ids, normed_sw, cot_sw, w_all, w_heads)
    split = ((rows, 8 * HD), BF16)
    own, *chunks = call(chunk_kernel, [((rows, 5 * HD), F32)] + [split] * 3, [], ids, mine, swap(theirs, "c"))
    chunks = [shift_x(chunks[s - 1], -s) for s in range(1, NX)]
    (partial,) = call(sum_kernel, [split], [], ids, own, *chunks)
    qa, kv = call(final_kernel, [((rows, 4 * HD), BF16), ((rows, HD), BF16)], [], ids, partial, swap(partial, "yl"))
    heads, row_sum = call(
        attend_kernel, [((rows, 6 * HD), BF16), ((1, rows), F32)], [], ids, qa, kv, swap(kv, "c")
    )
    row_sum = row_sum + swap(row_sum, "c")
    heads = [heads] + [shift_x(heads, s) for s in range(1, NX)]

    n = BLOCK
    t0, up, down, t2, m2, far_same, far_other, *back = call(
        gradient_kernel,
        [
            ((2 * n, HD), BF16),
            ((4 * n, HD), BF16),
            ((4 * n, HD), BF16),
            ((2 * n, HD), BF16),
            ((2 * n, HD), BF16),
            ((n, HD), BF16),
            ((n, HD), BF16),
        ]
        + [((rows + GROWS, sub), BF16)] * 4,
        [((512, 6 * HD), BF16), ((512, 4 * HD), BF16), ((sub, 2 * HD), F32)],
        ids,
        *heads,
        *[swap(h, "c") for h in heads],
        normed_sw,
        cot_sw,
        unit_sw,
        w_all,
    )
    a, b = shift_z(up, 1), shift_z(down, -1)
    arrived = [
        lax.ppermute(far_same, AXES, inverse(owner_perm(0, 4))),
        lax.ppermute(far_other, AXES, inverse(owner_perm(1, 4))),
    ]
    pieces = [back[0]] + [shift_x(back[s], -s) for s in range(1, NX)]
    a, b, *rest = lax.optimization_barrier((a, b, *pieces, *arrived))
    pieces, arrived = rest[:NX], rest[NX:]
    *sums, gain_z = call(
        relay_kernel, [((n, HD), BF16)] * 6 + [((4 * NX, HD), F32)], [], ids, t0, t2, m2, a, b, *pieces
    )
    arrived += [
        lax.ppermute(sums[2 * s + flip], AXES, inverse(owner_perm(flip, -by)))
        for s, by in enumerate((0, 2, -2))
        for flip in range(2)
    ]
    gain_z, arrived[2] = lax.optimization_barrier((gain_z, arrived[2]))
    gain_z = gain_z + shift_z(gain_z, 1)
    gain_z, arrived[4] = lax.optimization_barrier((gain_z, arrived[4]))
    gain_z = gain_z + shift_z(gain_z, 2)
    *arrived, gain_z = lax.optimization_barrier((*arrived, gain_z))
    gain_z = gain_z + shift_z(gain_z, 4)
    gain_z = gain_z + swap(gain_z, "yh")

    (shared_own,) = call(shared_kernel, [((2 * PIECE, HD), BF16)], [], ids, *arrived)
    grad_input, grad_query, grad_out = call(
        input_kernel,
        [((rows, quarter), F32)] + [((HD, HD), F32)] * 2,
        [],
        ids,
        *pieces,
        tokens,
        gain_f,
        total,
        row_sum,
        *arrived,
        static=(width, loss_scale),
    )
    shared_yl = swap(shared_own, "yl")
    grad_key, grad_value, grad_gain = call(
        join_kernel,
        [((rows, HD), F32)] * 2 + [((4 * NX, 1, HD), F32)],
        [],
        ids,
        shared_own,
        swap(shared_own, "c"),
        shared_yl,
        swap(shared_yl, "c"),
        gain_z,
        static=loss_scale,
    )
    grad_gain = grad_gain.reshape(quarter)
    return (grad_input, grad_gain, grad_query, grad_key, grad_value, grad_out)


def solution(mesh):
    fine = Mesh(mesh.devices.reshape(2, NX, NZ, 2, 2), AXES)
    in_specs = (P(FSDP, TP), P(TP), P(FSDP, TP), P(FSDP, None), P(FSDP, None), P(TP, FSDP), P(FSDP, TP))
    out_specs = (P(FSDP, TP), P(TP), P(FSDP, TP), P(FSDP, None), P(FSDP, None), P(TP, FSDP))
    return jax.shard_map(local, mesh=fine, in_specs=in_specs, out_specs=out_specs, check_vma=False)
```

```python
import functools
import math

import jax
import jax.numpy as jnp
from jax import lax
from jax.experimental import pallas as pl
from jax.experimental.pallas import tpu as pltpu
from jax.sharding import Mesh, PartitionSpec as P

HD = 128
NX = 4
NZ = 8
AXES = ("yh", "x", "z", "yl", "c")
FSDP = ("yh", "x", "z")
TP = ("yl", "c")
F32 = jnp.float32
BF16 = jnp.bfloat16
PIECE = 32
BLOCK = 2 * HD + 2 * PIECE
GROWS = 16
VMEM = pl.BlockSpec(memory_space=pltpu.VMEM)
SMEM = pl.BlockSpec(memory_space=pltpu.SMEM)


def flat(yh, x, z, yl, c):
    return (((yh * NX + x) * NZ + z) * 2 + yl) * 2 + c


def owner_perm(flip):
    pairs = []
    for yh in range(2):
        for x in range(NX):
            for z in range(NZ):
                for yl in range(2):
                    for c in range(2):
                        dest_x = (x % 2) * 2 + z % 2
                        dest_z = (z // 2) * 2 + c
                        pairs.append((flat(yh, x, z, yl, c), flat(yl ^ flip, dest_x, dest_z, yh, x // 2)))
    return pairs


def inverse(pairs):
    return [(d, s) for s, d in pairs]


def shift_x(value, by):
    return lax.ppermute(value, "x", [(i, (i + by) % NX) for i in range(NX)])


def shift_z(value, by):
    return lax.ppermute(value, "z", [(i, (i + by) % NZ) for i in range(NZ)])


def swap(value, axis):
    return lax.ppermute(value, axis, [(0, 1), (1, 0)])


def dot(a, b, ca, cb):
    return lax.dot_general(a, b, (((ca,), (cb,)), ((), ())), preferred_element_type=F32)


def lanes(start, size=HD):
    return pl.ds(pl.multiple_of(start, HD), size)


def feature(at, j):
    return ((at // 2) * 8 + 2 * j + at % 2) * HD


def call(body, outs, scratch, ids, *args, static=None, aliases={}):
    body = body if static is None else functools.partial(body, static)
    return pl.pallas_call(
        body,
        out_shape=[jax.ShapeDtypeStruct(s, d) for s, d in outs],
        in_specs=[SMEM] + [VMEM] * len(args),
        out_specs=[VMEM] * len(outs),
        input_output_aliases=aliases,
        scratch_shapes=[pltpu.VMEM(s, d) for s, d in scratch],
        compiler_params=pltpu.CompilerParams(vmem_limit_bytes=16 * 2**20),
    )(ids, *args)


def spread_kernel(ids, tokens, cot, total_out, *outs):
    rows = tokens.shape[0]
    squares = jnp.zeros((rows, HD), F32)
    for s in range(NX):
        at = (ids[4] + s) % NX
        for j in range(4):
            block, cols = lanes(feature(at, j)), slice(j * HD, (j + 1) * HD)
            value = tokens[:, block]
            squares = squares + value.astype(F32) * value.astype(F32)
            outs[s][:rows, cols] = value
            outs[s][rows : 2 * rows, cols] = cot[:, block]
    total_out[...] = jnp.sum(jnp.transpose(squares), axis=0, keepdims=True)


def stamp_kernel(ids, total, *refs):
    total = total[...]
    high = total.astype(BF16).astype(F32)
    middle = (total - high).astype(BF16).astype(F32)
    extra = jnp.concatenate([high, middle, total - high - middle, jnp.zeros((GROWS - 3, HD), F32)], axis=0)
    extra = jnp.concatenate([extra] * 4, axis=1).astype(BF16)
    for out in refs[NX:]:
        out[2 * HD :] = extra


def normalize_kernel(width, ids, *refs):
    parts, (gain, unit, normed, cot) = refs[:4], refs[4:]
    for s in range(NX):
        rows = slice(s * HD, (s + 1) * HD)
        terms = parts[s][2 * HD :, :HD].astype(F32)
        total = (terms[2:3] + terms[1:2]) + terms[0:1]
        column = jnp.transpose(jnp.broadcast_to(total, (HD, HD)))
        inv = lax.rsqrt(column / width + 1e-05)
        for j in range(4):
            cols = slice(j * HD, (j + 1) * HD)
            value = parts[s][:HD, cols].astype(F32) * inv
            unit[rows, cols] = value
            normed[rows, cols] = (value * gain[:, lanes(feature(ids[4], j))]).astype(BF16)
        cot[rows] = parts[s][HD : 2 * HD]


def forward_pack_kernel(ids, both, prev, after, up, down, far_first, far_second):
    for out, ref in ((up, prev), (down, after)):
        out[: 2 * BLOCK] = both[...]
        out[2 * BLOCK :] = ref[...]
    far_first[...] = prev[:BLOCK]
    far_second[...] = after[BLOCK:]


def product(out, side, normed, cot, w_all, w_out):
    w_q = w_all[:, lanes(side * 2 * HD, 2 * HD)]
    w_kv = w_all[:, lanes((4 + side) * HD)]
    w_o = w_out[side]
    for r in range(0, 512, 256):
        rows = slice(r, r + 256)
        out[rows, : 2 * HD] = dot(normed[rows], w_q, 1, 0)
        out[rows, 2 * HD : 4 * HD] = dot(cot[rows], w_o, 1, 1)
        out[rows, 4 * HD :] = dot(normed[rows], w_kv, 1, 0)


def theirs_kernel(ids, both, prev1, next1, prev2, next2, far_first, far_second, normed, cot, out, w_all, w_out):
    z, c = ids[0], ids[2]

    def place(ref, base, d, half):
        zt = (z + d + NZ) % NZ
        side, j = zt % 2, zt // 2
        rows = pl.ds(pl.multiple_of(j * HD, HD), HD)
        w_all[rows, lanes(side * 2 * HD + half * HD)] = ref[base : base + HD]
        w_out[side, half * HD : (half + 1) * HD, lanes(j * HD)] = ref[base + HD : base + 2 * HD]
        part = pl.ds(pl.multiple_of(j * HD + (2 * half + side) * PIECE, PIECE), PIECE)
        w_all[part, 4 * HD : 5 * HD] = ref[base + 2 * HD : base + 2 * HD + PIECE]
        w_all[part, 5 * HD : 6 * HD] = ref[base + 2 * HD + PIECE : base + BLOCK]

    for ref, base, d in (
        (both, 0, 0),
        (prev1, 0, -1),
        (prev1, 2 * BLOCK, -3),
        (next1, 0, 1),
        (next1, 2 * BLOCK, 3),
        (prev2, 0, -2),
        (next2, 0, 2),
    ):
        place(ref, base, d, 0)
        place(ref, base + BLOCK, d, 1)
    place(far_first, 0, 4, 0)
    place(far_second, 0, 4, 1)
    product(out, 1 - c, normed, cot, w_all, w_out)


def mine_kernel(ids, normed, cot, w_all, w_out, out):
    product(out, ids[2], normed, cot, w_all, w_out)


def split_store(ref, total):
    for start, size, at in ((0, 2 * HD, 0), (4 * HD, HD, 6 * HD)):
        value = total[:, start : start + size]
        high = value.astype(BF16)
        ref[:, at : at + size] = high
        ref[:, at + size : at + 2 * size] = (value - high.astype(F32)).astype(BF16)
    ref[:, 4 * HD : 6 * HD] = total[:, 2 * HD : 4 * HD].astype(BF16)


def joined(ref):
    value = ref[...].astype(F32)
    return jnp.concatenate(
        [
            value[:, : 2 * HD] + value[:, 2 * HD : 4 * HD],
            value[:, 4 * HD : 6 * HD],
            value[:, 6 * HD : 7 * HD] + value[:, 7 * HD :],
        ],
        axis=1,
    )


def chunk_kernel(ids, mine, got, own, *outs):
    own[...] = mine[:HD] + got[:HD]
    for s in range(1, NX):
        rows = slice(s * HD, (s + 1) * HD)
        split_store(outs[s - 1], mine[rows] + got[rows])


def sum_kernel(ids, own, a, b, c, out):
    split_store(out, own[...] + joined(a) + joined(b) + joined(c))


def final_kernel(ids, mine, got, qa, kv):
    total = (joined(mine) + joined(got)).astype(BF16)
    qa[...] = total[:, : 4 * HD]
    kv[...] = total[:, 4 * HD :]


def attend_kernel(ids, qa, kv_mine, kv_theirs, out, row_out):
    first = ids[2] == 0
    mine, theirs = kv_mine[...].astype(F32), kv_theirs[...].astype(F32)
    key_rows = jnp.where(first, mine, theirs).astype(BF16)
    value_rows = jnp.where(first, theirs, mine).astype(BF16)
    causal = lax.broadcasted_iota(jnp.int32, (HD, HD), 0) >= lax.broadcasted_iota(jnp.int32, (HD, HD), 1)
    keys = jnp.zeros((HD, HD), F32)
    values = jnp.zeros((HD, HD), F32)
    row_terms = jnp.zeros((HD, HD), F32)
    for h in range(2):
        query = qa[:, h * HD : (h + 1) * HD]
        attn_grad = qa[:, (2 + h) * HD : (3 + h) * HD]
        scores = dot(query, key_rows, 1, 1) * HD ** (-0.5)
        scores = jnp.where(causal, scores, jnp.float32(-1e30))
        shifted = jnp.exp(scores - jnp.max(scores, axis=-1, keepdims=True))
        softmax_out = shifted / jnp.sum(shifted, axis=-1, keepdims=True)
        rounded = softmax_out.astype(BF16)
        dprob = dot(attn_grad, value_rows, 1, 1)
        dscore = softmax_out * (dprob - jnp.sum(dprob * softmax_out, axis=-1, keepdims=True)) * HD ** (-0.5)
        dscore = dscore.astype(BF16)
        d_query = dot(dscore, key_rows, 1, 0).astype(BF16)
        out[:, h * HD : (h + 1) * HD] = d_query
        row_terms = row_terms + d_query.astype(F32) * query.astype(F32)
        out[:, (2 + h) * HD : (3 + h) * HD] = dot(rounded, value_rows, 1, 0).astype(BF16)
        keys = keys + dot(dscore, query, 0, 0).astype(BF16).astype(F32)
        values = values + dot(rounded, attn_grad, 0, 0).astype(BF16).astype(F32)
    out[:, 4 * HD : 5 * HD] = keys.astype(BF16)
    out[:, 5 * HD :] = values.astype(BF16)
    row_terms = row_terms + keys * key_rows.astype(F32) + values * value_rows.astype(F32)
    row_out[...] = jnp.sum(jnp.transpose(row_terms), axis=0, keepdims=True)


def gradient_kernel(ids, *refs):
    mine, theirs, (normed, cot, unit, w_all) = refs[:4], refs[4:8], refs[8:12]
    (t0, up, down, t2, m2, t4a, t4b), back = refs[12:19], refs[19:23]
    heads, attended, shared = refs[23:]
    z, c = ids[0], ids[2]
    for s in range(NX):
        rows = slice(s * HD, (s + 1) * HD)
        for ref, side in ((mine[s], c), (theirs[s], 1 - c)):
            heads[rows, lanes(side * 2 * HD, 2 * HD)] = ref[:, : 2 * HD]
            attended[rows, lanes(side * 2 * HD, 2 * HD)] = ref[:, 2 * HD : 4 * HD]
        total = mine[s][:, 4 * HD :].astype(F32) + theirs[s][:, 4 * HD :].astype(F32)
        heads[rows, 4 * HD :] = total.astype(BF16)

    gain_sum = jnp.zeros((1, 4 * HD), F32)
    for s in range(NX):
        rows = slice(s * HD, (s + 1) * HD)
        term = dot(heads[rows], w_all[...], 1, 1)
        back[s][:HD] = term.astype(BF16)
        gain_sum = gain_sum + jnp.sum(term * unit[rows], axis=0, keepdims=True)
    gain_rows = jnp.concatenate([gain_sum[:, j * HD : (j + 1) * HD] for j in range(4)], axis=0)
    high = gain_rows.astype(BF16).astype(F32)
    gain_rows = jnp.concatenate([high, gain_rows - high, jnp.zeros((8, HD), F32)], axis=0).astype(BF16)

    shared[...] = dot(normed[...], heads[:, 4 * HD :], 0, 0)
    g, n = GROWS, BLOCK
    for ref in (t0, up, down, t4a, t4b):
        ref[:g] = gain_rows
    for d, out_first, out_second in (
        (0, t0.at[g : g + n], t0.at[g + n :]),
        (1, up.at[g : g + n], up.at[g + n : g + 2 * n]),
        (3, up.at[g + 2 * n : g + 3 * n], up.at[g + 3 * n :]),
        (-1, down.at[g : g + n], down.at[g + n : g + 2 * n]),
        (-3, down.at[g + 2 * n : g + 3 * n], down.at[g + 3 * n :]),
        (2, t2.at[:n], t2.at[n:]),
        (-2, m2.at[:n], m2.at[n:]),
        (4, t4a.at[g:], t4b.at[g:]),
    ):
        zt = (z + d + NZ) % NZ
        side, j = zt % 2, zt // 2
        g_q = dot(normed[:, lanes(j * HD)], heads[:, lanes(side * 2 * HD, 2 * HD)], 0, 0).astype(BF16)
        g_o = dot(attended[:, lanes(side * 2 * HD, 2 * HD)], cot[:, lanes(j * HD)], 0, 0).astype(BF16)
        for half, out in enumerate((out_first, out_second)):
            out[:HD] = g_q[:, half * HD : (half + 1) * HD]
            out[HD : 2 * HD] = g_o[half * HD : (half + 1) * HD]
            part = shared[pl.ds(pl.multiple_of(j * HD + (2 * half + side) * PIECE, PIECE), PIECE), :].astype(BF16)
            out[2 * HD : 2 * HD + PIECE] = part[:, :HD]
            out[2 * HD + PIECE :] = part[:, HD:]


def relay_kernel(ids, t2, m2, a, b, c, d, t0, *refs):
    up, down, *back = refs[NX:]
    g, n = GROWS, BLOCK
    total = t2[...].astype(F32) + a[g + 2 * n :].astype(F32)
    up[:n] = (total[:n] + c[g:].astype(F32)).astype(BF16)
    up[n:] = total[n:].astype(BF16)
    total = m2[...].astype(F32) + b[g + 2 * n :].astype(F32)
    down[:n] = total[:n].astype(BF16)
    down[n:] = (total[n:] + d[g:].astype(F32)).astype(BF16)
    three = t0[:g].astype(F32) + a[:g].astype(F32) + b[:g].astype(F32)
    five = three + c[:g].astype(F32) + d[:g].astype(F32)
    terms = []
    for rows in (five, three):
        value = rows[:4] + rows[4:8]
        high = value.astype(BF16).astype(F32)
        terms += [high, value - high]
    for j in range(4):
        rows = jnp.concatenate([t[j : j + 1] for t in terms] + [jnp.zeros((g - 4, HD), F32)], axis=0).astype(BF16)
        for ref in back:
            ref[HD:, j * HD : (j + 1) * HD] = rows


def finish_kernel(ids, t0, a, b, up, down, same, other):
    g, n = GROWS, BLOCK
    flip = ids[3]
    near = slice(g, g + 2 * n)
    total = t0[near].astype(F32) + a[near].astype(F32) + b[near].astype(F32)
    total = total + up[...].astype(F32) + down[...].astype(F32)
    same[...] = jnp.where(flip == 0, total[:n], total[n:]).astype(BF16)
    other[...] = jnp.where(flip == 0, total[n:], total[:n]).astype(BF16)


def gain_kernel(ids, *refs):
    five, three = refs[NX:]
    for s in range(NX):
        rows = refs[s][HD:].astype(F32)
        for out, at in ((five, 0), (three, 2)):
            value = rows[at : at + 1] + rows[at + 1 : at + 2]
            for j in range(4):
                out[4 * s + j : 4 * s + j + 1] = value[:, j * HD : (j + 1) * HD]


def input_kernel(sizes, ids, a, b, c, d, tokens, gain, total, row_sum, same, other, out, grad_query, grad_out):
    width, scale = sizes
    inv = lax.rsqrt(jnp.transpose(jnp.broadcast_to(total[...], (HD, HD))) / width + 1e-05)
    row_mean = jnp.transpose(jnp.broadcast_to(row_sum[...], (HD, HD))) / width
    for s, ref in enumerate((a, b, c, d)):
        at = (ids[4] + s) % NX
        for j in range(4):
            cols = lanes(feature(at, j))
            unit = tokens[:, cols].astype(F32) * inv
            scaled = ref[:HD, j * HD : (j + 1) * HD].astype(F32) * gain[:, cols]
            out[:, cols] = inv * (scaled - unit * row_mean)
    for grad, at in ((grad_query, slice(0, HD)), (grad_out, slice(HD, 2 * HD))):
        grad[...] = (same[at].astype(F32) + other[at].astype(F32)) * scale


def shared_kernel(ids, a, b, shared):
    shared[...] = (a[2 * HD :].astype(F32) + b[2 * HD :].astype(F32)).astype(BF16)


def join_kernel(scale, ids, own, by_c, by_yl, by_both, gains, grad_key, grad_value, grad_gain):
    yl, c, x = ids[1], ids[2], ids[4]
    for ref, at in ((own, 2 * yl + c), (by_c, 2 * yl + 1 - c), (by_yl, 2 - 2 * yl + c), (by_both, 3 - 2 * yl - c)):
        rows = pl.ds(pl.multiple_of(at * PIECE, PIECE), PIECE)
        grad_key[rows] = ref[:PIECE].astype(F32) * scale
        grad_value[rows] = ref[PIECE:].astype(F32) * scale
    for s in range(NX):
        at = (x + s) % NX
        for j in range(4):
            grad_gain[(at // 2) * 8 + 2 * j + at % 2] = gains[4 * s + j : 4 * s + j + 1] * scale


def local(tokens, gain, w_query, w_key, w_value, w_out, cotangent):
    rows, quarter = tokens.shape
    sub = quarter // NX
    width = quarter * 4
    yh, x, z, yl, c = (lax.axis_index(a) for a in AXES)
    ids = jnp.stack([z, yl, c, yh, x]).astype(jnp.int32)
    head = yl * 2 + c
    loss_scale = 1.0 / math.sqrt(rows * 64)

    pack = jnp.concatenate(
        [
            w_query,
            w_out,
            lax.dynamic_slice_in_dim(w_key, head * PIECE, PIECE, 0),
            lax.dynamic_slice_in_dim(w_value, head * PIECE, PIECE, 0),
        ],
        axis=0,
    )
    same = lax.ppermute(pack, AXES, owner_perm(0))
    other = lax.ppermute(pack, AXES, owner_perm(1))
    part_shape = ((2 * rows + GROWS, sub), BF16)
    total, *parts = call(spread_kernel, [((1, rows), F32)] + [part_shape] * 4, [], ids, tokens, cotangent)
    total = total + swap(total, "c")
    same, other, total = lax.optimization_barrier((same, other, total))
    total = total + swap(total, "yl")
    both = jnp.where(yh == 0, jnp.concatenate([same, other]), jnp.concatenate([other, same]))
    prev2, next2 = shift_z(both, 2), shift_z(both, -2)
    double, half_shape = ((4 * BLOCK, HD), BF16), ((BLOCK, HD), BF16)
    relays = call(forward_pack_kernel, [double] * 2 + [half_shape] * 2, [], ids, both, prev2, next2)
    prev1, next1 = shift_z(relays[0], 1), shift_z(relays[1], -1)
    far_first, far_second = shift_z(relays[2], 2), shift_z(relays[3], -2)
    weights = (both, prev1, next1, prev2, next2, far_first, far_second)

    parts = call(stamp_kernel, [part_shape] * 4, [], ids, total, *parts, aliases={2 + s: s for s in range(4)})
    parts = [parts[0]] + [shift_x(parts[s], s) for s in range(1, NX)]
    gain_f = gain.astype(F32).reshape(1, quarter)
    unit_sw, normed_sw, cot_sw = call(
        normalize_kernel,
        [((512, sub), F32), ((512, sub), BF16), ((512, sub), BF16)],
        [],
        ids,
        *parts,
        gain_f,
        static=width,
    )

    theirs, w_all, w_heads = call(
        theirs_kernel,
        [((512, 5 * HD), F32), ((sub, 6 * HD), BF16), ((2, 2 * HD, sub), BF16)],
        [],
        ids,
        *weights,
        normed_sw,
        cot_sw,
    )
    (mine,) = call(mine_kernel, [((512, 5 * HD), F32)], [], ids, normed_sw, cot_sw, w_all, w_heads)
    split = ((rows, 8 * HD), BF16)
    own, *chunks = call(chunk_kernel, [((rows, 5 * HD), F32)] + [split] * 3, [], ids, mine, swap(theirs, "c"))
    chunks = [shift_x(chunks[s - 1], -s) for s in range(1, NX)]
    (partial,) = call(sum_kernel, [split], [], ids, own, *chunks)
    qa, kv = call(final_kernel, [((rows, 4 * HD), BF16), ((rows, HD), BF16)], [], ids, partial, swap(partial, "yl"))
    heads, row_sum = call(
        attend_kernel, [((rows, 6 * HD), BF16), ((1, rows), F32)], [], ids, qa, kv, swap(kv, "c")
    )
    row_sum = row_sum + swap(row_sum, "c")
    heads = [heads] + [shift_x(heads, s) for s in range(1, NX)]

    g, n = GROWS, BLOCK
    t0, up, down, t2, m2, t4a, t4b, *back = call(
        gradient_kernel,
        [
            ((g + 2 * n, HD), BF16),
            ((g + 4 * n, HD), BF16),
            ((g + 4 * n, HD), BF16),
            ((2 * n, HD), BF16),
            ((2 * n, HD), BF16),
            ((g + n, HD), BF16),
            ((g + n, HD), BF16),
        ]
        + [((rows + GROWS, sub), BF16)] * 4,
        [((512, 6 * HD), BF16), ((512, 4 * HD), BF16), ((sub, 2 * HD), F32)],
        ids,
        *heads,
        *[swap(h, "c") for h in heads],
        normed_sw,
        cot_sw,
        unit_sw,
        w_all,
    )
    c4, d4 = shift_z(t4a, 2), shift_z(t4b, -2)
    a, b = shift_z(up, 1), shift_z(down, -1)
    up, down, *back = call(
        relay_kernel,
        [((2 * n, HD), BF16)] * 2 + [((rows + g, sub), BF16)] * 4,
        [],
        ids,
        t2,
        m2,
        a,
        b,
        c4,
        d4,
        t0,
        *back,
        aliases={8 + s: 2 + s for s in range(NX)},
    )
    up, down = shift_z(up, 2), shift_z(down, -2)

    pieces = [back[0]] + [shift_x(back[s], -s) for s in range(1, NX)]
    to_same, to_other = call(finish_kernel, [((n, HD), BF16)] * 2, [], ids, t0, a, b, up, down)
    arrived = (lax.ppermute(to_same, AXES, inverse(owner_perm(0))), lax.ppermute(to_other, AXES, inverse(owner_perm(1))))
    gain_five, gain_three = call(gain_kernel, [((4 * NX, HD), F32)] * 2, [], ids, *pieces)
    gain_z = gain_five + shift_z(gain_three, 4)
    *arrived, gain_z = lax.optimization_barrier((*arrived, gain_z))
    gain_z = gain_z + swap(gain_z, "yh")
    (shared_own,) = call(shared_kernel, [((2 * PIECE, HD), BF16)], [], ids, *arrived)
    grad_input, grad_query, grad_out = call(
        input_kernel,
        [((rows, quarter), F32)] + [((HD, HD), F32)] * 2,
        [],
        ids,
        *pieces,
        tokens,
        gain_f,
        total,
        row_sum,
        *arrived,
        static=(width, loss_scale),
    )
    shared_yl = swap(shared_own, "yl")
    grad_key, grad_value, grad_gain = call(
        join_kernel,
        [((rows, HD), F32)] * 2 + [((4 * NX, 1, HD), F32)],
        [],
        ids,
        shared_own,
        swap(shared_own, "c"),
        shared_yl,
        swap(shared_yl, "c"),
        gain_z,
        static=loss_scale,
    )
    grad_gain = grad_gain.reshape(quarter)
    return (grad_input, grad_gain, grad_query, grad_key, grad_value, grad_out)


def solution(mesh):
    fine = Mesh(mesh.devices.reshape(2, NX, NZ, 2, 2), AXES)
    in_specs = (P(FSDP, TP), P(TP), P(FSDP, TP), P(FSDP, None), P(FSDP, None), P(TP, FSDP), P(FSDP, TP))
    out_specs = (P(FSDP, TP), P(TP), P(FSDP, TP), P(FSDP, None), P(FSDP, None), P(TP, FSDP))
    return jax.shard_map(local, mesh=fine, in_specs=in_specs, out_specs=out_specs, check_vma=False)
```

```python
import functools
import math

import jax
import jax.numpy as jnp
from jax import lax
from jax.experimental import pallas as pl
from jax.experimental.pallas import tpu as pltpu
from jax.sharding import Mesh, PartitionSpec as P

HD = 128
NX = 4
NZ = 8
AXES = ("yh", "x", "z", "yl", "c")
FSDP = ("yh", "x", "z")
TP = ("yl", "c")
F32 = jnp.float32
BF16 = jnp.bfloat16
PIECE = 32
BLOCK = 2 * HD + 2 * PIECE
GROWS = 16
VMEM = pl.BlockSpec(memory_space=pltpu.VMEM)
SMEM = pl.BlockSpec(memory_space=pltpu.SMEM)


def flat(yh, x, z, yl, c):
    return (((yh * NX + x) * NZ + z) * 2 + yl) * 2 + c


def owner_perm(flip):
    pairs = []
    for yh in range(2):
        for x in range(NX):
            for z in range(NZ):
                for yl in range(2):
                    for c in range(2):
                        dest_x = (x % 2) * 2 + z % 2
                        dest_z = (z // 2) * 2 + c
                        pairs.append((flat(yh, x, z, yl, c), flat(yl ^ flip, dest_x, dest_z, yh, x // 2)))
    return pairs


def inverse(pairs):
    return [(d, s) for s, d in pairs]


def shift_x(value, by):
    return lax.ppermute(value, "x", [(i, (i + by) % NX) for i in range(NX)])


def shift_z(value, by):
    return lax.ppermute(value, "z", [(i, (i + by) % NZ) for i in range(NZ)])


def swap(value, axis):
    return lax.ppermute(value, axis, [(0, 1), (1, 0)])


def dot(a, b, ca, cb):
    return lax.dot_general(a, b, (((ca,), (cb,)), ((), ())), preferred_element_type=F32)


def lanes(start, size=HD):
    return pl.ds(pl.multiple_of(start, HD), size)


def feature(at, j):
    return ((at // 2) * 8 + 2 * j + at % 2) * HD


def call(body, outs, scratch, ids, *args, static=None, aliases={}):
    body = body if static is None else functools.partial(body, static)
    return pl.pallas_call(
        body,
        out_shape=[jax.ShapeDtypeStruct(s, d) for s, d in outs],
        in_specs=[SMEM] + [VMEM] * len(args),
        out_specs=[VMEM] * len(outs),
        input_output_aliases=aliases,
        scratch_shapes=[pltpu.VMEM(s, d) for s, d in scratch],
        compiler_params=pltpu.CompilerParams(vmem_limit_bytes=16 * 2**20),
    )(ids, *args)


def spread_kernel(ids, tokens, cot, total_out, *outs):
    rows = tokens.shape[0]
    squares = jnp.zeros((rows, HD), F32)
    for s in range(NX):
        at = (ids[4] + s) % NX
        for j in range(4):
            block, cols = lanes(feature(at, j)), slice(j * HD, (j + 1) * HD)
            value = tokens[:, block]
            squares = squares + value.astype(F32) * value.astype(F32)
            outs[s][:rows, cols] = value
            outs[s][rows : 2 * rows, cols] = cot[:, block]
    total_out[...] = jnp.sum(jnp.transpose(squares), axis=0, keepdims=True)


def stamp_kernel(ids, total, *refs):
    total = total[...]
    high = total.astype(BF16).astype(F32)
    middle = (total - high).astype(BF16).astype(F32)
    extra = jnp.concatenate([high, middle, total - high - middle, jnp.zeros((GROWS - 3, HD), F32)], axis=0)
    extra = jnp.concatenate([extra] * 4, axis=1).astype(BF16)
    for out in refs[NX:]:
        out[2 * HD :] = extra


def normalize_kernel(width, ids, *refs):
    parts, (gain, unit, normed, cot) = refs[:4], refs[4:]
    for s in range(NX):
        rows = slice(s * HD, (s + 1) * HD)
        terms = parts[s][2 * HD :, :HD].astype(F32)
        total = (terms[2:3] + terms[1:2]) + terms[0:1]
        column = jnp.transpose(jnp.broadcast_to(total, (HD, HD)))
        inv = lax.rsqrt(column / width + 1e-05)
        for j in range(4):
            cols = slice(j * HD, (j + 1) * HD)
            value = parts[s][:HD, cols].astype(F32) * inv
            unit[rows, cols] = value
            normed[rows, cols] = (value * gain[:, lanes(feature(ids[4], j))]).astype(BF16)
        cot[rows] = parts[s][HD : 2 * HD]


def forward_pack_kernel(ids, both, prev, after, up, down, far_first, far_second):
    for out, ref in ((up, prev), (down, after)):
        out[: 2 * BLOCK] = both[...]
        out[2 * BLOCK :] = ref[...]
    far_first[...] = prev[:BLOCK]
    far_second[...] = after[BLOCK:]


def product(outs, side, normed, cot, w_all, w_out):
    w_q = w_all[:, lanes(side * 2 * HD, 2 * HD)]
    w_kv = w_all[:, lanes((4 + side) * HD)]
    w_o = w_out[side]
    for r in range(0, 512, 256):
        rows = slice(r, r + 256)
        query = dot(normed[rows], w_q, 1, 0)
        attn_grad = dot(cot[rows], w_o, 1, 1)
        shared = dot(normed[rows], w_kv, 1, 0)
        for half in range(2):
            out, part = outs[r // HD + half], slice(half * HD, (half + 1) * HD)
            out[:, : 2 * HD] = query[part]
            out[:, 2 * HD : 4 * HD] = attn_grad[part]
            out[:, 4 * HD :] = shared[part]


def theirs_kernel(ids, both, prev1, next1, prev2, next2, far_first, far_second, normed, cot, *refs):
    outs, w_all, w_out = refs[:NX], refs[NX], refs[NX + 1]
    z, c = ids[0], ids[2]

    def place(ref, base, d, half):
        zt = (z + d + NZ) % NZ
        side, j = zt % 2, zt // 2
        rows = pl.ds(pl.multiple_of(j * HD, HD), HD)
        w_all[rows, lanes(side * 2 * HD + half * HD)] = ref[base : base + HD]
        w_out[side, half * HD : (half + 1) * HD, lanes(j * HD)] = ref[base + HD : base + 2 * HD]
        part = pl.ds(pl.multiple_of(j * HD + (2 * half + side) * PIECE, PIECE), PIECE)
        w_all[part, 4 * HD : 5 * HD] = ref[base + 2 * HD : base + 2 * HD + PIECE]
        w_all[part, 5 * HD : 6 * HD] = ref[base + 2 * HD + PIECE : base + BLOCK]

    for ref, base, d in (
        (both, 0, 0),
        (prev1, 0, -1),
        (prev1, 2 * BLOCK, -3),
        (next1, 0, 1),
        (next1, 2 * BLOCK, 3),
        (prev2, 0, -2),
        (next2, 0, 2),
    ):
        place(ref, base, d, 0)
        place(ref, base + BLOCK, d, 1)
    place(far_first, 0, 4, 0)
    place(far_second, 0, 4, 1)
    product(outs, 1 - c, normed, cot, w_all, w_out)


def mine_kernel(ids, normed, cot, w_all, w_out, *refs):
    outs, normed_t = refs[:NX], refs[NX]
    product(outs, ids[2], normed, cot, w_all, w_out)
    for s in range(NX):
        for j in range(4):
            rows, cols = slice(s * HD, (s + 1) * HD), slice(j * HD, (j + 1) * HD)
            normed_t[cols, rows] = jnp.transpose(normed[rows, cols])


def split_store(ref, total):
    for start, size, at in ((0, 2 * HD, 0), (4 * HD, HD, 6 * HD)):
        value = total[:, start : start + size]
        high = value.astype(BF16)
        ref[:, at : at + size] = high
        ref[:, at + size : at + 2 * size] = (value - high.astype(F32)).astype(BF16)
    ref[:, 4 * HD : 6 * HD] = total[:, 2 * HD : 4 * HD].astype(BF16)


def joined(ref):
    value = ref[...].astype(F32)
    return jnp.concatenate(
        [
            value[:, : 2 * HD] + value[:, 2 * HD : 4 * HD],
            value[:, 4 * HD : 6 * HD],
            value[:, 6 * HD : 7 * HD] + value[:, 7 * HD :],
        ],
        axis=1,
    )


def chunk_kernel(ids, mine, got, out):
    split_store(out, mine[...] + got[...])


def own_kernel(ids, mine, got, out):
    out[...] = mine[...] + got[...]


def sum_kernel(ids, own, a, b, c, out):
    split_store(out, own[...] + joined(a) + joined(b) + joined(c))


def final_kernel(ids, mine, got, qa, kv):
    total = (joined(mine) + joined(got)).astype(BF16)
    qa[...] = total[:, : 4 * HD]
    kv[...] = total[:, 4 * HD :]


def attend_kernel(ids, qa, kv_mine, kv_theirs, out, row_out):
    first = ids[2] == 0
    mine, theirs = kv_mine[...].astype(F32), kv_theirs[...].astype(F32)
    key_rows = jnp.where(first, mine, theirs).astype(BF16)
    value_rows = jnp.where(first, theirs, mine).astype(BF16)
    causal = lax.broadcasted_iota(jnp.int32, (HD, HD), 0) >= lax.broadcasted_iota(jnp.int32, (HD, HD), 1)
    keys = jnp.zeros((HD, HD), F32)
    values = jnp.zeros((HD, HD), F32)
    row_terms = jnp.zeros((HD, HD), F32)
    for h in range(2):
        query = qa[:, h * HD : (h + 1) * HD]
        attn_grad = qa[:, (2 + h) * HD : (3 + h) * HD]
        scores = dot(query, key_rows, 1, 1) * HD ** (-0.5)
        scores = jnp.where(causal, scores, jnp.float32(-1e30))
        shifted = jnp.exp(scores - jnp.max(scores, axis=-1, keepdims=True))
        softmax_out = shifted / jnp.sum(shifted, axis=-1, keepdims=True)
        rounded = softmax_out.astype(BF16)
        dprob = dot(attn_grad, value_rows, 1, 1)
        dscore = softmax_out * (dprob - jnp.sum(dprob * softmax_out, axis=-1, keepdims=True)) * HD ** (-0.5)
        dscore = dscore.astype(BF16)
        d_query = dot(dscore, key_rows, 1, 0).astype(BF16)
        out[:, h * HD : (h + 1) * HD] = d_query
        row_terms = row_terms + d_query.astype(F32) * query.astype(F32)
        out[:, (2 + h) * HD : (3 + h) * HD] = dot(rounded, value_rows, 1, 0).astype(BF16)
        keys = keys + dot(dscore, query, 0, 0).astype(BF16).astype(F32)
        values = values + dot(rounded, attn_grad, 0, 0).astype(BF16).astype(F32)
    out[:, 4 * HD : 5 * HD] = keys.astype(BF16)
    out[:, 5 * HD :] = values.astype(BF16)
    row_terms = row_terms + keys * key_rows.astype(F32) + values * value_rows.astype(F32)
    row_out[...] = jnp.sum(jnp.transpose(row_terms), axis=0, keepdims=True)


def gradient_kernel(ids, *refs):
    mine, theirs, (normed_t, cot, unit, w_all) = refs[:4], refs[4:8], refs[8:12]
    (t0, up, down, t2, m2, t4a, t4b), back = refs[12:19], refs[19:23]
    heads, attended, shared = refs[23:]
    z, c = ids[0], ids[2]
    for s in range(NX):
        rows = slice(s * HD, (s + 1) * HD)
        for ref, side in ((mine[s], c), (theirs[s], 1 - c)):
            heads[rows, lanes(side * 2 * HD, 2 * HD)] = ref[:, : 2 * HD]
            for half in range(2):
                at = pl.ds(pl.multiple_of((2 * side + half) * HD, HD), HD)
                attended[at, rows] = jnp.transpose(ref[:, (2 + half) * HD : (3 + half) * HD])
        total = mine[s][:, 4 * HD :].astype(F32) + theirs[s][:, 4 * HD :].astype(F32)
        heads[rows, 4 * HD :] = total.astype(BF16)

    gain_sum = jnp.zeros((1, 4 * HD), F32)
    for s in range(NX):
        rows = slice(s * HD, (s + 1) * HD)
        term = dot(heads[rows], w_all[...], 1, 1)
        back[s][:HD] = term.astype(BF16)
        gain_sum = gain_sum + jnp.sum(term * unit[rows], axis=0, keepdims=True)
    gain_rows = jnp.concatenate([gain_sum[:, j * HD : (j + 1) * HD] for j in range(4)], axis=0)
    high = gain_rows.astype(BF16).astype(F32)
    gain_rows = jnp.concatenate([high, gain_rows - high, jnp.zeros((8, HD), F32)], axis=0).astype(BF16)

    shared[...] = dot(normed_t[...], heads[:, 4 * HD :], 1, 0)
    g, n = GROWS, BLOCK
    for ref in (t0, up, down, t4a, t4b):
        ref[:g] = gain_rows
    for d, out_first, out_second in (
        (0, t0.at[g : g + n], t0.at[g + n :]),
        (1, up.at[g : g + n], up.at[g + n : g + 2 * n]),
        (3, up.at[g + 2 * n : g + 3 * n], up.at[g + 3 * n :]),
        (-1, down.at[g : g + n], down.at[g + n : g + 2 * n]),
        (-3, down.at[g + 2 * n : g + 3 * n], down.at[g + 3 * n :]),
        (2, t2.at[:n], t2.at[n:]),
        (-2, m2.at[:n], m2.at[n:]),
        (4, t4a.at[g:], t4b.at[g:]),
    ):
        zt = (z + d + NZ) % NZ
        side, j = zt % 2, zt // 2
        g_q = dot(normed_t[pl.ds(pl.multiple_of(j * HD, HD), HD)], heads[:, lanes(side * 2 * HD, 2 * HD)], 1, 0).astype(BF16)
        g_o = dot(attended[pl.ds(pl.multiple_of(side * 2 * HD, 2 * HD), 2 * HD)], cot[:, lanes(j * HD)], 1, 0).astype(BF16)
        for half, out in enumerate((out_first, out_second)):
            out[:HD] = g_q[:, half * HD : (half + 1) * HD]
            out[HD : 2 * HD] = g_o[half * HD : (half + 1) * HD]
            part = shared[pl.ds(pl.multiple_of(j * HD + (2 * half + side) * PIECE, PIECE), PIECE), :].astype(BF16)
            out[2 * HD : 2 * HD + PIECE] = part[:, :HD]
            out[2 * HD + PIECE :] = part[:, HD:]


def relay_kernel(ids, t2, m2, a, b, c, d, t0, *refs):
    up, down, *back = refs[NX:]
    g, n = GROWS, BLOCK
    total = t2[...].astype(F32) + a[g + 2 * n :].astype(F32)
    up[:n] = (total[:n] + c[g:].astype(F32)).astype(BF16)
    up[n:] = total[n:].astype(BF16)
    total = m2[...].astype(F32) + b[g + 2 * n :].astype(F32)
    down[:n] = total[:n].astype(BF16)
    down[n:] = (total[n:] + d[g:].astype(F32)).astype(BF16)
    three = t0[:g].astype(F32) + a[:g].astype(F32) + b[:g].astype(F32)
    five = three + c[:g].astype(F32) + d[:g].astype(F32)
    terms = []
    for rows in (five, three):
        value = rows[:4] + rows[4:8]
        high = value.astype(BF16).astype(F32)
        terms += [high, value - high]
    for j in range(4):
        rows = jnp.concatenate([t[j : j + 1] for t in terms] + [jnp.zeros((g - 4, HD), F32)], axis=0).astype(BF16)
        for ref in back:
            ref[HD:, j * HD : (j + 1) * HD] = rows


def finish_kernel(ids, t0, a, b, up, down, same, other):
    g, n = GROWS, BLOCK
    flip = ids[3]
    near = slice(g, g + 2 * n)
    total = t0[near].astype(F32) + a[near].astype(F32) + b[near].astype(F32)
    total = total + up[...].astype(F32) + down[...].astype(F32)
    same[...] = jnp.where(flip == 0, total[:n], total[n:]).astype(BF16)
    other[...] = jnp.where(flip == 0, total[n:], total[:n]).astype(BF16)


def gain_kernel(ids, *refs):
    five, three = refs[NX:]
    for s in range(NX):
        rows = refs[s][HD:].astype(F32)
        for out, at in ((five, 0), (three, 2)):
            value = rows[at : at + 1] + rows[at + 1 : at + 2]
            for j in range(4):
                out[4 * s + j : 4 * s + j + 1] = value[:, j * HD : (j + 1) * HD]


def input_kernel(width, ids, a, b, c, d, tokens, gain, total, row_sum, out):
    inv = lax.rsqrt(jnp.transpose(jnp.broadcast_to(total[...], (HD, HD))) / width + 1e-05)
    row_mean = jnp.transpose(jnp.broadcast_to(row_sum[...], (HD, HD))) / width
    for s, ref in enumerate((a, b, c, d)):
        at = (ids[4] + s) % NX
        for j in range(4):
            cols = lanes(feature(at, j))
            unit = tokens[:, cols].astype(F32) * inv
            scaled = ref[:HD, j * HD : (j + 1) * HD].astype(F32) * gain[:, cols]
            out[:, cols] = inv * (scaled - unit * row_mean)


def owner_kernel(scale, ids, same, other, grad_query, grad_out):
    for grad, at in ((grad_query, slice(0, HD)), (grad_out, slice(HD, 2 * HD))):
        grad[...] = (same[at].astype(F32) + other[at].astype(F32)) * scale


def shared_kernel(ids, a, b, shared):
    shared[...] = (a[2 * HD :].astype(F32) + b[2 * HD :].astype(F32)).astype(BF16)


def join_kernel(scale, ids, own, by_c, by_yl, by_both, gains, grad_key, grad_value, grad_gain):
    yl, c, x = ids[1], ids[2], ids[4]
    for ref, at in ((own, 2 * yl + c), (by_c, 2 * yl + 1 - c), (by_yl, 2 - 2 * yl + c), (by_both, 3 - 2 * yl - c)):
        rows = pl.ds(pl.multiple_of(at * PIECE, PIECE), PIECE)
        grad_key[rows] = ref[:PIECE].astype(F32) * scale
        grad_value[rows] = ref[PIECE:].astype(F32) * scale
    for s in range(NX):
        at = (x + s) % NX
        for j in range(4):
            grad_gain[(at // 2) * 8 + 2 * j + at % 2] = gains[4 * s + j : 4 * s + j + 1] * scale


def local(tokens, gain, w_query, w_key, w_value, w_out, cotangent):
    rows, quarter = tokens.shape
    sub = quarter // NX
    width = quarter * 4
    yh, x, z, yl, c = (lax.axis_index(a) for a in AXES)
    ids = jnp.stack([z, yl, c, yh, x]).astype(jnp.int32)
    head = yl * 2 + c
    loss_scale = 1.0 / math.sqrt(rows * 64)

    pack = jnp.concatenate(
        [
            w_query,
            w_out,
            lax.dynamic_slice_in_dim(w_key, head * PIECE, PIECE, 0),
            lax.dynamic_slice_in_dim(w_value, head * PIECE, PIECE, 0),
        ],
        axis=0,
    )
    same = lax.ppermute(pack, AXES, owner_perm(0))
    other = lax.ppermute(pack, AXES, owner_perm(1))
    part_shape = ((2 * rows + GROWS, sub), BF16)
    total, *parts = call(spread_kernel, [((1, rows), F32)] + [part_shape] * 4, [], ids, tokens, cotangent)
    total = total + swap(total, "c")
    same, other, total = lax.optimization_barrier((same, other, total))
    total = total + swap(total, "yl")
    both = jnp.where(yh == 0, jnp.concatenate([same, other]), jnp.concatenate([other, same]))
    prev2, next2 = shift_z(both, 2), shift_z(both, -2)
    double, half_shape = ((4 * BLOCK, HD), BF16), ((BLOCK, HD), BF16)
    relays = call(forward_pack_kernel, [double] * 2 + [half_shape] * 2, [], ids, both, prev2, next2)
    prev1, next1 = shift_z(relays[0], 1), shift_z(relays[1], -1)
    far_first, far_second = shift_z(relays[2], 2), shift_z(relays[3], -2)
    weights = (both, prev1, next1, prev2, next2, far_first, far_second)

    parts = call(stamp_kernel, [part_shape] * 4, [], ids, total, *parts, aliases={2 + s: s for s in range(4)})
    parts = [parts[0]] + [shift_x(parts[s], s) for s in range(1, NX)]
    gain_f = gain.astype(F32).reshape(1, quarter)
    unit_sw, normed_sw, cot_sw = call(
        normalize_kernel,
        [((512, sub), F32), ((512, sub), BF16), ((512, sub), BF16)],
        [],
        ids,
        *parts,
        gain_f,
        static=width,
    )

    *theirs, w_all, w_heads = call(
        theirs_kernel,
        [((rows, 5 * HD), F32)] * 4 + [((sub, 6 * HD), BF16), ((2, 2 * HD, sub), BF16)],
        [],
        ids,
        *weights,
        normed_sw,
        cot_sw,
    )
    got = [None] + [swap(theirs[s], "c") for s in range(1, NX)]
    got[0] = swap(theirs[0], "c")
    *mine, normed_t = call(
        mine_kernel,
        [((rows, 5 * HD), F32)] * 4 + [((sub, 512), BF16)],
        [],
        ids,
        normed_sw,
        cot_sw,
        w_all,
        w_heads,
    )
    split = ((rows, 8 * HD), BF16)
    chunks = [shift_x(call(chunk_kernel, [split], [], ids, mine[s], got[s])[0], -s) for s in range(1, NX)]
    (own,) = call(own_kernel, [((rows, 5 * HD), F32)], [], ids, mine[0], got[0])
    (partial,) = call(sum_kernel, [split], [], ids, own, *chunks)
    qa, kv = call(final_kernel, [((rows, 4 * HD), BF16), ((rows, HD), BF16)], [], ids, partial, swap(partial, "yl"))
    heads, row_sum = call(
        attend_kernel, [((rows, 6 * HD), BF16), ((1, rows), F32)], [], ids, qa, kv, swap(kv, "c")
    )
    row_sum = row_sum + swap(row_sum, "c")
    heads = [heads] + [shift_x(heads, s) for s in range(1, NX)]

    g, n = GROWS, BLOCK
    t0, up, down, t2, m2, t4a, t4b, *back = call(
        gradient_kernel,
        [
            ((g + 2 * n, HD), BF16),
            ((g + 4 * n, HD), BF16),
            ((g + 4 * n, HD), BF16),
            ((2 * n, HD), BF16),
            ((2 * n, HD), BF16),
            ((g + n, HD), BF16),
            ((g + n, HD), BF16),
        ]
        + [((rows + GROWS, sub), BF16)] * 4,
        [((512, 6 * HD), BF16), ((512, 4 * HD), BF16), ((sub, 2 * HD), F32)],
        ids,
        *heads,
        *[swap(h, "c") for h in heads],
        normed_t,
        cot_sw,
        unit_sw,
        w_all,
    )
    c4, d4 = shift_z(t4a, 2), shift_z(t4b, -2)
    a, b = shift_z(up, 1), shift_z(down, -1)
    a, row_sum = lax.optimization_barrier((a, row_sum))
    up, down, *back = call(
        relay_kernel,
        [((2 * n, HD), BF16)] * 2 + [((rows + g, sub), BF16)] * 4,
        [],
        ids,
        t2,
        m2,
        a,
        b,
        c4,
        d4,
        t0,
        *back,
        aliases={8 + s: 2 + s for s in range(NX)},
    )
    up, down = shift_z(up, 2), shift_z(down, -2)

    pieces = [back[0]] + [shift_x(back[s], -s) for s in range(1, NX)]
    to_same, to_other = call(finish_kernel, [((n, HD), BF16)] * 2, [], ids, t0, a, b, up, down)
    arrived = (lax.ppermute(to_same, AXES, inverse(owner_perm(0))), lax.ppermute(to_other, AXES, inverse(owner_perm(1))))
    gain_five, gain_three = call(gain_kernel, [((4 * NX, HD), F32)] * 2, [], ids, *pieces)
    gain_z = gain_five + shift_z(gain_three, 4)
    (grad_input,) = call(
        input_kernel,
        [((rows, quarter), F32)],
        [],
        ids,
        *pieces,
        tokens,
        gain_f,
        total,
        row_sum,
        static=width,
    )
    *arrived, grad_input, gain_z = lax.optimization_barrier((*arrived, grad_input, gain_z))
    (shared_own,) = call(shared_kernel, [((2 * PIECE, HD), BF16)], [], ids, *arrived)
    grad_query, grad_out = call(owner_kernel, [((HD, HD), F32)] * 2, [], ids, *arrived, static=loss_scale)
    shared_yl = swap(shared_own, "yl")
    gain_z = gain_z + swap(gain_z, "yh")
    grad_key, grad_value, grad_gain = call(
        join_kernel,
        [((rows, HD), F32)] * 2 + [((4 * NX, 1, HD), F32)],
        [],
        ids,
        shared_own,
        swap(shared_own, "c"),
        shared_yl,
        swap(shared_yl, "c"),
        gain_z,
        static=loss_scale,
    )
    grad_gain = grad_gain.reshape(quarter)
    return (grad_input, grad_gain, grad_query, grad_key, grad_value, grad_out)


def solution(mesh):
    fine = Mesh(mesh.devices.reshape(2, NX, NZ, 2, 2), AXES)
    in_specs = (P(FSDP, TP), P(TP), P(FSDP, TP), P(FSDP, None), P(FSDP, None), P(TP, FSDP), P(FSDP, TP))
    out_specs = (P(FSDP, TP), P(TP), P(FSDP, TP), P(FSDP, None), P(FSDP, None), P(TP, FSDP))
    return jax.shard_map(local, mesh=fine, in_specs=in_specs, out_specs=out_specs, check_vma=False)
```

```python
import functools
import math

import jax
import jax.numpy as jnp
from jax import lax
from jax.experimental import pallas as pl
from jax.experimental.pallas import tpu as pltpu
from jax.sharding import Mesh, PartitionSpec as P

HD = 128
NX = 4
NZ = 8
AXES = ("yh", "x", "z", "yl", "c")
FSDP = ("yh", "x", "z")
TP = ("yl", "c")
F32 = jnp.float32
BF16 = jnp.bfloat16
PIECE = 32
BLOCK = 2 * HD + 2 * PIECE
GROWS = 16
VMEM = pl.BlockSpec(memory_space=pltpu.VMEM)
SMEM = pl.BlockSpec(memory_space=pltpu.SMEM)


def flat(yh, x, z, yl, c):
    return (((yh * NX + x) * NZ + z) * 2 + yl) * 2 + c


def owner_perm(flip):
    pairs = []
    for yh in range(2):
        for x in range(NX):
            for z in range(NZ):
                for yl in range(2):
                    for c in range(2):
                        dest_x = (x % 2) * 2 + z % 2
                        dest_z = (z // 2) * 2 + c
                        pairs.append((flat(yh, x, z, yl, c), flat(yl ^ flip, dest_x, dest_z, yh, x // 2)))
    return pairs


def inverse(pairs):
    return [(d, s) for s, d in pairs]


def shift_x(value, by):
    return lax.ppermute(value, "x", [(i, (i + by) % NX) for i in range(NX)])


def shift_z(value, by):
    return lax.ppermute(value, "z", [(i, (i + by) % NZ) for i in range(NZ)])


def swap(value, axis):
    return lax.ppermute(value, axis, [(0, 1), (1, 0)])


def dot(a, b, ca, cb):
    return lax.dot_general(a, b, (((ca,), (cb,)), ((), ())), preferred_element_type=F32)


def lanes(start, size=HD):
    return pl.ds(pl.multiple_of(start, HD), size)


def feature(at, j):
    return ((at // 2) * 8 + 2 * j + at % 2) * HD


def call(body, outs, scratch, ids, *args, static=None, aliases={}):
    body = body if static is None else functools.partial(body, static)
    return pl.pallas_call(
        body,
        out_shape=[jax.ShapeDtypeStruct(s, d) for s, d in outs],
        in_specs=[SMEM] + [VMEM] * len(args),
        out_specs=[VMEM] * len(outs),
        input_output_aliases=aliases,
        scratch_shapes=[pltpu.VMEM(s, d) for s, d in scratch],
        compiler_params=pltpu.CompilerParams(vmem_limit_bytes=16 * 2**20),
    )(ids, *args)


def spread_kernel(ids, tokens, cot, total_out, *outs):
    rows = tokens.shape[0]
    squares = jnp.zeros((rows, HD), F32)
    for s in range(NX):
        at = (ids[4] + s) % NX
        for j in range(4):
            block, cols = lanes(feature(at, j)), slice(j * HD, (j + 1) * HD)
            value = tokens[:, block]
            squares = squares + value.astype(F32) * value.astype(F32)
            outs[s][:rows, cols] = value
            outs[s][rows : 2 * rows, cols] = cot[:, block]
    total_out[...] = jnp.sum(jnp.transpose(squares), axis=0, keepdims=True)


def stamp_kernel(ids, total, *refs):
    total = total[...]
    high = total.astype(BF16).astype(F32)
    middle = (total - high).astype(BF16).astype(F32)
    extra = jnp.concatenate([high, middle, total - high - middle, jnp.zeros((GROWS - 3, HD), F32)], axis=0)
    extra = jnp.concatenate([extra] * 4, axis=1).astype(BF16)
    for out in refs[NX:]:
        out[2 * HD :] = extra


def normalize_kernel(width, ids, *refs):
    parts, (gain, unit, normed, cot) = refs[:4], refs[4:]
    for s in range(NX):
        rows = slice(s * HD, (s + 1) * HD)
        terms = parts[s][2 * HD :, :HD].astype(F32)
        total = (terms[2:3] + terms[1:2]) + terms[0:1]
        column = jnp.transpose(jnp.broadcast_to(total, (HD, HD)))
        inv = lax.rsqrt(column / width + 1e-05)
        for j in range(4):
            cols = slice(j * HD, (j + 1) * HD)
            value = parts[s][:HD, cols].astype(F32) * inv
            unit[rows, cols] = value
            normed[rows, cols] = (value * gain[:, lanes(feature(ids[4], j))]).astype(BF16)
        cot[rows] = parts[s][HD : 2 * HD]


def forward_pack_kernel(ids, both, prev, after, up, down, far_first, far_second):
    for out, ref in ((up, prev), (down, after)):
        out[: 2 * BLOCK] = both[...]
        out[2 * BLOCK :] = ref[...]
    far_first[...] = prev[:BLOCK]
    far_second[...] = after[BLOCK:]


def product(outs, side, normed, cot, w_all, w_out):
    w_q = w_all[:, lanes(side * 2 * HD, 2 * HD)]
    w_kv = w_all[:, lanes((4 + side) * HD)]
    w_o = w_out[side]
    for r in range(0, 512, 256):
        rows = slice(r, r + 256)
        query = dot(normed[rows], w_q, 1, 0)
        attn_grad = dot(cot[rows], w_o, 1, 1)
        shared = dot(normed[rows], w_kv, 1, 0)
        for half in range(2):
            out, part = outs[r // HD + half], slice(half * HD, (half + 1) * HD)
            out[:, : 2 * HD] = query[part]
            out[:, 2 * HD : 4 * HD] = attn_grad[part]
            out[:, 4 * HD :] = shared[part]


def theirs_kernel(ids, both, prev1, next1, prev2, next2, far_first, far_second, normed, cot, *refs):
    outs, w_all, w_out = refs[:NX], refs[NX], refs[NX + 1]
    z, c = ids[0], ids[2]

    def place(ref, base, d, half):
        zt = (z + d + NZ) % NZ
        side, j = zt % 2, zt // 2
        rows = pl.ds(pl.multiple_of(j * HD, HD), HD)
        w_all[rows, lanes(side * 2 * HD + half * HD)] = ref[base : base + HD]
        w_out[side, half * HD : (half + 1) * HD, lanes(j * HD)] = ref[base + HD : base + 2 * HD]
        part = pl.ds(pl.multiple_of(j * HD + (2 * half + side) * PIECE, PIECE), PIECE)
        w_all[part, 4 * HD : 5 * HD] = ref[base + 2 * HD : base + 2 * HD + PIECE]
        w_all[part, 5 * HD : 6 * HD] = ref[base + 2 * HD + PIECE : base + BLOCK]

    for ref, base, d in (
        (both, 0, 0),
        (prev1, 0, -1),
        (prev1, 2 * BLOCK, -3),
        (next1, 0, 1),
        (next1, 2 * BLOCK, 3),
        (prev2, 0, -2),
        (next2, 0, 2),
    ):
        place(ref, base, d, 0)
        place(ref, base + BLOCK, d, 1)
    place(far_first, 0, 4, 0)
    place(far_second, 0, 4, 1)
    product(outs, 1 - c, normed, cot, w_all, w_out)


def mine_kernel(ids, normed, cot, w_all, w_out, *refs):
    outs, normed_t = refs[:NX], refs[NX]
    product(outs, ids[2], normed, cot, w_all, w_out)
    for s in range(NX):
        for j in range(4):
            rows, cols = slice(s * HD, (s + 1) * HD), slice(j * HD, (j + 1) * HD)
            normed_t[cols, rows] = jnp.transpose(normed[rows, cols])


def split_store(ref, total):
    for start, size, at in ((0, 2 * HD, 0), (4 * HD, HD, 6 * HD)):
        value = total[:, start : start + size]
        high = value.astype(BF16)
        ref[:, at : at + size] = high
        ref[:, at + size : at + 2 * size] = (value - high.astype(F32)).astype(BF16)
    ref[:, 4 * HD : 6 * HD] = total[:, 2 * HD : 4 * HD].astype(BF16)


def joined(ref):
    value = ref[...].astype(F32)
    return jnp.concatenate(
        [
            value[:, : 2 * HD] + value[:, 2 * HD : 4 * HD],
            value[:, 4 * HD : 6 * HD],
            value[:, 6 * HD : 7 * HD] + value[:, 7 * HD :],
        ],
        axis=1,
    )


def chunk_kernel(ids, mine, got, out):
    split_store(out, mine[...] + got[...])


def own_kernel(ids, mine, got, out):
    out[...] = mine[...] + got[...]


def sum_kernel(ids, own, a, b, c, out):
    split_store(out, own[...] + joined(a) + joined(b) + joined(c))


def final_kernel(ids, mine, got, qa, kv):
    total = (joined(mine) + joined(got)).astype(BF16)
    qa[...] = total[:, : 4 * HD]
    kv[...] = total[:, 4 * HD :]


def attend_kernel(ids, qa, kv_mine, kv_theirs, out, row_out):
    first = ids[2] == 0
    mine, theirs = kv_mine[...].astype(F32), kv_theirs[...].astype(F32)
    key_rows = jnp.where(first, mine, theirs).astype(BF16)
    value_rows = jnp.where(first, theirs, mine).astype(BF16)
    causal = lax.broadcasted_iota(jnp.int32, (HD, HD), 0) >= lax.broadcasted_iota(jnp.int32, (HD, HD), 1)
    keys = jnp.zeros((HD, HD), F32)
    values = jnp.zeros((HD, HD), F32)
    row_terms = jnp.zeros((HD, HD), F32)
    for h in range(2):
        query = qa[:, h * HD : (h + 1) * HD]
        attn_grad = qa[:, (2 + h) * HD : (3 + h) * HD]
        scores = dot(query, key_rows, 1, 1) * HD ** (-0.5)
        scores = jnp.where(causal, scores, jnp.float32(-1e30))
        shifted = jnp.exp(scores - jnp.max(scores, axis=-1, keepdims=True))
        softmax_out = shifted / jnp.sum(shifted, axis=-1, keepdims=True)
        rounded = softmax_out.astype(BF16)
        dprob = dot(attn_grad, value_rows, 1, 1)
        dscore = softmax_out * (dprob - jnp.sum(dprob * softmax_out, axis=-1, keepdims=True)) * HD ** (-0.5)
        dscore = dscore.astype(BF16)
        d_query = dot(dscore, key_rows, 1, 0).astype(BF16)
        out[:, h * HD : (h + 1) * HD] = d_query
        row_terms = row_terms + d_query.astype(F32) * query.astype(F32)
        out[:, (2 + h) * HD : (3 + h) * HD] = dot(rounded, value_rows, 1, 0).astype(BF16)
        keys = keys + dot(dscore, query, 0, 0).astype(BF16).astype(F32)
        values = values + dot(rounded, attn_grad, 0, 0).astype(BF16).astype(F32)
    out[:, 4 * HD : 5 * HD] = keys.astype(BF16)
    out[:, 5 * HD :] = values.astype(BF16)
    row_terms = row_terms + keys * key_rows.astype(F32) + values * value_rows.astype(F32)
    row_out[...] = jnp.sum(jnp.transpose(row_terms), axis=0, keepdims=True)


def gradient_kernel(ids, *refs):
    mine, theirs, (normed_t, cot, unit, w_all) = refs[:4], refs[4:8], refs[8:12]
    (up, down, t4a, t4b), back, (gain_out, heads, attended, shared) = refs[12:16], refs[16:20], refs[20:]
    c = ids[2]
    for s in range(NX):
        rows = slice(s * HD, (s + 1) * HD)
        for ref, side in ((mine[s], c), (theirs[s], 1 - c)):
            heads[rows, lanes(side * 2 * HD, 2 * HD)] = ref[:, : 2 * HD]
            for half in range(2):
                at = pl.ds(pl.multiple_of((2 * side + half) * HD, HD), HD)
                attended[at, rows] = jnp.transpose(ref[:, (2 + half) * HD : (3 + half) * HD])
        total = mine[s][:, 4 * HD :].astype(F32) + theirs[s][:, 4 * HD :].astype(F32)
        heads[rows, 4 * HD :] = total.astype(BF16)

    gain_sum = jnp.zeros((1, 4 * HD), F32)
    for s in range(NX):
        rows = slice(s * HD, (s + 1) * HD)
        term = dot(heads[rows], w_all[...], 1, 1)
        back[s][:HD] = term.astype(BF16)
        gain_sum = gain_sum + jnp.sum(term * unit[rows], axis=0, keepdims=True)
    gain_rows = jnp.concatenate([gain_sum[:, j * HD : (j + 1) * HD] for j in range(4)], axis=0)
    high = gain_rows.astype(BF16).astype(F32)
    gain_rows = jnp.concatenate([high, gain_rows - high, jnp.zeros((8, HD), F32)], axis=0).astype(BF16)

    shared[...] = dot(normed_t[...], heads[:, 4 * HD :], 1, 0)
    g, n = GROWS, BLOCK
    for ref in (up, down, t4a, t4b):
        ref[:g] = gain_rows
    terms(
        ids,
        normed_t,
        cot,
        heads,
        attended,
        shared,
        (
            (1, up.at[g : g + n], up.at[g + n : g + 2 * n]),
            (3, up.at[g + 2 * n : g + 3 * n], up.at[g + 3 * n :]),
            (-1, down.at[g : g + n], down.at[g + n : g + 2 * n]),
            (-3, down.at[g + 2 * n : g + 3 * n], down.at[g + 3 * n :]),
            (4, t4a.at[g:], t4b.at[g:]),
        ),
    )
    gain_out[...] = gain_rows


def terms(ids, normed_t, cot, heads, attended, shared, places):
    z = ids[0]
    for d, out_first, out_second in places:
        zt = (z + d + NZ) % NZ
        side, j = zt % 2, zt // 2
        rows = pl.ds(pl.multiple_of(j * HD, HD), HD)
        g_q = dot(normed_t[rows], heads[:, lanes(side * 2 * HD, 2 * HD)], 1, 0).astype(BF16)
        rows = pl.ds(pl.multiple_of(side * 2 * HD, 2 * HD), 2 * HD)
        g_o = dot(attended[rows], cot[:, lanes(j * HD)], 1, 0).astype(BF16)
        for half, out in enumerate((out_first, out_second)):
            out[:HD] = g_q[:, half * HD : (half + 1) * HD]
            out[HD : 2 * HD] = g_o[half * HD : (half + 1) * HD]
            part = shared[pl.ds(pl.multiple_of(j * HD + (2 * half + side) * PIECE, PIECE), PIECE), :].astype(BF16)
            out[2 * HD : 2 * HD + PIECE] = part[:, :HD]
            out[2 * HD + PIECE :] = part[:, HD:]


def near_kernel(ids, normed_t, cot, heads, attended, shared, t0, t2, m2):
    n = BLOCK
    terms(ids, normed_t, cot, heads, attended, shared, [(d, r.at[:n], r.at[n:]) for d, r in ((0, t0), (2, t2), (-2, m2))])


def relay_kernel(ids, t2, m2, a, b, c, d, gain_own, *refs):
    up, down, *back = refs[NX:]
    g, n = GROWS, BLOCK
    total = t2[...].astype(F32) + a[g + 2 * n :].astype(F32)
    up[:n] = (total[:n] + c[g:].astype(F32)).astype(BF16)
    up[n:] = total[n:].astype(BF16)
    total = m2[...].astype(F32) + b[g + 2 * n :].astype(F32)
    down[:n] = total[:n].astype(BF16)
    down[n:] = (total[n:] + d[g:].astype(F32)).astype(BF16)
    three = gain_own[...].astype(F32) + a[:g].astype(F32) + b[:g].astype(F32)
    five = three + c[:g].astype(F32) + d[:g].astype(F32)
    terms = []
    for rows in (five, three):
        value = rows[:4] + rows[4:8]
        high = value.astype(BF16).astype(F32)
        terms += [high, value - high]
    for j in range(4):
        rows = jnp.concatenate([t[j : j + 1] for t in terms] + [jnp.zeros((g - 4, HD), F32)], axis=0).astype(BF16)
        for ref in back:
            ref[HD:, j * HD : (j + 1) * HD] = rows


def finish_kernel(ids, t0, a, b, up, down, same, other):
    g, n = GROWS, BLOCK
    flip = ids[3]
    near = slice(g, g + 2 * n)
    total = t0[...].astype(F32) + a[near].astype(F32) + b[near].astype(F32)
    total = total + up[...].astype(F32) + down[...].astype(F32)
    same[...] = jnp.where(flip == 0, total[:n], total[n:]).astype(BF16)
    other[...] = jnp.where(flip == 0, total[n:], total[:n]).astype(BF16)


def gain_kernel(ids, *refs):
    out = refs[NX]
    for s in range(NX):
        rows = refs[s][HD:].astype(F32)
        for at in (0, 2):
            value = rows[at : at + 1] + rows[at + 1 : at + 2]
            for j in range(4):
                row = 2 * NX * at + 4 * s + j
                out[row : row + 1] = value[:, j * HD : (j + 1) * HD]


def input_kernel(width, ids, a, b, c, d, tokens, gain, total, row_sum, out):
    inv = lax.rsqrt(jnp.transpose(jnp.broadcast_to(total[...], (HD, HD))) / width + 1e-05)
    row_mean = jnp.transpose(jnp.broadcast_to(row_sum[...], (HD, HD))) / width
    for s, ref in enumerate((a, b, c, d)):
        at = (ids[4] + s) % NX
        for j in range(4):
            cols = lanes(feature(at, j))
            unit = tokens[:, cols].astype(F32) * inv
            scaled = ref[:HD, j * HD : (j + 1) * HD].astype(F32) * gain[:, cols]
            out[:, cols] = inv * (scaled - unit * row_mean)


def owner_kernel(scale, ids, same, other, grad_query, grad_out):
    for grad, at in ((grad_query, slice(0, HD)), (grad_out, slice(HD, 2 * HD))):
        grad[...] = (same[at].astype(F32) + other[at].astype(F32)) * scale


def shared_kernel(ids, a, b, shared):
    shared[...] = (a[2 * HD :].astype(F32) + b[2 * HD :].astype(F32)).astype(BF16)


def join_kernel(scale, ids, own, by_c, by_yl, by_both, gains, grad_key, grad_value, grad_gain):
    yl, c, x = ids[1], ids[2], ids[4]
    for ref, at in ((own, 2 * yl + c), (by_c, 2 * yl + 1 - c), (by_yl, 2 - 2 * yl + c), (by_both, 3 - 2 * yl - c)):
        rows = pl.ds(pl.multiple_of(at * PIECE, PIECE), PIECE)
        grad_key[rows] = ref[:PIECE].astype(F32) * scale
        grad_value[rows] = ref[PIECE:].astype(F32) * scale
    for s in range(NX):
        at = (x + s) % NX
        for j in range(4):
            grad_gain[(at // 2) * 8 + 2 * j + at % 2] = gains[4 * s + j : 4 * s + j + 1] * scale


def local(tokens, gain, w_query, w_key, w_value, w_out, cotangent):
    rows, quarter = tokens.shape
    sub = quarter // NX
    width = quarter * 4
    yh, x, z, yl, c = (lax.axis_index(a) for a in AXES)
    ids = jnp.stack([z, yl, c, yh, x]).astype(jnp.int32)
    head = yl * 2 + c
    loss_scale = 1.0 / math.sqrt(rows * 64)

    pack = jnp.concatenate(
        [
            w_query,
            w_out,
            lax.dynamic_slice_in_dim(w_key, head * PIECE, PIECE, 0),
            lax.dynamic_slice_in_dim(w_value, head * PIECE, PIECE, 0),
        ],
        axis=0,
    )
    same = lax.ppermute(pack, AXES, owner_perm(0))
    other = lax.ppermute(pack, AXES, owner_perm(1))
    part_shape = ((2 * rows + GROWS, sub), BF16)
    total, *parts = call(spread_kernel, [((1, rows), F32)] + [part_shape] * 4, [], ids, tokens, cotangent)
    total = total + swap(total, "c")
    same, other, total = lax.optimization_barrier((same, other, total))
    total = total + swap(total, "yl")
    both = jnp.where(yh == 0, jnp.concatenate([same, other]), jnp.concatenate([other, same]))
    prev2, next2 = shift_z(both, 2), shift_z(both, -2)
    double, half_shape = ((4 * BLOCK, HD), BF16), ((BLOCK, HD), BF16)
    relays = call(forward_pack_kernel, [double] * 2 + [half_shape] * 2, [], ids, both, prev2, next2)
    prev1, next1 = shift_z(relays[0], 1), shift_z(relays[1], -1)
    far_first, far_second = shift_z(relays[2], 2), shift_z(relays[3], -2)
    weights = (both, prev1, next1, prev2, next2, far_first, far_second)

    parts = call(stamp_kernel, [part_shape] * 4, [], ids, total, *parts, aliases={2 + s: s for s in range(4)})
    parts = [parts[0]] + [shift_x(parts[s], s) for s in range(1, NX)]
    gain_f = gain.astype(F32).reshape(1, quarter)
    unit_sw, normed_sw, cot_sw = call(
        normalize_kernel,
        [((512, sub), F32), ((512, sub), BF16), ((512, sub), BF16)],
        [],
        ids,
        *parts,
        gain_f,
        static=width,
    )

    *theirs, w_all, w_heads = call(
        theirs_kernel,
        [((rows, 5 * HD), F32)] * 4 + [((sub, 6 * HD), BF16), ((2, 2 * HD, sub), BF16)],
        [],
        ids,
        *weights,
        normed_sw,
        cot_sw,
    )
    got = [None] + [swap(theirs[s], "c") for s in range(1, NX)]
    got[0] = swap(theirs[0], "c")
    *mine, normed_t = call(
        mine_kernel,
        [((rows, 5 * HD), F32)] * 4 + [((sub, 512), BF16)],
        [],
        ids,
        normed_sw,
        cot_sw,
        w_all,
        w_heads,
    )
    split = ((rows, 8 * HD), BF16)
    chunks = [shift_x(call(chunk_kernel, [split], [], ids, mine[s], got[s])[0], -s) for s in range(1, NX)]
    (own,) = call(own_kernel, [((rows, 5 * HD), F32)], [], ids, mine[0], got[0])
    (partial,) = call(sum_kernel, [split], [], ids, own, *chunks)
    qa, kv = call(final_kernel, [((rows, 4 * HD), BF16), ((rows, HD), BF16)], [], ids, partial, swap(partial, "yl"))
    heads, row_sum = call(
        attend_kernel, [((rows, 6 * HD), BF16), ((1, rows), F32)], [], ids, qa, kv, swap(kv, "c")
    )
    row_sum = row_sum + swap(row_sum, "c")
    heads = [heads] + [shift_x(heads, s) for s in range(1, NX)]

    g, n = GROWS, BLOCK
    up, down, t4a, t4b, *back, gain_own, d_heads, attended_t, shared_terms = call(
        gradient_kernel,
        [((g + 4 * n, HD), BF16)] * 2
        + [((g + n, HD), BF16)] * 2
        + [((rows + g, sub), BF16)] * 4
        + [((g, HD), BF16), ((512, 6 * HD), BF16), ((4 * HD, 512), BF16), ((sub, 2 * HD), F32)],
        [],
        ids,
        *heads,
        *[swap(h, "c") for h in heads],
        normed_t,
        cot_sw,
        unit_sw,
        w_all,
    )
    t0, t2, m2 = call(
        near_kernel, [((2 * n, HD), BF16)] * 3, [], ids, normed_t, cot_sw, d_heads, attended_t, shared_terms
    )
    c4, d4 = shift_z(t4a, 2), shift_z(t4b, -2)
    a, b = shift_z(up, 1), shift_z(down, -1)
    a, row_sum = lax.optimization_barrier((a, row_sum))
    up, down, *back = call(
        relay_kernel,
        [((2 * n, HD), BF16)] * 2 + [((rows + g, sub), BF16)] * 4,
        [],
        ids,
        t2,
        m2,
        a,
        b,
        c4,
        d4,
        gain_own,
        *back,
        aliases={8 + s: 2 + s for s in range(NX)},
    )
    up, down = shift_z(up, 2), shift_z(down, -2)

    pieces = [back[0]] + [shift_x(back[s], -s) for s in range(1, NX)]
    to_same, to_other = call(finish_kernel, [((n, HD), BF16)] * 2, [], ids, t0, a, b, up, down)
    arrived = (lax.ppermute(to_same, AXES, inverse(owner_perm(0))), lax.ppermute(to_other, AXES, inverse(owner_perm(1))))
    (gain_z,) = call(gain_kernel, [((8 * NX, HD), F32)], [], ids, *pieces)
    gain_z = gain_z + swap(gain_z, "yh")
    (grad_input,) = call(
        input_kernel,
        [((rows, quarter), F32)],
        [],
        ids,
        *pieces,
        tokens,
        gain_f,
        total,
        row_sum,
        static=width,
    )
    *arrived, grad_input, gain_z = lax.optimization_barrier((*arrived, grad_input, gain_z))
    (shared_own,) = call(shared_kernel, [((2 * PIECE, HD), BF16)], [], ids, *arrived)
    grad_query, grad_out = call(owner_kernel, [((HD, HD), F32)] * 2, [], ids, *arrived, static=loss_scale)
    shared_yl = swap(shared_own, "yl")
    gain_z = gain_z[: 4 * NX] + shift_z(gain_z[4 * NX :], 4)
    grad_key, grad_value, grad_gain = call(
        join_kernel,
        [((rows, HD), F32)] * 2 + [((4 * NX, 1, HD), F32)],
        [],
        ids,
        shared_own,
        swap(shared_own, "c"),
        shared_yl,
        swap(shared_yl, "c"),
        gain_z,
        static=loss_scale,
    )
    grad_gain = grad_gain.reshape(quarter)
    return (grad_input, grad_gain, grad_query, grad_key, grad_value, grad_out)


def solution(mesh):
    fine = Mesh(mesh.devices.reshape(2, NX, NZ, 2, 2), AXES)
    in_specs = (P(FSDP, TP), P(TP), P(FSDP, TP), P(FSDP, None), P(FSDP, None), P(TP, FSDP), P(FSDP, TP))
    out_specs = (P(FSDP, TP), P(TP), P(FSDP, TP), P(FSDP, None), P(FSDP, None), P(TP, FSDP))
    return jax.shard_map(local, mesh=fine, in_specs=in_specs, out_specs=out_specs, check_vma=False)
```

```python
import functools
import math

import jax
import jax.numpy as jnp
from jax import lax
from jax.experimental import pallas as pl
from jax.experimental.pallas import tpu as pltpu
from jax.sharding import Mesh, PartitionSpec as P

HD = 128
NX = 4
NZ = 8
AXES = ("yh", "x", "z", "yl", "c")
FSDP = ("yh", "x", "z")
TP = ("yl", "c")
F32 = jnp.float32
BF16 = jnp.bfloat16
PIECE = 32
BLOCK = 2 * HD + 2 * PIECE
GROWS = 16
VMEM = pl.BlockSpec(memory_space=pltpu.VMEM)
SMEM = pl.BlockSpec(memory_space=pltpu.SMEM)
ANY = pl.BlockSpec(memory_space=pl.ANY)


def flat(yh, x, z, yl, c):
    return (((yh * NX + x) * NZ + z) * 2 + yl) * 2 + c


def owner_perm(flip):
    pairs = []
    for yh in range(2):
        for x in range(NX):
            for z in range(NZ):
                for yl in range(2):
                    for c in range(2):
                        dest_x = (x % 2) * 2 + z % 2
                        dest_z = (z // 2) * 2 + c
                        pairs.append((flat(yh, x, z, yl, c), flat(yl ^ flip, dest_x, dest_z, yh, x // 2)))
    return pairs


def inverse(pairs):
    return [(d, s) for s, d in pairs]


def shift_x(value, by):
    return lax.ppermute(value, "x", [(i, (i + by) % NX) for i in range(NX)])


def shift_z(value, by):
    return lax.ppermute(value, "z", [(i, (i + by) % NZ) for i in range(NZ)])


def swap(value, axis):
    return lax.ppermute(value, axis, [(0, 1), (1, 0)])


def dot(a, b, ca, cb):
    return lax.dot_general(a, b, (((ca,), (cb,)), ((), ())), preferred_element_type=F32)


def lanes(start, size=HD):
    return pl.ds(pl.multiple_of(start, HD), size)


def feature(at, j):
    return ((at // 2) * 8 + 2 * j + at % 2) * HD


def call(body, outs, scratch, ids, *args, static=None, aliases={}, after=None, copies=0):
    body = body if static is None else functools.partial(body, static)
    return pl.pallas_call(
        body,
        out_shape=[jax.ShapeDtypeStruct(s, d) for s, d in outs],
        in_specs=[SMEM] + [ANY if copies else VMEM] * len(args) + [ANY] * (after is not None),
        out_specs=[VMEM] * len(outs),
        input_output_aliases=aliases,
        scratch_shapes=[pltpu.VMEM(s, d) for s, d in scratch]
        + [pltpu.SemaphoreType.DMA((copies,))] * (copies > 0),
        compiler_params=pltpu.CompilerParams(vmem_limit_bytes=16 * 2**20),
    )(ids, *args, *(() if after is None else (after,)))


def pack_kernel(ids, w_query, w_key, w_value, w_out, out, sems):
    part = pl.ds(pl.multiple_of((2 * ids[1] + ids[2]) * PIECE, PIECE), PIECE)
    copies = [
        pltpu.make_async_copy(src, dst, sems.at[k])
        for k, (src, dst) in enumerate(
            (
                (w_query, out.at[:HD]),
                (w_out, out.at[HD : 2 * HD]),
                (w_key.at[part], out.at[2 * HD : 2 * HD + PIECE]),
                (w_value.at[part], out.at[2 * HD + PIECE :]),
            )
        )
    ]
    for copy in copies:
        copy.start()
    for copy in copies:
        copy.wait()


def spread_kernel(ids, tokens_in, cot_in, total_out, *refs):
    outs, tokens, cot, sems = refs[:NX], refs[NX], refs[NX + 1], refs[NX + 2]
    copies = [pltpu.make_async_copy(tokens_in, tokens, sems.at[0]), pltpu.make_async_copy(cot_in, cot, sems.at[1])]
    for copy in copies:
        copy.start()
    for copy in copies:
        copy.wait()
    rows = tokens.shape[0]
    squares = jnp.zeros((rows, HD), F32)
    for s in range(NX):
        at = (ids[4] + s) % NX
        for j in range(4):
            block, cols = lanes(feature(at, j)), slice(j * HD, (j + 1) * HD)
            value = tokens[:, block]
            squares = squares + value.astype(F32) * value.astype(F32)
            outs[s][:rows, cols] = value
            outs[s][rows : 2 * rows, cols] = cot[:, block]
    total_out[...] = jnp.sum(jnp.transpose(squares), axis=0, keepdims=True)


def stamp_kernel(ids, total, *refs):
    total = total[...]
    high = total.astype(BF16).astype(F32)
    middle = (total - high).astype(BF16).astype(F32)
    extra = jnp.concatenate([high, middle, total - high - middle, jnp.zeros((GROWS - 3, HD), F32)], axis=0)
    extra = jnp.concatenate([extra] * 4, axis=1).astype(BF16)
    for out in refs[NX:]:
        out[2 * HD :] = extra


def normalize_kernel(width, ids, *refs):
    parts, (gain, unit, normed, cot) = refs[:4], refs[4:]
    for s in range(NX):
        rows = slice(s * HD, (s + 1) * HD)
        terms = parts[s][2 * HD :, :HD].astype(F32)
        total = (terms[2:3] + terms[1:2]) + terms[0:1]
        column = jnp.transpose(jnp.broadcast_to(total, (HD, HD)))
        inv = lax.rsqrt(column / width + 1e-05)
        for j in range(4):
            cols = slice(j * HD, (j + 1) * HD)
            value = parts[s][:HD, cols].astype(F32) * inv
            unit[rows, cols] = value
            normed[rows, cols] = (value * gain[:, lanes(feature(ids[4], j))]).astype(BF16)
        cot[rows] = parts[s][HD : 2 * HD]


def forward_pack_kernel(ids, both, prev, after, up, down, far_first, far_second):
    for out, ref in ((up, prev), (down, after)):
        out[: 2 * BLOCK] = both[...]
        out[2 * BLOCK :] = ref[...]
    far_first[...] = prev[:BLOCK]
    far_second[...] = after[BLOCK:]


def product(outs, side, normed, cot, w_all, w_out):
    w_q = w_all[:, lanes(side * 2 * HD, 2 * HD)]
    w_kv = w_all[:, lanes((4 + side) * HD)]
    w_o = w_out[side]
    for r in range(0, 512, 256):
        rows = slice(r, r + 256)
        query = dot(normed[rows], w_q, 1, 0)
        attn_grad = dot(cot[rows], w_o, 1, 1)
        shared = dot(normed[rows], w_kv, 1, 0)
        for half in range(2):
            out, part = outs[r // HD + half], slice(half * HD, (half + 1) * HD)
            out[:, : 2 * HD] = query[part]
            out[:, 2 * HD : 4 * HD] = attn_grad[part]
            out[:, 4 * HD :] = shared[part]


def theirs_kernel(ids, both, prev1, next1, prev2, next2, far_first, far_second, normed, cot, *refs):
    outs, w_all, w_out = refs[:NX], refs[NX], refs[NX + 1]
    z, c = ids[0], ids[2]

    def place(ref, base, d, half):
        zt = (z + d + NZ) % NZ
        side, j = zt % 2, zt // 2
        rows = pl.ds(pl.multiple_of(j * HD, HD), HD)
        w_all[rows, lanes(side * 2 * HD + half * HD)] = ref[base : base + HD]
        w_out[side, half * HD : (half + 1) * HD, lanes(j * HD)] = ref[base + HD : base + 2 * HD]
        part = pl.ds(pl.multiple_of(j * HD + (2 * half + side) * PIECE, PIECE), PIECE)
        w_all[part, 4 * HD : 5 * HD] = ref[base + 2 * HD : base + 2 * HD + PIECE]
        w_all[part, 5 * HD : 6 * HD] = ref[base + 2 * HD + PIECE : base + BLOCK]

    for ref, base, d in (
        (both, 0, 0),
        (prev1, 0, -1),
        (prev1, 2 * BLOCK, -3),
        (next1, 0, 1),
        (next1, 2 * BLOCK, 3),
        (prev2, 0, -2),
        (next2, 0, 2),
    ):
        place(ref, base, d, 0)
        place(ref, base + BLOCK, d, 1)
    place(far_first, 0, 4, 0)
    place(far_second, 0, 4, 1)
    product(outs, 1 - c, normed, cot, w_all, w_out)


def mine_kernel(ids, normed, cot, w_all, w_out, *refs):
    outs, normed_t = refs[:NX], refs[NX]
    product(outs, ids[2], normed, cot, w_all, w_out)
    for s in range(NX):
        for j in range(4):
            rows, cols = slice(s * HD, (s + 1) * HD), slice(j * HD, (j + 1) * HD)
            normed_t[cols, rows] = jnp.transpose(normed[rows, cols])


def split_store(ref, total):
    for start, size, at in ((0, 2 * HD, 0), (4 * HD, HD, 6 * HD)):
        value = total[:, start : start + size]
        high = value.astype(BF16)
        ref[:, at : at + size] = high
        ref[:, at + size : at + 2 * size] = (value - high.astype(F32)).astype(BF16)
    ref[:, 4 * HD : 6 * HD] = total[:, 2 * HD : 4 * HD].astype(BF16)


def joined(ref):
    value = ref[...].astype(F32)
    return jnp.concatenate(
        [
            value[:, : 2 * HD] + value[:, 2 * HD : 4 * HD],
            value[:, 4 * HD : 6 * HD],
            value[:, 6 * HD : 7 * HD] + value[:, 7 * HD :],
        ],
        axis=1,
    )


def chunk_kernel(ids, mine, got, out):
    split_store(out, mine[...] + got[...])


def own_kernel(ids, mine, got, out):
    out[...] = mine[...] + got[...]


def sum_kernel(ids, own, a, b, c, out):
    split_store(out, own[...] + joined(a) + joined(b) + joined(c))


def final_kernel(ids, mine, got, qa, kv):
    total = (joined(mine) + joined(got)).astype(BF16)
    qa[...] = total[:, : 4 * HD]
    kv[...] = total[:, 4 * HD :]


def attend_kernel(ids, qa, kv_mine, kv_theirs, out, row_out):
    first = ids[2] == 0
    mine, theirs = kv_mine[...].astype(F32), kv_theirs[...].astype(F32)
    key_rows = jnp.where(first, mine, theirs).astype(BF16)
    value_rows = jnp.where(first, theirs, mine).astype(BF16)
    causal = lax.broadcasted_iota(jnp.int32, (HD, HD), 0) >= lax.broadcasted_iota(jnp.int32, (HD, HD), 1)
    keys = jnp.zeros((HD, HD), F32)
    values = jnp.zeros((HD, HD), F32)
    row_terms = jnp.zeros((HD, HD), F32)
    for h in range(2):
        query = qa[:, h * HD : (h + 1) * HD]
        attn_grad = qa[:, (2 + h) * HD : (3 + h) * HD]
        scores = dot(query, key_rows, 1, 1) * HD ** (-0.5)
        scores = jnp.where(causal, scores, jnp.float32(-1e30))
        shifted = jnp.exp(scores - jnp.max(scores, axis=-1, keepdims=True))
        softmax_out = shifted / jnp.sum(shifted, axis=-1, keepdims=True)
        rounded = softmax_out.astype(BF16)
        dprob = dot(attn_grad, value_rows, 1, 1)
        dscore = softmax_out * (dprob - jnp.sum(dprob * softmax_out, axis=-1, keepdims=True)) * HD ** (-0.5)
        dscore = dscore.astype(BF16)
        d_query = dot(dscore, key_rows, 1, 0).astype(BF16)
        out[:, h * HD : (h + 1) * HD] = d_query
        row_terms = row_terms + d_query.astype(F32) * query.astype(F32)
        out[:, (2 + h) * HD : (3 + h) * HD] = dot(rounded, value_rows, 1, 0).astype(BF16)
        keys = keys + dot(dscore, query, 0, 0).astype(BF16).astype(F32)
        values = values + dot(rounded, attn_grad, 0, 0).astype(BF16).astype(F32)
    out[:, 4 * HD : 5 * HD] = keys.astype(BF16)
    out[:, 5 * HD :] = values.astype(BF16)
    row_terms = row_terms + keys * key_rows.astype(F32) + values * value_rows.astype(F32)
    row_out[...] = jnp.sum(jnp.transpose(row_terms), axis=0, keepdims=True)


def gradient_kernel(ids, *refs):
    mine, theirs, (normed_t, cot, unit, w_all) = refs[:4], refs[4:8], refs[8:12]
    (up, down, t4a, t4b), back, (gain_out, heads, attended, shared) = refs[12:16], refs[16:20], refs[20:]
    c = ids[2]
    for s in range(NX):
        rows = slice(s * HD, (s + 1) * HD)
        for ref, side in ((mine[s], c), (theirs[s], 1 - c)):
            heads[rows, lanes(side * 2 * HD, 2 * HD)] = ref[:, : 2 * HD]
            for half in range(2):
                at = pl.ds(pl.multiple_of((2 * side + half) * HD, HD), HD)
                attended[at, rows] = jnp.transpose(ref[:, (2 + half) * HD : (3 + half) * HD])
        total = mine[s][:, 4 * HD :].astype(F32) + theirs[s][:, 4 * HD :].astype(F32)
        heads[rows, 4 * HD :] = total.astype(BF16)

    gain_sum = jnp.zeros((1, 4 * HD), F32)
    for s in range(NX):
        rows = slice(s * HD, (s + 1) * HD)
        term = dot(heads[rows], w_all[...], 1, 1)
        back[s][:HD] = term.astype(BF16)
        gain_sum = gain_sum + jnp.sum(term * unit[rows], axis=0, keepdims=True)
    gain_rows = jnp.concatenate([gain_sum[:, j * HD : (j + 1) * HD] for j in range(4)], axis=0)
    high = gain_rows.astype(BF16).astype(F32)
    gain_rows = jnp.concatenate([high, gain_rows - high, jnp.zeros((8, HD), F32)], axis=0).astype(BF16)

    shared[...] = dot(normed_t[...], heads[:, 4 * HD :], 1, 0)
    g, n = GROWS, BLOCK
    for ref in (up, down, t4a, t4b):
        ref[:g] = gain_rows
    terms(
        ids,
        normed_t,
        cot,
        heads,
        attended,
        shared,
        (
            (1, up.at[g : g + n], up.at[g + n : g + 2 * n]),
            (3, up.at[g + 2 * n : g + 3 * n], up.at[g + 3 * n :]),
            (-1, down.at[g : g + n], down.at[g + n : g + 2 * n]),
            (-3, down.at[g + 2 * n : g + 3 * n], down.at[g + 3 * n :]),
            (4, t4a.at[g:], t4b.at[g:]),
        ),
    )
    gain_out[...] = gain_rows


def terms(ids, normed_t, cot, heads, attended, shared, places):
    z = ids[0]
    for d, out_first, out_second in places:
        zt = (z + d + NZ) % NZ
        side, j = zt % 2, zt // 2
        rows = pl.ds(pl.multiple_of(j * HD, HD), HD)
        g_q = dot(normed_t[rows], heads[:, lanes(side * 2 * HD, 2 * HD)], 1, 0).astype(BF16)
        rows = pl.ds(pl.multiple_of(side * 2 * HD, 2 * HD), 2 * HD)
        g_o = dot(attended[rows], cot[:, lanes(j * HD)], 1, 0).astype(BF16)
        for half, out in enumerate((out_first, out_second)):
            out[:HD] = g_q[:, half * HD : (half + 1) * HD]
            out[HD : 2 * HD] = g_o[half * HD : (half + 1) * HD]
            part = shared[pl.ds(pl.multiple_of(j * HD + (2 * half + side) * PIECE, PIECE), PIECE), :].astype(BF16)
            out[2 * HD : 2 * HD + PIECE] = part[:, :HD]
            out[2 * HD + PIECE :] = part[:, HD:]


def near_kernel(ids, normed_t, cot, heads, attended, shared, t0, t2, m2):
    n = BLOCK
    terms(ids, normed_t, cot, heads, attended, shared, [(d, r.at[:n], r.at[n:]) for d, r in ((0, t0), (2, t2), (-2, m2))])


def relay_kernel(ids, t2, m2, a, b, c, d, gain_own, *refs):
    up, down, *back = refs[NX:]
    g, n = GROWS, BLOCK
    total = t2[...].astype(F32) + a[g + 2 * n :].astype(F32)
    up[:n] = (total[:n] + c[g:].astype(F32)).astype(BF16)
    up[n:] = total[n:].astype(BF16)
    total = m2[...].astype(F32) + b[g + 2 * n :].astype(F32)
    down[:n] = total[:n].astype(BF16)
    down[n:] = (total[n:] + d[g:].astype(F32)).astype(BF16)
    three = gain_own[...].astype(F32) + a[:g].astype(F32) + b[:g].astype(F32)
    five = three + c[:g].astype(F32) + d[:g].astype(F32)
    terms = []
    for rows in (five, three):
        value = rows[:4] + rows[4:8]
        high = value.astype(BF16).astype(F32)
        terms += [high, value - high]
    for j in range(4):
        rows = jnp.concatenate([t[j : j + 1] for t in terms] + [jnp.zeros((g - 4, HD), F32)], axis=0).astype(BF16)
        for ref in back:
            ref[HD:, j * HD : (j + 1) * HD] = rows


def finish_kernel(ids, t0, a, b, up, down, same, other):
    g, n = GROWS, BLOCK
    flip = ids[3]
    near = slice(g, g + 2 * n)
    total = t0[...].astype(F32) + a[near].astype(F32) + b[near].astype(F32)
    total = total + up[...].astype(F32) + down[...].astype(F32)
    same[...] = jnp.where(flip == 0, total[:n], total[n:]).astype(BF16)
    other[...] = jnp.where(flip == 0, total[n:], total[:n]).astype(BF16)


def gain_kernel(ids, *refs):
    out = refs[NX]
    for s in range(NX):
        rows = refs[s][HD:].astype(F32)
        for at in (0, 2):
            value = rows[at : at + 1] + rows[at + 1 : at + 2]
            for j in range(4):
                row = 2 * NX * at + 4 * s + j
                out[row : row + 1] = value[:, j * HD : (j + 1) * HD]


def input_kernel(sizes, ids, a, b, c, d, tokens, gain, total, row_sum, same, other, later, out, grad_query, grad_out):
    width, scale = sizes
    for grad, at in ((grad_query, slice(0, HD)), (grad_out, slice(HD, 2 * HD))):
        grad[...] = (same[at].astype(F32) + other[at].astype(F32)) * scale
    inv = lax.rsqrt(jnp.transpose(jnp.broadcast_to(total[...], (HD, HD))) / width + 1e-05)
    row_mean = jnp.transpose(jnp.broadcast_to(row_sum[...], (HD, HD))) / width
    for s, ref in enumerate((a, b, c, d)):
        at = (ids[4] + s) % NX
        for j in range(4):
            cols = lanes(feature(at, j))
            unit = tokens[:, cols].astype(F32) * inv
            scaled = ref[:HD, j * HD : (j + 1) * HD].astype(F32) * gain[:, cols]
            out[:, cols] = inv * (scaled - unit * row_mean)


def shared_kernel(ids, a, b, shared):
    shared[...] = (a[2 * HD :].astype(F32) + b[2 * HD :].astype(F32)).astype(BF16)


def join_kernel(scale, ids, own, by_c, by_yl, by_both, gains, grad_key, grad_value, grad_gain):
    yl, c, x = ids[1], ids[2], ids[4]
    for ref, at in ((own, 2 * yl + c), (by_c, 2 * yl + 1 - c), (by_yl, 2 - 2 * yl + c), (by_both, 3 - 2 * yl - c)):
        rows = pl.ds(pl.multiple_of(at * PIECE, PIECE), PIECE)
        grad_key[rows] = ref[:PIECE].astype(F32) * scale
        grad_value[rows] = ref[PIECE:].astype(F32) * scale
    for s in range(NX):
        at = (x + s) % NX
        for j in range(4):
            grad_gain[pl.ds((at // 2) * 8 + 2 * j + at % 2, 1)] = gains[4 * s + j : 4 * s + j + 1] * scale


def local(tokens, gain, w_query, w_key, w_value, w_out, cotangent):
    rows, quarter = tokens.shape
    sub = quarter // NX
    width = quarter * 4
    yh, x, z, yl, c = (lax.axis_index(a) for a in AXES)
    ids = jnp.stack([z, yl, c, yh, x]).astype(jnp.int32)
    loss_scale = 1.0 / math.sqrt(rows * 64)

    (pack,) = call(pack_kernel, [((BLOCK, HD), BF16)], [], ids, w_query, w_key, w_value, w_out, copies=4)
    same = lax.ppermute(pack, AXES, owner_perm(0))
    other = lax.ppermute(pack, AXES, owner_perm(1))
    part_shape = ((2 * rows + GROWS, sub), BF16)
    total, *parts = call(
        spread_kernel,
        [((1, rows), F32)] + [part_shape] * 4,
        [(tokens.shape, BF16)] * 2,
        ids,
        tokens,
        cotangent,
        copies=2,
    )
    total = total + swap(total, "c")
    same, other, total = lax.optimization_barrier((same, other, total))
    total = total + swap(total, "yl")
    both = jnp.where(yh == 0, jnp.concatenate([same, other]), jnp.concatenate([other, same]))
    prev2, next2 = shift_z(both, 2), shift_z(both, -2)
    double, half_shape = ((4 * BLOCK, HD), BF16), ((BLOCK, HD), BF16)
    relays = call(forward_pack_kernel, [double] * 2 + [half_shape] * 2, [], ids, both, prev2, next2)
    prev1, next1 = shift_z(relays[0], 1), shift_z(relays[1], -1)
    far_first, far_second = shift_z(relays[2], 2), shift_z(relays[3], -2)
    weights = (both, prev1, next1, prev2, next2, far_first, far_second)

    parts = call(stamp_kernel, [part_shape] * 4, [], ids, total, *parts, aliases={2 + s: s for s in range(4)})
    parts = [parts[0]] + [shift_x(parts[s], s) for s in range(1, NX)]
    gain_f = gain.astype(F32).reshape(1, quarter)
    unit_sw, normed_sw, cot_sw = call(
        normalize_kernel,
        [((512, sub), F32), ((512, sub), BF16), ((512, sub), BF16)],
        [],
        ids,
        *parts,
        gain_f,
        static=width,
    )

    *theirs, w_all, w_heads = call(
        theirs_kernel,
        [((rows, 5 * HD), F32)] * 4 + [((sub, 6 * HD), BF16), ((2, 2 * HD, sub), BF16)],
        [],
        ids,
        *weights,
        normed_sw,
        cot_sw,
    )
    got = [None] + [swap(theirs[s], "c") for s in range(1, NX)]
    got[0] = swap(theirs[0], "c")
    *mine, normed_t = call(
        mine_kernel,
        [((rows, 5 * HD), F32)] * 4 + [((sub, 512), BF16)],
        [],
        ids,
        normed_sw,
        cot_sw,
        w_all,
        w_heads,
    )
    split = ((rows, 8 * HD), BF16)
    chunks = [shift_x(call(chunk_kernel, [split], [], ids, mine[s], got[s])[0], -s) for s in range(1, NX)]
    (own,) = call(own_kernel, [((rows, 5 * HD), F32)], [], ids, mine[0], got[0])
    (partial,) = call(sum_kernel, [split], [], ids, own, *chunks)
    qa, kv = call(final_kernel, [((rows, 4 * HD), BF16), ((rows, HD), BF16)], [], ids, partial, swap(partial, "yl"))
    heads, row_sum = call(
        attend_kernel, [((rows, 6 * HD), BF16), ((1, rows), F32)], [], ids, qa, kv, swap(kv, "c")
    )
    row_sum = row_sum + swap(row_sum, "c")
    heads = [heads] + [shift_x(heads, s) for s in range(1, NX)]

    g, n = GROWS, BLOCK
    up, down, t4a, t4b, *back, gain_own, d_heads, attended_t, shared_terms = call(
        gradient_kernel,
        [((g + 4 * n, HD), BF16)] * 2
        + [((g + n, HD), BF16)] * 2
        + [((rows + g, sub), BF16)] * 4
        + [((g, HD), BF16), ((512, 6 * HD), BF16), ((4 * HD, 512), BF16), ((sub, 2 * HD), F32)],
        [],
        ids,
        *heads,
        *[swap(h, "c") for h in heads],
        normed_t,
        cot_sw,
        unit_sw,
        w_all,
    )
    t0, t2, m2 = call(
        near_kernel, [((2 * n, HD), BF16)] * 3, [], ids, normed_t, cot_sw, d_heads, attended_t, shared_terms
    )
    c4, d4 = shift_z(t4a, 2), shift_z(t4b, -2)
    a, b = shift_z(up, 1), shift_z(down, -1)
    a, row_sum = lax.optimization_barrier((a, row_sum))
    up, down, *back = call(
        relay_kernel,
        [((2 * n, HD), BF16)] * 2 + [((rows + g, sub), BF16)] * 4,
        [],
        ids,
        t2,
        m2,
        a,
        b,
        c4,
        d4,
        gain_own,
        *back,
        aliases={8 + s: 2 + s for s in range(NX)},
    )
    up, down = shift_z(up, 2), shift_z(down, -2)

    pieces = [back[0]] + [shift_x(back[s], -s) for s in range(1, NX)]
    to_same, to_other = call(finish_kernel, [((n, HD), BF16)] * 2, [], ids, t0, a, b, up, down)
    arrived = (lax.ppermute(to_same, AXES, inverse(owner_perm(0))), lax.ppermute(to_other, AXES, inverse(owner_perm(1))))
    (gain_z,) = call(gain_kernel, [((8 * NX, HD), F32)], [], ids, *pieces)
    gain_z = gain_z + swap(gain_z, "yh")
    *arrived, gain_z = lax.optimization_barrier((*arrived, gain_z))
    (shared_own,) = call(shared_kernel, [((2 * PIECE, HD), BF16)], [], ids, *arrived)
    shared_yl = swap(shared_own, "yl")
    grad_input, grad_query, grad_out = call(
        input_kernel,
        [((rows, quarter), F32)] + [((HD, HD), F32)] * 2,
        [],
        ids,
        *pieces,
        tokens,
        gain_f,
        total,
        row_sum,
        *arrived,
        static=(width, loss_scale),
        after=shared_own,
    )
    gain_z = gain_z[: 4 * NX] + shift_z(gain_z[4 * NX :], 4)
    grad_key, grad_value, grad_gain = call(
        join_kernel,
        [((rows, HD), F32)] * 2 + [((4 * NX, HD), F32)],
        [],
        ids,
        shared_own,
        swap(shared_own, "c"),
        shared_yl,
        swap(shared_yl, "c"),
        gain_z,
        static=loss_scale,
    )
    grad_gain = grad_gain.reshape(quarter)
    return (grad_input, grad_gain, grad_query, grad_key, grad_value, grad_out)


def solution(mesh):
    fine = Mesh(mesh.devices.reshape(2, NX, NZ, 2, 2), AXES)
    in_specs = (P(FSDP, TP), P(TP), P(FSDP, TP), P(FSDP, None), P(FSDP, None), P(TP, FSDP), P(FSDP, TP))
    out_specs = (P(FSDP, TP), P(TP), P(FSDP, TP), P(FSDP, None), P(FSDP, None), P(TP, FSDP))
    return jax.shard_map(local, mesh=fine, in_specs=in_specs, out_specs=out_specs, check_vma=False)
```

```python
import functools
import math

import jax
import jax.numpy as jnp
from jax import lax
from jax.experimental import pallas as pl
from jax.experimental.pallas import tpu as pltpu
from jax.sharding import Mesh, PartitionSpec as P

HD = 128
NX = 4
NZ = 8
AXES = ("yh", "x", "z", "yl", "c")
FSDP = ("yh", "x", "z")
TP = ("yl", "c")
F32 = jnp.float32
BF16 = jnp.bfloat16
PIECE = 32
BLOCK = 2 * HD + 2 * PIECE
GROWS = 16
VMEM = pl.BlockSpec(memory_space=pltpu.VMEM)
SMEM = pl.BlockSpec(memory_space=pltpu.SMEM)


def flat(yh, x, z, yl, c):
    return (((yh * NX + x) * NZ + z) * 2 + yl) * 2 + c


def owner_perm(flip):
    pairs = []
    for yh in range(2):
        for x in range(NX):
            for z in range(NZ):
                for yl in range(2):
                    for c in range(2):
                        dest_x = (z % 2) * 2 + 1 - x % 2
                        dest_z = (z // 2) * 2 + c
                        pairs.append((flat(yh, x, z, yl, c), flat(yl ^ flip, dest_x, dest_z, yh, x // 2)))
    return pairs


def inverse(pairs):
    return [(d, s) for s, d in pairs]


def shift_x(value, by):
    return lax.ppermute(value, "x", [(i, (i + by) % NX) for i in range(NX)])


def shift_z(value, by):
    return lax.ppermute(value, "z", [(i, (i + by) % NZ) for i in range(NZ)])


def swap(value, axis):
    return lax.ppermute(value, axis, [(0, 1), (1, 0)])


def dot(a, b, ca, cb):
    return lax.dot_general(a, b, (((ca,), (cb,)), ((), ())), preferred_element_type=F32)


def lanes(start, size=HD):
    return pl.ds(pl.multiple_of(start, HD), size)


def feature(at, j):
    return ((1 - at % 2) * 8 + 2 * j + at // 2) * HD


def call(body, outs, scratch, ids, *args, static=None, aliases={}):
    body = body if static is None else functools.partial(body, static)
    return pl.pallas_call(
        body,
        out_shape=[jax.ShapeDtypeStruct(s, d) for s, d in outs],
        in_specs=[SMEM] + [VMEM] * len(args),
        out_specs=[VMEM] * len(outs),
        input_output_aliases=aliases,
        scratch_shapes=[pltpu.VMEM(s, d) for s, d in scratch],
        compiler_params=pltpu.CompilerParams(vmem_limit_bytes=16 * 2**20),
    )(ids, *args)


def spread_kernel(ids, tokens, cot, total_out, *outs):
    rows = tokens.shape[0]
    squares = jnp.zeros((rows, HD), F32)
    for s in range(NX):
        at = (ids[4] + s) % NX
        for j in range(4):
            block, cols = lanes(feature(at, j)), slice(j * HD, (j + 1) * HD)
            value = tokens[:, block]
            squares = squares + value.astype(F32) * value.astype(F32)
            outs[s][:rows, cols] = value
            outs[s][rows : 2 * rows, cols] = cot[:, block]
    total_out[...] = jnp.sum(jnp.transpose(squares), axis=0, keepdims=True)


def stamp_kernel(ids, total, *refs):
    total = total[...]
    high = total.astype(BF16).astype(F32)
    middle = (total - high).astype(BF16).astype(F32)
    extra = jnp.concatenate([high, middle, total - high - middle, jnp.zeros((GROWS - 3, HD), F32)], axis=0)
    extra = jnp.concatenate([extra] * 4, axis=1).astype(BF16)
    for out in refs[NX:]:
        out[2 * HD :] = extra


def normalize_kernel(width, ids, *refs):
    parts, (gain, unit, normed, cot) = refs[:4], refs[4:]
    for s in range(NX):
        rows = slice(s * HD, (s + 1) * HD)
        terms = parts[s][2 * HD :, :HD].astype(F32)
        total = (terms[2:3] + terms[1:2]) + terms[0:1]
        column = jnp.transpose(jnp.broadcast_to(total, (HD, HD)))
        inv = lax.rsqrt(column / width + 1e-05)
        for j in range(4):
            cols = slice(j * HD, (j + 1) * HD)
            value = parts[s][:HD, cols].astype(F32) * inv
            unit[rows, cols] = value
            normed[rows, cols] = (value * gain[:, lanes(feature(ids[4], j))]).astype(BF16)
        cot[rows] = parts[s][HD : 2 * HD]


def forward_pack_kernel(ids, both, prev, after, up, down, far_first, far_second):
    for out, ref in ((up, prev), (down, after)):
        out[: 2 * BLOCK] = both[...]
        out[2 * BLOCK :] = ref[...]
    far_first[...] = prev[:BLOCK]
    far_second[...] = after[BLOCK:]


def product(outs, side, normed, cot, w_all, w_out):
    w_q = w_all[:, lanes(side * 2 * HD, 2 * HD)]
    w_kv = w_all[:, lanes((4 + side) * HD)]
    w_o = w_out[side]
    for r in range(0, 512, 256):
        rows = slice(r, r + 256)
        query = dot(normed[rows], w_q, 1, 0)
        attn_grad = dot(cot[rows], w_o, 1, 1)
        shared = dot(normed[rows], w_kv, 1, 0)
        for half in range(2):
            out, part = outs[r // HD + half], slice(half * HD, (half + 1) * HD)
            out[:, : 2 * HD] = query[part]
            out[:, 2 * HD : 4 * HD] = attn_grad[part]
            out[:, 4 * HD :] = shared[part]


def theirs_kernel(ids, both, prev1, next1, prev2, next2, far_first, far_second, normed, cot, *refs):
    outs, w_all, w_out = refs[:NX], refs[NX], refs[NX + 1]
    z, c = ids[0], ids[2]

    def place(ref, base, d, half):
        zt = (z + d + NZ) % NZ
        side, j = zt % 2, zt // 2
        rows = pl.ds(pl.multiple_of(j * HD, HD), HD)
        w_all[rows, lanes(side * 2 * HD + half * HD)] = ref[base : base + HD]
        w_out[side, half * HD : (half + 1) * HD, lanes(j * HD)] = ref[base + HD : base + 2 * HD]
        part = pl.ds(pl.multiple_of(j * HD + (2 * half + side) * PIECE, PIECE), PIECE)
        w_all[part, 4 * HD : 5 * HD] = ref[base + 2 * HD : base + 2 * HD + PIECE]
        w_all[part, 5 * HD : 6 * HD] = ref[base + 2 * HD + PIECE : base + BLOCK]

    for ref, base, d in (
        (both, 0, 0),
        (prev1, 0, -1),
        (prev1, 2 * BLOCK, -3),
        (next1, 0, 1),
        (next1, 2 * BLOCK, 3),
        (prev2, 0, -2),
        (next2, 0, 2),
    ):
        place(ref, base, d, 0)
        place(ref, base + BLOCK, d, 1)
    place(far_first, 0, 4, 0)
    place(far_second, 0, 4, 1)
    product(outs, 1 - c, normed, cot, w_all, w_out)


def mine_kernel(ids, normed, cot, w_all, w_out, *outs):
    product(outs, ids[2], normed, cot, w_all, w_out)


def split_store(ref, total):
    for start, size, at in ((0, 2 * HD, 0), (4 * HD, HD, 6 * HD)):
        value = total[:, start : start + size]
        high = value.astype(BF16)
        ref[:, at : at + size] = high
        ref[:, at + size : at + 2 * size] = (value - high.astype(F32)).astype(BF16)
    ref[:, 4 * HD : 6 * HD] = total[:, 2 * HD : 4 * HD].astype(BF16)


def joined(ref):
    value = ref[...].astype(F32)
    return jnp.concatenate(
        [
            value[:, : 2 * HD] + value[:, 2 * HD : 4 * HD],
            value[:, 4 * HD : 6 * HD],
            value[:, 6 * HD : 7 * HD] + value[:, 7 * HD :],
        ],
        axis=1,
    )


def chunk_kernel(ids, mine, got, out):
    split_store(out, mine[...] + got[...])


def own_kernel(ids, mine, got, normed, out, normed_t):
    out[...] = mine[...] + got[...]
    for s in range(NX):
        for j in range(4):
            rows, cols = slice(s * HD, (s + 1) * HD), slice(j * HD, (j + 1) * HD)
            normed_t[cols, rows] = jnp.transpose(normed[rows, cols])


def sum_kernel(ids, own, a, b, c, out):
    split_store(out, own[...] + joined(a) + joined(b) + joined(c))


def final_kernel(ids, mine, got, qa, kv):
    total = (joined(mine) + joined(got)).astype(BF16)
    qa[...] = total[:, : 4 * HD]
    kv[...] = total[:, 4 * HD :]


def attend_kernel(ids, qa, kv_mine, kv_theirs, out, row_out):
    first = ids[2] == 0
    mine, theirs = kv_mine[...].astype(F32), kv_theirs[...].astype(F32)
    key_rows = jnp.where(first, mine, theirs).astype(BF16)
    value_rows = jnp.where(first, theirs, mine).astype(BF16)
    causal = lax.broadcasted_iota(jnp.int32, (HD, HD), 0) >= lax.broadcasted_iota(jnp.int32, (HD, HD), 1)
    keys = jnp.zeros((HD, HD), F32)
    values = jnp.zeros((HD, HD), F32)
    row_terms = jnp.zeros((HD, HD), F32)
    for h in range(2):
        query = qa[:, h * HD : (h + 1) * HD]
        attn_grad = qa[:, (2 + h) * HD : (3 + h) * HD]
        scores = dot(query, key_rows, 1, 1) * HD ** (-0.5)
        scores = jnp.where(causal, scores, jnp.float32(-1e30))
        shifted = jnp.exp(scores - jnp.max(scores, axis=-1, keepdims=True))
        softmax_out = shifted / jnp.sum(shifted, axis=-1, keepdims=True)
        rounded = softmax_out.astype(BF16)
        dprob = dot(attn_grad, value_rows, 1, 1)
        dscore = softmax_out * (dprob - jnp.sum(dprob * softmax_out, axis=-1, keepdims=True)) * HD ** (-0.5)
        dscore = dscore.astype(BF16)
        d_query = dot(dscore, key_rows, 1, 0).astype(BF16)
        out[:, h * HD : (h + 1) * HD] = d_query
        row_terms = row_terms + d_query.astype(F32) * query.astype(F32)
        out[:, (2 + h) * HD : (3 + h) * HD] = dot(rounded, value_rows, 1, 0).astype(BF16)
        keys = keys + dot(dscore, query, 0, 0).astype(BF16).astype(F32)
        values = values + dot(rounded, attn_grad, 0, 0).astype(BF16).astype(F32)
    out[:, 4 * HD : 5 * HD] = keys.astype(BF16)
    out[:, 5 * HD :] = values.astype(BF16)
    row_terms = row_terms + keys * key_rows.astype(F32) + values * value_rows.astype(F32)
    row_out[...] = jnp.sum(jnp.transpose(row_terms), axis=0, keepdims=True)


def gradient_kernel(ids, *refs):
    mine, theirs, (normed_t, cot, unit, w_all) = refs[:4], refs[4:8], refs[8:12]
    (up, down, t4a, t4b), back, (gain_out, heads, attended, shared) = refs[12:16], refs[16:20], refs[20:]
    c = ids[2]
    for s in range(NX):
        rows = slice(s * HD, (s + 1) * HD)
        for ref, side in ((mine[s], c), (theirs[s], 1 - c)):
            heads[rows, lanes(side * 2 * HD, 2 * HD)] = ref[:, : 2 * HD]
            for half in range(2):
                at = pl.ds(pl.multiple_of((2 * side + half) * HD, HD), HD)
                attended[at, rows] = jnp.transpose(ref[:, (2 + half) * HD : (3 + half) * HD])
        total = mine[s][:, 4 * HD :].astype(F32) + theirs[s][:, 4 * HD :].astype(F32)
        heads[rows, 4 * HD :] = total.astype(BF16)

    gain_sum = jnp.zeros((1, 4 * HD), F32)
    for s in range(NX):
        rows = slice(s * HD, (s + 1) * HD)
        term = dot(heads[rows], w_all[...], 1, 1)
        back[s][:HD] = term.astype(BF16)
        gain_sum = gain_sum + jnp.sum(term * unit[rows], axis=0, keepdims=True)
    gain_rows = jnp.concatenate([gain_sum[:, j * HD : (j + 1) * HD] for j in range(4)], axis=0)
    high = gain_rows.astype(BF16).astype(F32)
    gain_rows = jnp.concatenate([high, gain_rows - high, jnp.zeros((8, HD), F32)], axis=0).astype(BF16)

    shared[...] = dot(normed_t[...], heads[:, 4 * HD :], 1, 0)
    g, n = GROWS, BLOCK
    for ref in (up, down, t4a, t4b):
        ref[:g] = gain_rows
    terms(
        ids,
        normed_t,
        cot,
        heads,
        attended,
        shared,
        (
            (1, up.at[g : g + n], up.at[g + n : g + 2 * n]),
            (3, up.at[g + 2 * n : g + 3 * n], up.at[g + 3 * n :]),
            (-1, down.at[g : g + n], down.at[g + n : g + 2 * n]),
            (-3, down.at[g + 2 * n : g + 3 * n], down.at[g + 3 * n :]),
            (4, t4a.at[g:], t4b.at[g:]),
        ),
    )
    gain_out[...] = gain_rows


def terms(ids, normed_t, cot, heads, attended, shared, places):
    z = ids[0]
    for d, out_first, out_second in places:
        zt = (z + d + NZ) % NZ
        side, j = zt % 2, zt // 2
        rows = pl.ds(pl.multiple_of(j * HD, HD), HD)
        g_q = dot(normed_t[rows], heads[:, lanes(side * 2 * HD, 2 * HD)], 1, 0).astype(BF16)
        rows = pl.ds(pl.multiple_of(side * 2 * HD, 2 * HD), 2 * HD)
        g_o = dot(attended[rows], cot[:, lanes(j * HD)], 1, 0).astype(BF16)
        for half, out in enumerate((out_first, out_second)):
            out[:HD] = g_q[:, half * HD : (half + 1) * HD]
            out[HD : 2 * HD] = g_o[half * HD : (half + 1) * HD]
            part = shared[pl.ds(pl.multiple_of(j * HD + (2 * half + side) * PIECE, PIECE), PIECE), :].astype(BF16)
            out[2 * HD : 2 * HD + PIECE] = part[:, :HD]
            out[2 * HD + PIECE :] = part[:, HD:]


def near_kernel(ids, normed_t, cot, heads, attended, shared, t0, t2, m2):
    n = BLOCK
    terms(ids, normed_t, cot, heads, attended, shared, [(d, r.at[:n], r.at[n:]) for d, r in ((0, t0), (2, t2), (-2, m2))])


def relay_kernel(ids, t2, m2, a, b, c, d, gain_own, *refs):
    up, down, *back = refs[NX:]
    g, n = GROWS, BLOCK
    total = t2[...].astype(F32) + a[g + 2 * n :].astype(F32)
    up[:n] = (total[:n] + c[g:].astype(F32)).astype(BF16)
    up[n:] = total[n:].astype(BF16)
    total = m2[...].astype(F32) + b[g + 2 * n :].astype(F32)
    down[:n] = total[:n].astype(BF16)
    down[n:] = (total[n:] + d[g:].astype(F32)).astype(BF16)
    three = gain_own[...].astype(F32) + a[:g].astype(F32) + b[:g].astype(F32)
    five = three + c[:g].astype(F32) + d[:g].astype(F32)
    terms = []
    for rows in (five, three):
        value = rows[:4] + rows[4:8]
        high = value.astype(BF16).astype(F32)
        terms += [high, value - high]
    for j in range(4):
        rows = jnp.concatenate([t[j : j + 1] for t in terms] + [jnp.zeros((g - 4, HD), F32)], axis=0).astype(BF16)
        for ref in back:
            ref[HD:, j * HD : (j + 1) * HD] = rows


def finish_kernel(ids, t0, a, b, up, down, same, other):
    g, n = GROWS, BLOCK
    flip = ids[3]
    near = slice(g, g + 2 * n)
    total = t0[...].astype(F32) + a[near].astype(F32) + b[near].astype(F32)
    total = total + up[...].astype(F32) + down[...].astype(F32)
    same[...] = jnp.where(flip == 0, total[:n], total[n:]).astype(BF16)
    other[...] = jnp.where(flip == 0, total[n:], total[:n]).astype(BF16)


def gain_kernel(ids, *refs):
    out = refs[NX]
    for s in range(NX):
        rows = refs[s][HD:].astype(F32)
        for at in (0, 2):
            value = rows[at : at + 1] + rows[at + 1 : at + 2]
            for j in range(4):
                row = 2 * NX * at + 4 * s + j
                out[row : row + 1] = value[:, j * HD : (j + 1) * HD]


def input_kernel(width, ids, a, b, c, d, tokens, gain, total, row_sum, out):
    inv = lax.rsqrt(jnp.transpose(jnp.broadcast_to(total[...], (HD, HD))) / width + 1e-05)
    row_mean = jnp.transpose(jnp.broadcast_to(row_sum[...], (HD, HD))) / width
    for s, ref in enumerate((a, b, c, d)):
        at = (ids[4] + s) % NX
        for j in range(4):
            cols = lanes(feature(at, j))
            unit = tokens[:, cols].astype(F32) * inv
            scaled = ref[:HD, j * HD : (j + 1) * HD].astype(F32) * gain[:, cols]
            out[:, cols] = inv * (scaled - unit * row_mean)


def owner_kernel(scale, ids, same, other, grad_query, grad_out):
    for grad, at in ((grad_query, slice(0, HD)), (grad_out, slice(HD, 2 * HD))):
        grad[...] = (same[at].astype(F32) + other[at].astype(F32)) * scale


def shared_kernel(ids, a, b, shared):
    shared[...] = (a[2 * HD :].astype(F32) + b[2 * HD :].astype(F32)).astype(BF16)


def join_kernel(scale, ids, own, by_c, by_yl, by_both, gains, grad_key, grad_value, grad_gain):
    yl, c, x = ids[1], ids[2], ids[4]
    for ref, at in ((own, 2 * yl + c), (by_c, 2 * yl + 1 - c), (by_yl, 2 - 2 * yl + c), (by_both, 3 - 2 * yl - c)):
        rows = pl.ds(pl.multiple_of(at * PIECE, PIECE), PIECE)
        grad_key[rows] = ref[:PIECE].astype(F32) * scale
        grad_value[rows] = ref[PIECE:].astype(F32) * scale
    for s in range(NX):
        at = (x + s) % NX
        for j in range(4):
            grad_gain[(1 - at % 2) * 8 + 2 * j + at // 2] = gains[4 * s + j : 4 * s + j + 1] * scale


def local(tokens, gain, w_query, w_key, w_value, w_out, cotangent):
    rows, quarter = tokens.shape
    sub = quarter // NX
    width = quarter * 4
    yh, x, z, yl, c = (lax.axis_index(a) for a in AXES)
    ids = jnp.stack([z, yl, c, yh, x]).astype(jnp.int32)
    head = yl * 2 + c
    loss_scale = 1.0 / math.sqrt(rows * 64)

    pack = jnp.concatenate(
        [
            w_query,
            w_out,
            lax.dynamic_slice_in_dim(w_key, head * PIECE, PIECE, 0),
            lax.dynamic_slice_in_dim(w_value, head * PIECE, PIECE, 0),
        ],
        axis=0,
    )
    same = lax.ppermute(pack, AXES, owner_perm(0))
    other = lax.ppermute(pack, AXES, owner_perm(1))
    part_shape = ((2 * rows + GROWS, sub), BF16)
    total, *parts = call(spread_kernel, [((1, rows), F32)] + [part_shape] * 4, [], ids, tokens, cotangent)
    total = total + swap(total, "c")
    same, other, total = lax.optimization_barrier((same, other, total))
    total = total + swap(total, "yl")
    both = jnp.where(yh == 0, jnp.concatenate([same, other]), jnp.concatenate([other, same]))
    prev2, next2 = shift_z(both, 2), shift_z(both, -2)
    double, half_shape = ((4 * BLOCK, HD), BF16), ((BLOCK, HD), BF16)
    relays = call(forward_pack_kernel, [double] * 2 + [half_shape] * 2, [], ids, both, prev2, next2)
    prev1, next1 = shift_z(relays[0], 1), shift_z(relays[1], -1)
    far_first, far_second = shift_z(relays[2], 2), shift_z(relays[3], -2)
    weights = (both, prev1, next1, prev2, next2, far_first, far_second)

    parts = call(stamp_kernel, [part_shape] * 4, [], ids, total, *parts, aliases={2 + s: s for s in range(4)})
    parts = [parts[0]] + [shift_x(parts[s], s) for s in range(1, NX)]
    gain_f = gain.astype(F32).reshape(1, quarter)
    unit_sw, normed_sw, cot_sw = call(
        normalize_kernel,
        [((512, sub), F32), ((512, sub), BF16), ((512, sub), BF16)],
        [],
        ids,
        *parts,
        gain_f,
        static=width,
    )

    *theirs, w_all, w_heads = call(
        theirs_kernel,
        [((rows, 5 * HD), F32)] * 4 + [((sub, 6 * HD), BF16), ((2, 2 * HD, sub), BF16)],
        [],
        ids,
        *weights,
        normed_sw,
        cot_sw,
    )
    got = [None] + [swap(theirs[s], "c") for s in range(1, NX)]
    got[0] = swap(theirs[0], "c")
    mine = call(
        mine_kernel,
        [((rows, 5 * HD), F32)] * 4,
        [],
        ids,
        normed_sw,
        cot_sw,
        w_all,
        w_heads,
    )
    split = ((rows, 8 * HD), BF16)
    chunks = [shift_x(call(chunk_kernel, [split], [], ids, mine[s], got[s])[0], -s) for s in range(1, NX)]
    own, normed_t = call(
        own_kernel, [((rows, 5 * HD), F32), ((sub, 512), BF16)], [], ids, mine[0], got[0], normed_sw
    )
    (partial,) = call(sum_kernel, [split], [], ids, own, *chunks)
    qa, kv = call(final_kernel, [((rows, 4 * HD), BF16), ((rows, HD), BF16)], [], ids, partial, swap(partial, "yl"))
    heads, row_sum = call(
        attend_kernel, [((rows, 6 * HD), BF16), ((1, rows), F32)], [], ids, qa, kv, swap(kv, "c")
    )
    row_sum = row_sum + swap(row_sum, "c")
    heads = [heads] + [shift_x(heads, s) for s in range(1, NX)]

    g, n = GROWS, BLOCK
    up, down, t4a, t4b, *back, gain_own, d_heads, attended_t, shared_terms = call(
        gradient_kernel,
        [((g + 4 * n, HD), BF16)] * 2
        + [((g + n, HD), BF16)] * 2
        + [((rows + g, sub), BF16)] * 4
        + [((g, HD), BF16), ((512, 6 * HD), BF16), ((4 * HD, 512), BF16), ((sub, 2 * HD), F32)],
        [],
        ids,
        *heads,
        *[swap(h, "c") for h in heads],
        normed_t,
        cot_sw,
        unit_sw,
        w_all,
    )
    t0, t2, m2 = call(
        near_kernel, [((2 * n, HD), BF16)] * 3, [], ids, normed_t, cot_sw, d_heads, attended_t, shared_terms
    )
    c4, d4 = shift_z(t4a, 2), shift_z(t4b, -2)
    a, b = shift_z(up, 1), shift_z(down, -1)
    a, row_sum = lax.optimization_barrier((a, row_sum))
    up, down, *back = call(
        relay_kernel,
        [((2 * n, HD), BF16)] * 2 + [((rows + g, sub), BF16)] * 4,
        [],
        ids,
        t2,
        m2,
        a,
        b,
        c4,
        d4,
        gain_own,
        *back,
        aliases={8 + s: 2 + s for s in range(NX)},
    )
    up, down = shift_z(up, 2), shift_z(down, -2)

    pieces = [back[0]] + [shift_x(back[s], -s) for s in range(1, NX)]
    to_same, to_other = call(finish_kernel, [((n, HD), BF16)] * 2, [], ids, t0, a, b, up, down)
    arrived = (lax.ppermute(to_same, AXES, inverse(owner_perm(0))), lax.ppermute(to_other, AXES, inverse(owner_perm(1))))
    (gain_z,) = call(gain_kernel, [((8 * NX, HD), F32)], [], ids, *pieces)
    gain_z = gain_z + swap(gain_z, "yh")
    (grad_input,) = call(
        input_kernel,
        [((rows, quarter), F32)],
        [],
        ids,
        *pieces,
        tokens,
        gain_f,
        total,
        row_sum,
        static=width,
    )
    *arrived, grad_input, gain_z = lax.optimization_barrier((*arrived, grad_input, gain_z))
    (shared_own,) = call(shared_kernel, [((2 * PIECE, HD), BF16)], [], ids, *arrived)
    grad_query, grad_out = call(owner_kernel, [((HD, HD), F32)] * 2, [], ids, *arrived, static=loss_scale)
    shared_yl = swap(shared_own, "yl")
    gain_z = gain_z[: 4 * NX] + shift_z(gain_z[4 * NX :], 4)
    grad_key, grad_value, grad_gain = call(
        join_kernel,
        [((rows, HD), F32)] * 2 + [((4 * NX, 1, HD), F32)],
        [],
        ids,
        shared_own,
        swap(shared_own, "c"),
        shared_yl,
        swap(shared_yl, "c"),
        gain_z,
        static=loss_scale,
    )
    grad_gain = grad_gain.reshape(quarter)
    return (grad_input, grad_gain, grad_query, grad_key, grad_value, grad_out)


def solution(mesh):
    fine = Mesh(mesh.devices.reshape(2, NX, NZ, 2, 2), AXES)
    in_specs = (P(FSDP, TP), P(TP), P(FSDP, TP), P(FSDP, None), P(FSDP, None), P(TP, FSDP), P(FSDP, TP))
    out_specs = (P(FSDP, TP), P(TP), P(FSDP, TP), P(FSDP, None), P(FSDP, None), P(TP, FSDP))
    return jax.shard_map(local, mesh=fine, in_specs=in_specs, out_specs=out_specs, check_vma=False)
```

```python
import functools
import math

import jax
import jax.numpy as jnp
from jax import lax
from jax.experimental import pallas as pl
from jax.experimental.pallas import tpu as pltpu
from jax.sharding import Mesh, PartitionSpec as P

HD = 128
NX = 4
NZ = 8
AXES = ("yh", "x", "z", "yl", "c")
FSDP = ("yh", "x", "z")
TP = ("yl", "c")
F32 = jnp.float32
BF16 = jnp.bfloat16
PIECE = 32
BLOCK = 2 * HD + 2 * PIECE
GROWS = 16
VMEM = pl.BlockSpec(memory_space=pltpu.VMEM)
SMEM = pl.BlockSpec(memory_space=pltpu.SMEM)


def flat(yh, x, z, yl, c):
    return (((yh * NX + x) * NZ + z) * 2 + yl) * 2 + c


def owner_perm(flip):
    pairs = []
    for yh in range(2):
        for x in range(NX):
            for z in range(NZ):
                for yl in range(2):
                    for c in range(2):
                        dest_x = (z % 2) * 2 + 1 - x % 2
                        dest_z = (z // 2) * 2 + c
                        pairs.append((flat(yh, x, z, yl, c), flat(yl ^ flip, dest_x, dest_z, yh, x // 2)))
    return pairs


def inverse(pairs):
    return [(d, s) for s, d in pairs]


def shift_x(value, by):
    return lax.ppermute(value, "x", [(i, (i + by) % NX) for i in range(NX)])


def shift_z(value, by):
    return lax.ppermute(value, "z", [(i, (i + by) % NZ) for i in range(NZ)])


def swap(value, axis):
    return lax.ppermute(value, axis, [(0, 1), (1, 0)])


def dot(a, b, ca, cb):
    return lax.dot_general(a, b, (((ca,), (cb,)), ((), ())), preferred_element_type=F32)


def lanes(start, size=HD):
    return pl.ds(pl.multiple_of(start, HD), size)


def feature(at, j):
    return ((1 - at % 2) * 8 + 2 * j + at // 2) * HD


def call(body, outs, scratch, ids, *args, static=None, aliases={}):
    body = body if static is None else functools.partial(body, static)
    return pl.pallas_call(
        body,
        out_shape=[jax.ShapeDtypeStruct(s, d) for s, d in outs],
        in_specs=[SMEM] + [VMEM] * len(args),
        out_specs=[VMEM] * len(outs),
        input_output_aliases=aliases,
        scratch_shapes=[pltpu.VMEM(s, d) for s, d in scratch],
        compiler_params=pltpu.CompilerParams(vmem_limit_bytes=16 * 2**20),
    )(ids, *args)


def spread_kernel(ids, tokens, cot, total_out, *outs):
    rows = tokens.shape[0]
    squares = jnp.zeros((rows, HD), F32)
    for s in range(NX):
        at = (ids[4] + s) % NX

        def cut(j, squares, s=s, at=at):
            block, cols = lanes(feature(at, j)), lanes(j * HD)
            value = tokens[:, block]
            outs[s][:rows, cols] = value
            outs[s][rows : 2 * rows, cols] = cot[:, block]
            return squares + value.astype(F32) * value.astype(F32)

        squares = lax.fori_loop(0, 4, cut, squares)
    total_out[...] = jnp.sum(jnp.transpose(squares), axis=0, keepdims=True)


def stamp_kernel(ids, total, *refs):
    total = total[...]
    high = total.astype(BF16).astype(F32)
    middle = (total - high).astype(BF16).astype(F32)
    extra = jnp.concatenate([high, middle, total - high - middle, jnp.zeros((GROWS - 3, HD), F32)], axis=0)
    extra = jnp.concatenate([extra] * 4, axis=1).astype(BF16)
    for out in refs[NX:]:
        out[2 * HD :] = extra


def normalize_kernel(width, ids, *refs):
    parts, (gain, unit, normed, cot) = refs[:4], refs[4:]
    for s in range(NX):
        rows = slice(s * HD, (s + 1) * HD)
        terms = parts[s][2 * HD :, :HD].astype(F32)
        total = (terms[2:3] + terms[1:2]) + terms[0:1]
        column = jnp.transpose(jnp.broadcast_to(total, (HD, HD)))
        inv = lax.rsqrt(column / width + 1e-05)

        @pl.loop(0, 4)
        def scale(j, s=s, rows=rows, inv=inv):
            cols = lanes(j * HD)
            value = parts[s][:HD, cols].astype(F32) * inv
            unit[rows, cols] = value
            normed[rows, cols] = (value * gain[:, lanes(feature(ids[4], j))]).astype(BF16)

        cot[rows] = parts[s][HD : 2 * HD]


def forward_pack_kernel(ids, both, prev, after, up, down, far_first, far_second):
    for out, ref in ((up, prev), (down, after)):
        out[: 2 * BLOCK] = both[...]
        out[2 * BLOCK :] = ref[...]
    far_first[...] = prev[:BLOCK]
    far_second[...] = after[BLOCK:]


def product(outs, side, normed, cot, w_all, w_out):
    w_q = w_all[:, lanes(side * 2 * HD, 2 * HD)]
    w_kv = w_all[:, lanes((4 + side) * HD)]
    w_o = w_out[side]
    for r in range(0, 512, 256):
        rows = slice(r, r + 256)
        query = dot(normed[rows], w_q, 1, 0)
        attn_grad = dot(cot[rows], w_o, 1, 1)
        shared = dot(normed[rows], w_kv, 1, 0)
        for half in range(2):
            out, part = outs[r // HD + half], slice(half * HD, (half + 1) * HD)
            out[:, : 2 * HD] = query[part]
            out[:, 2 * HD : 4 * HD] = attn_grad[part]
            out[:, 4 * HD :] = shared[part]


def theirs_kernel(ids, both, prev1, next1, prev2, next2, far_first, far_second, normed, cot, *refs):
    outs, w_all, w_out = refs[:NX], refs[NX], refs[NX + 1]
    z, c = ids[0], ids[2]

    def place(ref, base, d, half):
        zt = (z + d + NZ) % NZ
        side, j = zt % 2, zt // 2

        def block(start, size, unit=PIECE):
            return pl.ds(pl.multiple_of(start, unit), size)

        w_all[block(j * HD, HD), lanes(side * 2 * HD + half * HD)] = ref[block(base, HD)]
        w_out[side, block(half * HD, HD, HD), lanes(j * HD)] = ref[block(base + HD, HD)]
        part = block(j * HD + (2 * half + side) * PIECE, PIECE)
        w_all[part, 4 * HD : 5 * HD] = ref[block(base + 2 * HD, PIECE)]
        w_all[part, 5 * HD : 6 * HD] = ref[block(base + 2 * HD + PIECE, PIECE)]

    for ref, base, d in (
        (both, 0, 0),
        (prev1, 0, -1),
        (prev1, 2 * BLOCK, -3),
        (next1, 0, 1),
        (next1, 2 * BLOCK, 3),
        (prev2, 0, -2),
        (next2, 0, 2),
    ):


        @pl.loop(0, 2)
        def both_halves(half, ref=ref, base=base, d=d):
            place(ref, base + half * BLOCK, d, half)

    place(far_first, 0, 4, 0)
    place(far_second, 0, 4, 1)
    product(outs, 1 - c, normed, cot, w_all, w_out)


def mine_kernel(ids, normed, cot, w_all, w_out, *refs):
    outs, normed_t = refs[:NX], refs[NX]
    product(outs, ids[2], normed, cot, w_all, w_out)
    for s in range(NX):
        for j in range(4):
            rows, cols = slice(s * HD, (s + 1) * HD), slice(j * HD, (j + 1) * HD)
            normed_t[cols, rows] = jnp.transpose(normed[rows, cols])


def split_store(ref, total):
    for start, size, at in ((0, 2 * HD, 0), (4 * HD, HD, 6 * HD)):
        value = total[:, start : start + size]
        high = value.astype(BF16)
        ref[:, at : at + size] = high
        ref[:, at + size : at + 2 * size] = (value - high.astype(F32)).astype(BF16)
    ref[:, 4 * HD : 6 * HD] = total[:, 2 * HD : 4 * HD].astype(BF16)


def joined(ref):
    value = ref[...].astype(F32)
    return jnp.concatenate(
        [
            value[:, : 2 * HD] + value[:, 2 * HD : 4 * HD],
            value[:, 4 * HD : 6 * HD],
            value[:, 6 * HD : 7 * HD] + value[:, 7 * HD :],
        ],
        axis=1,
    )


def chunk_kernel(ids, mine, got, out):
    split_store(out, mine[...] + got[...])


def own_kernel(ids, mine, got, out):
    out[...] = mine[...] + got[...]


def sum_kernel(ids, own, a, b, c, out):
    split_store(out, own[...] + joined(a) + joined(b) + joined(c))


def final_kernel(ids, mine, got, qa, kv):
    total = (joined(mine) + joined(got)).astype(BF16)
    qa[...] = total[:, : 4 * HD]
    kv[...] = total[:, 4 * HD :]


def attend_kernel(ids, qa, kv_mine, kv_theirs, out, row_out):
    first = ids[2] == 0
    mine, theirs = kv_mine[...].astype(F32), kv_theirs[...].astype(F32)
    key_rows = jnp.where(first, mine, theirs).astype(BF16)
    value_rows = jnp.where(first, theirs, mine).astype(BF16)
    causal = lax.broadcasted_iota(jnp.int32, (HD, HD), 0) >= lax.broadcasted_iota(jnp.int32, (HD, HD), 1)
    keys = jnp.zeros((HD, HD), F32)
    values = jnp.zeros((HD, HD), F32)
    row_terms = jnp.zeros((HD, HD), F32)
    for h in range(2):
        query = qa[:, h * HD : (h + 1) * HD]
        attn_grad = qa[:, (2 + h) * HD : (3 + h) * HD]
        scores = dot(query, key_rows, 1, 1) * HD ** (-0.5)
        scores = jnp.where(causal, scores, jnp.float32(-1e30))
        shifted = jnp.exp(scores - jnp.max(scores, axis=-1, keepdims=True))
        softmax_out = shifted / jnp.sum(shifted, axis=-1, keepdims=True)
        rounded = softmax_out.astype(BF16)
        dprob = dot(attn_grad, value_rows, 1, 1)
        dscore = softmax_out * (dprob - jnp.sum(dprob * softmax_out, axis=-1, keepdims=True)) * HD ** (-0.5)
        dscore = dscore.astype(BF16)
        d_query = dot(dscore, key_rows, 1, 0).astype(BF16)
        out[:, h * HD : (h + 1) * HD] = d_query
        row_terms = row_terms + d_query.astype(F32) * query.astype(F32)
        out[:, (2 + h) * HD : (3 + h) * HD] = dot(rounded, value_rows, 1, 0).astype(BF16)
        keys = keys + dot(dscore, query, 0, 0).astype(BF16).astype(F32)
        values = values + dot(rounded, attn_grad, 0, 0).astype(BF16).astype(F32)
    out[:, 4 * HD : 5 * HD] = keys.astype(BF16)
    out[:, 5 * HD :] = values.astype(BF16)
    row_terms = row_terms + keys * key_rows.astype(F32) + values * value_rows.astype(F32)
    row_out[...] = jnp.sum(jnp.transpose(row_terms), axis=0, keepdims=True)


def gradient_kernel(ids, *refs):
    mine, theirs, (normed_t, cot, unit, w_all) = refs[:4], refs[4:8], refs[8:12]
    (up, down, t4a, t4b), back, (gain_out, heads, attended, shared) = refs[12:16], refs[16:20], refs[20:]
    c = ids[2]
    for s in range(NX):
        rows = slice(s * HD, (s + 1) * HD)
        for ref, side in ((mine[s], c), (theirs[s], 1 - c)):
            heads[rows, lanes(side * 2 * HD, 2 * HD)] = ref[:, : 2 * HD]
            for half in range(2):
                at = pl.ds(pl.multiple_of((2 * side + half) * HD, HD), HD)
                attended[at, rows] = jnp.transpose(ref[:, (2 + half) * HD : (3 + half) * HD])
        total = mine[s][:, 4 * HD :].astype(F32) + theirs[s][:, 4 * HD :].astype(F32)
        heads[rows, 4 * HD :] = total.astype(BF16)

    gain_sum = jnp.zeros((1, 4 * HD), F32)
    for s in range(NX):
        rows = slice(s * HD, (s + 1) * HD)
        term = dot(heads[rows], w_all[...], 1, 1)
        back[s][:HD] = term.astype(BF16)
        gain_sum = gain_sum + jnp.sum(term * unit[rows], axis=0, keepdims=True)
    gain_rows = jnp.concatenate([gain_sum[:, j * HD : (j + 1) * HD] for j in range(4)], axis=0)
    high = gain_rows.astype(BF16).astype(F32)
    gain_rows = jnp.concatenate([high, gain_rows - high, jnp.zeros((8, HD), F32)], axis=0).astype(BF16)

    shared[...] = dot(normed_t[...], heads[:, 4 * HD :], 1, 0)
    g, n = GROWS, BLOCK
    for ref in (up, down, t4a, t4b):
        ref[:g] = gain_rows
    terms(
        ids,
        normed_t,
        cot,
        heads,
        attended,
        shared,
        (
            (1, up.at[g : g + n], up.at[g + n : g + 2 * n]),
            (3, up.at[g + 2 * n : g + 3 * n], up.at[g + 3 * n :]),
            (-1, down.at[g : g + n], down.at[g + n : g + 2 * n]),
            (-3, down.at[g + 2 * n : g + 3 * n], down.at[g + 3 * n :]),
            (4, t4a.at[g:], t4b.at[g:]),
        ),
    )
    gain_out[...] = gain_rows


def terms(ids, normed_t, cot, heads, attended, shared, places):
    z = ids[0]
    for d, out_first, out_second in places:
        zt = (z + d + NZ) % NZ
        side, j = zt % 2, zt // 2
        rows = pl.ds(pl.multiple_of(j * HD, HD), HD)
        g_q = dot(normed_t[rows], heads[:, lanes(side * 2 * HD, 2 * HD)], 1, 0).astype(BF16)
        rows = pl.ds(pl.multiple_of(side * 2 * HD, 2 * HD), 2 * HD)
        g_o = dot(attended[rows], cot[:, lanes(j * HD)], 1, 0).astype(BF16)
        for half, out in enumerate((out_first, out_second)):
            out[:HD] = g_q[:, half * HD : (half + 1) * HD]
            out[HD : 2 * HD] = g_o[half * HD : (half + 1) * HD]
            part = shared[pl.ds(pl.multiple_of(j * HD + (2 * half + side) * PIECE, PIECE), PIECE), :].astype(BF16)
            out[2 * HD : 2 * HD + PIECE] = part[:, :HD]
            out[2 * HD + PIECE :] = part[:, HD:]


def near_kernel(ids, normed_t, cot, heads, attended, shared, t0, t2, m2):
    n = BLOCK
    terms(ids, normed_t, cot, heads, attended, shared, [(d, r.at[:n], r.at[n:]) for d, r in ((0, t0), (2, t2), (-2, m2))])


def relay_kernel(ids, t2, m2, a, b, c, d, gain_own, *refs):
    up, down, *back = refs[NX:]
    g, n = GROWS, BLOCK
    total = t2[...].astype(F32) + a[g + 2 * n :].astype(F32)
    up[:n] = (total[:n] + c[g:].astype(F32)).astype(BF16)
    up[n:] = total[n:].astype(BF16)
    total = m2[...].astype(F32) + b[g + 2 * n :].astype(F32)
    down[:n] = total[:n].astype(BF16)
    down[n:] = (total[n:] + d[g:].astype(F32)).astype(BF16)
    three = gain_own[...].astype(F32) + a[:g].astype(F32) + b[:g].astype(F32)
    five = three + c[:g].astype(F32) + d[:g].astype(F32)
    terms = []
    for rows in (five, three):
        value = rows[:4] + rows[4:8]
        high = value.astype(BF16).astype(F32)
        terms += [high, value - high]
    for j in range(4):
        rows = jnp.concatenate([t[j : j + 1] for t in terms] + [jnp.zeros((g - 4, HD), F32)], axis=0).astype(BF16)
        for ref in back:
            ref[HD:, j * HD : (j + 1) * HD] = rows


def finish_kernel(ids, t0, a, b, up, down, same, other):
    g, n = GROWS, BLOCK
    flip = ids[3]
    near = slice(g, g + 2 * n)
    total = t0[...].astype(F32) + a[near].astype(F32) + b[near].astype(F32)
    total = total + up[...].astype(F32) + down[...].astype(F32)
    same[...] = jnp.where(flip == 0, total[:n], total[n:]).astype(BF16)
    other[...] = jnp.where(flip == 0, total[n:], total[:n]).astype(BF16)


def gain_kernel(ids, *refs):
    out = refs[NX]
    for s in range(NX):
        rows = refs[s][HD:].astype(F32)
        for at in (0, 2):
            value = rows[at : at + 1] + rows[at + 1 : at + 2]
            for j in range(4):
                row = 2 * NX * at + 4 * s + j
                out[row : row + 1] = value[:, j * HD : (j + 1) * HD]


def input_kernel(width, ids, a, b, c, d, tokens, gain, total, row_sum, out):
    inv = lax.rsqrt(jnp.transpose(jnp.broadcast_to(total[...], (HD, HD))) / width + 1e-05)
    row_mean = jnp.transpose(jnp.broadcast_to(row_sum[...], (HD, HD))) / width
    for s, ref in enumerate((a, b, c, d)):
        at = (ids[4] + s) % NX

        @pl.loop(0, 4)
        def place(j, ref=ref, at=at):
            cols = lanes(feature(at, j))
            unit = tokens[:, cols].astype(F32) * inv
            scaled = ref[:HD, lanes(j * HD)].astype(F32) * gain[:, cols]
            out[:, cols] = inv * (scaled - unit * row_mean)


def owner_kernel(scale, ids, same, other, grad_query, grad_out):
    for grad, at in ((grad_query, slice(0, HD)), (grad_out, slice(HD, 2 * HD))):
        grad[...] = (same[at].astype(F32) + other[at].astype(F32)) * scale


def shared_kernel(ids, a, b, shared):
    shared[...] = (a[2 * HD :].astype(F32) + b[2 * HD :].astype(F32)).astype(BF16)


def join_kernel(scale, ids, own, by_c, by_yl, by_both, gains, grad_key, grad_value, grad_gain):
    yl, c, x = ids[1], ids[2], ids[4]
    for ref, at in ((own, 2 * yl + c), (by_c, 2 * yl + 1 - c), (by_yl, 2 - 2 * yl + c), (by_both, 3 - 2 * yl - c)):
        rows = pl.ds(pl.multiple_of(at * PIECE, PIECE), PIECE)
        grad_key[rows] = ref[:PIECE].astype(F32) * scale
        grad_value[rows] = ref[PIECE:].astype(F32) * scale
    for s in range(NX):
        at = (x + s) % NX
        for j in range(4):
            grad_gain[(1 - at % 2) * 8 + 2 * j + at // 2] = gains[4 * s + j : 4 * s + j + 1] * scale


def local(tokens, gain, w_query, w_key, w_value, w_out, cotangent):
    rows, quarter = tokens.shape
    sub = quarter // NX
    width = quarter * 4
    yh, x, z, yl, c = (lax.axis_index(a) for a in AXES)
    ids = jnp.stack([z, yl, c, yh, x]).astype(jnp.int32)
    head = yl * 2 + c
    loss_scale = 1.0 / math.sqrt(rows * 64)

    pack = jnp.concatenate(
        [
            w_query,
            w_out,
            lax.dynamic_slice_in_dim(w_key, head * PIECE, PIECE, 0),
            lax.dynamic_slice_in_dim(w_value, head * PIECE, PIECE, 0),
        ],
        axis=0,
    )
    same = lax.ppermute(pack, AXES, owner_perm(0))
    other = lax.ppermute(pack, AXES, owner_perm(1))
    part_shape = ((2 * rows + GROWS, sub), BF16)
    total, *parts = call(spread_kernel, [((1, rows), F32)] + [part_shape] * 4, [], ids, tokens, cotangent)
    total = total + swap(total, "c")
    same, other, total = lax.optimization_barrier((same, other, total))
    total = total + swap(total, "yl")
    both = jnp.where(yh == 0, jnp.concatenate([same, other]), jnp.concatenate([other, same]))
    prev2, next2 = shift_z(both, 2), shift_z(both, -2)
    double, half_shape = ((4 * BLOCK, HD), BF16), ((BLOCK, HD), BF16)
    relays = call(forward_pack_kernel, [double] * 2 + [half_shape] * 2, [], ids, both, prev2, next2)
    prev1, next1 = shift_z(relays[0], 1), shift_z(relays[1], -1)
    far_first, far_second = shift_z(relays[2], 2), shift_z(relays[3], -2)
    weights = (both, prev1, next1, prev2, next2, far_first, far_second)

    parts = call(stamp_kernel, [part_shape] * 4, [], ids, total, *parts, aliases={2 + s: s for s in range(4)})
    parts = [parts[0]] + [shift_x(parts[s], s) for s in range(1, NX)]
    gain_f = gain.astype(F32).reshape(1, quarter)
    unit_sw, normed_sw, cot_sw = call(
        normalize_kernel,
        [((512, sub), F32), ((512, sub), BF16), ((512, sub), BF16)],
        [],
        ids,
        *parts,
        gain_f,
        static=width,
    )

    *theirs, w_all, w_heads = call(
        theirs_kernel,
        [((rows, 5 * HD), F32)] * 4 + [((sub, 6 * HD), BF16), ((2, 2 * HD, sub), BF16)],
        [],
        ids,
        *weights,
        normed_sw,
        cot_sw,
    )
    got = [None] + [swap(theirs[s], "c") for s in range(1, NX)]
    got[0] = swap(theirs[0], "c")
    *mine, normed_t = call(
        mine_kernel,
        [((rows, 5 * HD), F32)] * 4 + [((sub, 512), BF16)],
        [],
        ids,
        normed_sw,
        cot_sw,
        w_all,
        w_heads,
    )
    split = ((rows, 8 * HD), BF16)
    chunks = [shift_x(call(chunk_kernel, [split], [], ids, mine[s], got[s])[0], -s) for s in range(1, NX)]
    (own,) = call(own_kernel, [((rows, 5 * HD), F32)], [], ids, mine[0], got[0])
    (partial,) = call(sum_kernel, [split], [], ids, own, *chunks)
    qa, kv = call(final_kernel, [((rows, 4 * HD), BF16), ((rows, HD), BF16)], [], ids, partial, swap(partial, "yl"))
    heads, row_sum = call(
        attend_kernel, [((rows, 6 * HD), BF16), ((1, rows), F32)], [], ids, qa, kv, swap(kv, "c")
    )
    row_sum = row_sum + swap(row_sum, "c")
    heads = [heads] + [shift_x(heads, s) for s in range(1, NX)]

    g, n = GROWS, BLOCK
    up, down, t4a, t4b, *back, gain_own, d_heads, attended_t, shared_terms = call(
        gradient_kernel,
        [((g + 4 * n, HD), BF16)] * 2
        + [((g + n, HD), BF16)] * 2
        + [((rows + g, sub), BF16)] * 4
        + [((g, HD), BF16), ((512, 6 * HD), BF16), ((4 * HD, 512), BF16), ((sub, 2 * HD), F32)],
        [],
        ids,
        *heads,
        *[swap(h, "c") for h in heads],
        normed_t,
        cot_sw,
        unit_sw,
        w_all,
    )
    t0, t2, m2 = call(
        near_kernel, [((2 * n, HD), BF16)] * 3, [], ids, normed_t, cot_sw, d_heads, attended_t, shared_terms
    )
    c4, d4 = shift_z(t4a, 2), shift_z(t4b, -2)
    a, b = shift_z(up, 1), shift_z(down, -1)
    a, row_sum = lax.optimization_barrier((a, row_sum))
    up, down, *back = call(
        relay_kernel,
        [((2 * n, HD), BF16)] * 2 + [((rows + g, sub), BF16)] * 4,
        [],
        ids,
        t2,
        m2,
        a,
        b,
        c4,
        d4,
        gain_own,
        *back,
        aliases={8 + s: 2 + s for s in range(NX)},
    )
    up, down = shift_z(up, 2), shift_z(down, -2)

    pieces = [back[0]] + [shift_x(back[s], -s) for s in range(1, NX)]
    to_same, to_other = call(finish_kernel, [((n, HD), BF16)] * 2, [], ids, t0, a, b, up, down)
    arrived = (lax.ppermute(to_same, AXES, inverse(owner_perm(0))), lax.ppermute(to_other, AXES, inverse(owner_perm(1))))
    (gain_z,) = call(gain_kernel, [((8 * NX, HD), F32)], [], ids, *pieces)
    gain_z = gain_z + swap(gain_z, "yh")
    (grad_input,) = call(
        input_kernel,
        [((rows, quarter), F32)],
        [],
        ids,
        *pieces,
        tokens,
        gain_f,
        total,
        row_sum,
        static=width,
    )
    *arrived, grad_input, gain_z = lax.optimization_barrier((*arrived, grad_input, gain_z))
    (shared_own,) = call(shared_kernel, [((2 * PIECE, HD), BF16)], [], ids, *arrived)
    grad_query, grad_out = call(owner_kernel, [((HD, HD), F32)] * 2, [], ids, *arrived, static=loss_scale)
    shared_yl = swap(shared_own, "yl")
    gain_z = gain_z[: 4 * NX] + shift_z(gain_z[4 * NX :], 4)
    grad_key, grad_value, grad_gain = call(
        join_kernel,
        [((rows, HD), F32)] * 2 + [((4 * NX, 1, HD), F32)],
        [],
        ids,
        shared_own,
        swap(shared_own, "c"),
        shared_yl,
        swap(shared_yl, "c"),
        gain_z,
        static=loss_scale,
    )
    grad_gain = grad_gain.reshape(quarter)
    return (grad_input, grad_gain, grad_query, grad_key, grad_value, grad_out)


def solution(mesh):
    fine = Mesh(mesh.devices.reshape(2, NX, NZ, 2, 2), AXES)
    in_specs = (P(FSDP, TP), P(TP), P(FSDP, TP), P(FSDP, None), P(FSDP, None), P(TP, FSDP), P(FSDP, TP))
    out_specs = (P(FSDP, TP), P(TP), P(FSDP, TP), P(FSDP, None), P(FSDP, None), P(TP, FSDP))
    return jax.shard_map(local, mesh=fine, in_specs=in_specs, out_specs=out_specs, check_vma=False)
```

```python
import functools
import math

import jax
import jax.numpy as jnp
from jax import lax
from jax.experimental import pallas as pl
from jax.experimental.pallas import tpu as pltpu
from jax.sharding import Mesh, PartitionSpec as P

HD = 128
NX = 4
NZ = 8
AXES = ("yh", "x", "z", "yl", "c")
FSDP = ("yh", "x", "z")
TP = ("yl", "c")
F32 = jnp.float32
BF16 = jnp.bfloat16
PIECE = 32
BLOCK = 2 * HD + 2 * PIECE
GROWS = 16
VMEM = pl.BlockSpec(memory_space=pltpu.VMEM)
SMEM = pl.BlockSpec(memory_space=pltpu.SMEM)


def flat(yh, x, z, yl, c):
    return (((yh * NX + x) * NZ + z) * 2 + yl) * 2 + c


def owner_perm(flip):
    pairs = []
    for yh in range(2):
        for x in range(NX):
            for z in range(NZ):
                for yl in range(2):
                    for c in range(2):
                        dest_x = (z % 2) * 2 + 1 - x % 2
                        dest_z = (z // 2) * 2 + c
                        pairs.append((flat(yh, x, z, yl, c), flat(yl ^ flip, dest_x, dest_z, yh, x // 2)))
    return pairs


def inverse(pairs):
    return [(d, s) for s, d in pairs]


def shift_x(value, by):
    return lax.ppermute(value, "x", [(i, (i + by) % NX) for i in range(NX)])


def shift_z(value, by):
    return lax.ppermute(value, "z", [(i, (i + by) % NZ) for i in range(NZ)])


def swap(value, axis):
    return lax.ppermute(value, axis, [(0, 1), (1, 0)])


def dot(a, b, ca, cb):
    return lax.dot_general(a, b, (((ca,), (cb,)), ((), ())), preferred_element_type=F32)


def lanes(start, size=HD):
    return pl.ds(pl.multiple_of(start, HD), size)


def feature(at, j):
    return ((1 - at % 2) * 8 + 2 * j + at // 2) * HD


def call(body, outs, scratch, ids, *args, static=None, aliases={}):
    body = body if static is None else functools.partial(body, static)
    return pl.pallas_call(
        body,
        out_shape=[jax.ShapeDtypeStruct(s, d) for s, d in outs],
        in_specs=[SMEM] + [VMEM] * len(args),
        out_specs=[VMEM] * len(outs),
        input_output_aliases=aliases,
        scratch_shapes=[pltpu.VMEM(s, d) for s, d in scratch],
        compiler_params=pltpu.CompilerParams(vmem_limit_bytes=16 * 2**20),
    )(ids, *args)


def spread_kernel(ids, tokens, cot, total_out, *outs):
    rows = tokens.shape[0]
    squares = jnp.zeros((rows, HD), F32)
    for s in range(NX):
        at = (ids[4] + s) % NX

        def cut(j, squares, s=s, at=at):
            block, cols = lanes(feature(at, j)), lanes(j * HD)
            value = tokens[:, block]
            outs[s][:rows, cols] = value
            outs[s][rows : 2 * rows, cols] = cot[:, block]
            return squares + value.astype(F32) * value.astype(F32)

        squares = lax.fori_loop(0, 4, cut, squares)
    total_out[...] = jnp.sum(jnp.transpose(squares), axis=0, keepdims=True)


def stamp_kernel(ids, total, *refs):
    total = total[...]
    high = total.astype(BF16).astype(F32)
    middle = (total - high).astype(BF16).astype(F32)
    extra = jnp.concatenate([high, middle, total - high - middle, jnp.zeros((GROWS - 3, HD), F32)], axis=0)
    extra = jnp.concatenate([extra] * 4, axis=1).astype(BF16)
    for out in refs[NX:]:
        out[2 * HD :] = extra


def normalize_kernel(width, ids, *refs):
    parts, (gain, unit, normed, cot) = refs[:4], refs[4:]
    for s in range(NX):
        rows = slice(s * HD, (s + 1) * HD)
        terms = parts[s][2 * HD :, :HD].astype(F32)
        total = (terms[2:3] + terms[1:2]) + terms[0:1]
        column = jnp.transpose(jnp.broadcast_to(total, (HD, HD)))
        inv = lax.rsqrt(column / width + 1e-05)

        @pl.loop(0, 4)
        def scale(j, s=s, rows=rows, inv=inv):
            cols = lanes(j * HD)
            value = parts[s][:HD, cols].astype(F32) * inv
            unit[rows, cols] = value
            normed[rows, cols] = (value * gain[:, lanes(feature(ids[4], j))]).astype(BF16)

        cot[rows] = parts[s][HD : 2 * HD]


def forward_pack_kernel(ids, both, prev, after, up, down, far_first, far_second):
    for out, ref in ((up, prev), (down, after)):
        out[: 2 * BLOCK] = both[...]
        out[2 * BLOCK :] = ref[...]
    far_first[...] = prev[:BLOCK]
    far_second[...] = after[BLOCK:]


def product(outs, side, normed, cot, w_all, w_out):
    w_q = w_all[:, lanes(side * 2 * HD, 2 * HD)]
    w_kv = w_all[:, lanes((4 + side) * HD)]
    w_o = w_out[side]
    for r in range(0, 512, 256):
        rows = slice(r, r + 256)
        query = dot(normed[rows], w_q, 1, 0)
        attn_grad = dot(cot[rows], w_o, 1, 1)
        shared = dot(normed[rows], w_kv, 1, 0)
        for half in range(2):
            out, part = outs[r // HD + half], slice(half * HD, (half + 1) * HD)
            out[:, : 2 * HD] = query[part]
            out[:, 2 * HD : 4 * HD] = attn_grad[part]
            out[:, 4 * HD :] = shared[part]


def theirs_kernel(ids, both, prev1, next1, prev2, next2, far_first, far_second, normed, cot, *refs):
    outs, w_all, w_out = refs[:NX], refs[NX], refs[NX + 1]
    z, c = ids[0], ids[2]

    def place(ref, base, d, half):
        zt = (z + d + NZ) % NZ
        side, j = zt % 2, zt // 2

        def block(start, size, unit=PIECE):
            return pl.ds(pl.multiple_of(start, unit), size)

        w_all[block(j * HD, HD), lanes(side * 2 * HD + half * HD)] = ref[block(base, HD)]
        w_out[side, block(half * HD, HD, HD), lanes(j * HD)] = ref[block(base + HD, HD)]
        part = block(j * HD + (2 * half + side) * PIECE, PIECE)
        w_all[part, 4 * HD : 5 * HD] = ref[block(base + 2 * HD, PIECE)]
        w_all[part, 5 * HD : 6 * HD] = ref[block(base + 2 * HD + PIECE, PIECE)]

    for ref, base, d in (
        (both, 0, 0),
        (prev1, 0, -1),
        (prev1, 2 * BLOCK, -3),
        (next1, 0, 1),
        (next1, 2 * BLOCK, 3),
        (prev2, 0, -2),
        (next2, 0, 2),
    ):


        @pl.loop(0, 2)
        def both_halves(half, ref=ref, base=base, d=d):
            place(ref, base + half * BLOCK, d, half)

    place(far_first, 0, 4, 0)
    place(far_second, 0, 4, 1)
    product(outs, 1 - c, normed, cot, w_all, w_out)


def mine_kernel(ids, normed, cot, w_all, w_out, *refs):
    outs, normed_t = refs[:NX], refs[NX]
    product(outs, ids[2], normed, cot, w_all, w_out)
    for s in range(NX):
        for j in range(4):
            rows, cols = slice(s * HD, (s + 1) * HD), slice(j * HD, (j + 1) * HD)
            normed_t[cols, rows] = jnp.transpose(normed[rows, cols])


def split_store(ref, total):
    for start, size, at in ((0, 2 * HD, 0), (4 * HD, HD, 6 * HD)):
        value = total[:, start : start + size]
        high = value.astype(BF16)
        ref[:, at : at + size] = high
        ref[:, at + size : at + 2 * size] = (value - high.astype(F32)).astype(BF16)
    ref[:, 4 * HD : 6 * HD] = total[:, 2 * HD : 4 * HD].astype(BF16)


def joined(ref):
    value = ref[...].astype(F32)
    return jnp.concatenate(
        [
            value[:, : 2 * HD] + value[:, 2 * HD : 4 * HD],
            value[:, 4 * HD : 6 * HD],
            value[:, 6 * HD : 7 * HD] + value[:, 7 * HD :],
        ],
        axis=1,
    )


def chunk_kernel(ids, mine, got, out):
    split_store(out, mine[...] + got[...])


def own_kernel(ids, mine, got, out):
    out[...] = mine[...] + got[...]


def sum_kernel(ids, own, a, b, c, out):
    split_store(out, own[...] + joined(a) + joined(b) + joined(c))


def final_kernel(ids, mine, got, qa, kv):
    total = (joined(mine) + joined(got)).astype(BF16)
    qa[...] = total[:, : 4 * HD]
    kv[...] = total[:, 4 * HD :]


def attend_kernel(ids, qa, kv_mine, kv_theirs, out, row_out):
    first = ids[2] == 0
    mine, theirs = kv_mine[...].astype(F32), kv_theirs[...].astype(F32)
    key_rows = jnp.where(first, mine, theirs).astype(BF16)
    value_rows = jnp.where(first, theirs, mine).astype(BF16)
    causal = lax.broadcasted_iota(jnp.int32, (HD, HD), 0) >= lax.broadcasted_iota(jnp.int32, (HD, HD), 1)
    keys = jnp.zeros((HD, HD), F32)
    values = jnp.zeros((HD, HD), F32)
    row_terms = jnp.zeros((HD, HD), F32)
    for h in range(2):
        query = qa[:, h * HD : (h + 1) * HD]
        attn_grad = qa[:, (2 + h) * HD : (3 + h) * HD]
        scores = dot(query, key_rows, 1, 1) * HD ** (-0.5)
        scores = jnp.where(causal, scores, jnp.float32(-1e30))
        shifted = jnp.exp(scores - jnp.max(scores, axis=-1, keepdims=True))
        softmax_out = shifted / jnp.sum(shifted, axis=-1, keepdims=True)
        rounded = softmax_out.astype(BF16)
        dprob = dot(attn_grad, value_rows, 1, 1)
        dscore = softmax_out * (dprob - jnp.sum(dprob * softmax_out, axis=-1, keepdims=True)) * HD ** (-0.5)
        dscore = dscore.astype(BF16)
        d_query = dot(dscore, key_rows, 1, 0).astype(BF16)
        out[:, h * HD : (h + 1) * HD] = d_query
        row_terms = row_terms + d_query.astype(F32) * query.astype(F32)
        out[:, (2 + h) * HD : (3 + h) * HD] = dot(rounded, value_rows, 1, 0).astype(BF16)
        keys = keys + dot(dscore, query, 0, 0).astype(BF16).astype(F32)
        values = values + dot(rounded, attn_grad, 0, 0).astype(BF16).astype(F32)
    out[:, 4 * HD : 5 * HD] = keys.astype(BF16)
    out[:, 5 * HD :] = values.astype(BF16)
    row_terms = row_terms + keys * key_rows.astype(F32) + values * value_rows.astype(F32)
    row_out[...] = jnp.sum(jnp.transpose(row_terms), axis=0, keepdims=True)


def gradient_kernel(ids, *refs):
    mine, theirs, (normed_t, cot, unit, w_all) = refs[:4], refs[4:8], refs[8:12]
    (up, down, t4a, t4b), back, (gain_out, heads, attended, shared) = refs[12:16], refs[16:20], refs[20:]
    c = ids[2]
    for s in range(NX):
        rows = slice(s * HD, (s + 1) * HD)
        for ref, side in ((mine[s], c), (theirs[s], 1 - c)):
            heads[rows, lanes(side * 2 * HD, 2 * HD)] = ref[:, : 2 * HD]
            for half in range(2):
                at = pl.ds(pl.multiple_of((2 * side + half) * HD, HD), HD)
                attended[at, rows] = jnp.transpose(ref[:, (2 + half) * HD : (3 + half) * HD])
        total = mine[s][:, 4 * HD :].astype(F32) + theirs[s][:, 4 * HD :].astype(F32)
        heads[rows, 4 * HD :] = total.astype(BF16)

    gain_sum = jnp.zeros((1, 4 * HD), F32)
    for s in range(NX):
        rows = slice(s * HD, (s + 1) * HD)
        term = dot(heads[rows], w_all[...], 1, 1)
        back[s][:HD] = term.astype(BF16)
        gain_sum = gain_sum + jnp.sum(term * unit[rows], axis=0, keepdims=True)
    gain_rows = jnp.concatenate([gain_sum[:, j * HD : (j + 1) * HD] for j in range(4)], axis=0)
    high = gain_rows.astype(BF16).astype(F32)
    gain_rows = jnp.concatenate([high, gain_rows - high, jnp.zeros((8, HD), F32)], axis=0).astype(BF16)

    shared[...] = dot(normed_t[...], heads[:, 4 * HD :], 1, 0)
    g, n = GROWS, BLOCK
    for ref in (up, down, t4a, t4b):
        ref[:g] = gain_rows
    terms(
        ids,
        normed_t,
        cot,
        heads,
        attended,
        shared,
        (
            (1, up.at[g : g + n], up.at[g + n : g + 2 * n]),
            (3, up.at[g + 2 * n : g + 3 * n], up.at[g + 3 * n :]),
            (-1, down.at[g : g + n], down.at[g + n : g + 2 * n]),
            (-3, down.at[g + 2 * n : g + 3 * n], down.at[g + 3 * n :]),
            (4, t4a.at[g:], t4b.at[g:]),
        ),
    )
    gain_out[...] = gain_rows


def terms(ids, normed_t, cot, heads, attended, shared, places):
    z = ids[0]
    for d, out_first, out_second in places:
        zt = (z + d + NZ) % NZ
        side, j = zt % 2, zt // 2
        rows = pl.ds(pl.multiple_of(j * HD, HD), HD)
        g_q = dot(normed_t[rows], heads[:, lanes(side * 2 * HD, 2 * HD)], 1, 0).astype(BF16)
        rows = pl.ds(pl.multiple_of(side * 2 * HD, 2 * HD), 2 * HD)
        g_o = dot(attended[rows], cot[:, lanes(j * HD)], 1, 0).astype(BF16)
        for half, out in enumerate((out_first, out_second)):
            out[:HD] = g_q[:, half * HD : (half + 1) * HD]
            out[HD : 2 * HD] = g_o[half * HD : (half + 1) * HD]
            part = shared[pl.ds(pl.multiple_of(j * HD + (2 * half + side) * PIECE, PIECE), PIECE), :].astype(BF16)
            out[2 * HD : 2 * HD + PIECE] = part[:, :HD]
            out[2 * HD + PIECE :] = part[:, HD:]


def near_kernel(ids, normed_t, cot, heads, attended, shared, t0, t2, m2):
    n = BLOCK
    terms(ids, normed_t, cot, heads, attended, shared, [(d, r.at[:n], r.at[n:]) for d, r in ((0, t0), (2, t2), (-2, m2))])


def relay_kernel(ids, t2, m2, a, b, c, d, gain_own, *refs):
    up, down, *back = refs[NX:]
    g, n = GROWS, BLOCK
    total = t2[...].astype(F32) + a[g + 2 * n :].astype(F32)
    up[:n] = (total[:n] + c[g:].astype(F32)).astype(BF16)
    up[n:] = total[n:].astype(BF16)
    total = m2[...].astype(F32) + b[g + 2 * n :].astype(F32)
    down[:n] = total[:n].astype(BF16)
    down[n:] = (total[n:] + d[g:].astype(F32)).astype(BF16)
    three = gain_own[...].astype(F32) + a[:g].astype(F32) + b[:g].astype(F32)
    five = three + c[:g].astype(F32) + d[:g].astype(F32)
    terms = []
    for rows in (five, three):
        value = rows[:4] + rows[4:8]
        high = value.astype(BF16).astype(F32)
        terms += [high, value - high]
    for j in range(4):
        rows = jnp.concatenate([t[j : j + 1] for t in terms] + [jnp.zeros((g - 4, HD), F32)], axis=0).astype(BF16)
        for ref in back:
            ref[HD:, j * HD : (j + 1) * HD] = rows


def finish_kernel(ids, t0, a, b, up, down, same, other):
    g, n = GROWS, BLOCK
    flip = ids[3]
    near = slice(g, g + 2 * n)
    total = t0[...].astype(F32) + a[near].astype(F32) + b[near].astype(F32)
    total = total + up[...].astype(F32) + down[...].astype(F32)
    same[...] = jnp.where(flip == 0, total[:n], total[n:]).astype(BF16)
    other[...] = jnp.where(flip == 0, total[n:], total[:n]).astype(BF16)


def gain_kernel(ids, *refs):
    out = refs[NX]
    for s in range(NX):
        rows = refs[s][HD:].astype(F32)
        for at in (0, 2):
            value = rows[at : at + 1] + rows[at + 1 : at + 2]
            for j in range(4):
                row = 2 * NX * at + 4 * s + j
                out[row : row + 1] = value[:, j * HD : (j + 1) * HD]


def input_kernel(width, ids, a, b, c, d, tokens, gain, total, row_sum, out):
    inv = lax.rsqrt(jnp.transpose(jnp.broadcast_to(total[...], (HD, HD))) / width + 1e-05)
    row_mean = jnp.transpose(jnp.broadcast_to(row_sum[...], (HD, HD))) / width
    for s, ref in enumerate((a, b, c, d)):
        at = (ids[4] + s) % NX

        @pl.loop(0, 4)
        def place(j, ref=ref, at=at):
            cols = lanes(feature(at, j))
            unit = tokens[:, cols].astype(F32) * inv
            scaled = ref[:HD, lanes(j * HD)].astype(F32) * gain[:, cols]
            out[:, cols] = inv * (scaled - unit * row_mean)


def owner_kernel(scale, ids, same, other, grad_query, grad_out):
    for grad, at in ((grad_query, slice(0, HD)), (grad_out, slice(HD, 2 * HD))):
        grad[...] = (same[at].astype(F32) + other[at].astype(F32)) * scale


def shared_kernel(ids, a, b, shared):
    shared[...] = (a[2 * HD :].astype(F32) + b[2 * HD :].astype(F32)).astype(BF16)


def join_kernel(scale, ids, own, by_c, by_yl, by_both, gains, grad_key, grad_value, grad_gain):
    yl, c, x = ids[1], ids[2], ids[4]
    for ref, at in ((own, 2 * yl + c), (by_c, 2 * yl + 1 - c), (by_yl, 2 - 2 * yl + c), (by_both, 3 - 2 * yl - c)):
        rows = pl.ds(pl.multiple_of(at * PIECE, PIECE), PIECE)
        grad_key[rows] = ref[:PIECE].astype(F32) * scale
        grad_value[rows] = ref[PIECE:].astype(F32) * scale
    for s in range(NX):
        at = (x + s) % NX
        for j in range(4):
            grad_gain[(1 - at % 2) * 8 + 2 * j + at // 2] = gains[4 * s + j : 4 * s + j + 1] * scale


def local(tokens, gain, w_query, w_key, w_value, w_out, cotangent):
    rows, quarter = tokens.shape
    sub = quarter // NX
    width = quarter * 4
    yh, x, z, yl, c = (lax.axis_index(a) for a in AXES)
    ids = jnp.stack([z, yl, c, yh, x]).astype(jnp.int32)
    head = yl * 2 + c
    loss_scale = 1.0 / math.sqrt(rows * 64)

    pack = jnp.concatenate(
        [
            w_query,
            w_out,
            lax.dynamic_slice_in_dim(w_key, head * PIECE, PIECE, 0),
            lax.dynamic_slice_in_dim(w_value, head * PIECE, PIECE, 0),
        ],
        axis=0,
    )
    same = lax.ppermute(pack, AXES, owner_perm(0))
    other = lax.ppermute(pack, AXES, owner_perm(1))
    part_shape = ((2 * rows + GROWS, sub), BF16)
    total, *parts = call(spread_kernel, [((1, rows), F32)] + [part_shape] * 4, [], ids, tokens, cotangent)
    total = total + swap(total, "c")
    same, other, total = lax.optimization_barrier((same, other, total))
    total = total + swap(total, "yl")
    both = jnp.where(yh == 0, jnp.concatenate([same, other]), jnp.concatenate([other, same]))
    prev2, next2 = shift_z(both, 2), shift_z(both, -2)
    double, half_shape = ((4 * BLOCK, HD), BF16), ((BLOCK, HD), BF16)
    relays = call(forward_pack_kernel, [double] * 2 + [half_shape] * 2, [], ids, both, prev2, next2)
    prev1, next1 = shift_z(relays[0], 1), shift_z(relays[1], -1)
    far_first, far_second = shift_z(relays[2], 2), shift_z(relays[3], -2)
    weights = (both, prev1, next1, prev2, next2, far_first, far_second)

    parts = call(stamp_kernel, [part_shape] * 4, [], ids, total, *parts, aliases={2 + s: s for s in range(4)})
    parts = [parts[0]] + [shift_x(parts[s], s) for s in range(1, NX)]
    gain_f = gain.astype(F32).reshape(1, quarter)
    unit_sw, normed_sw, cot_sw = call(
        normalize_kernel,
        [((512, sub), F32), ((512, sub), BF16), ((512, sub), BF16)],
        [],
        ids,
        *parts,
        gain_f,
        static=width,
    )

    *theirs, w_all, w_heads = call(
        theirs_kernel,
        [((rows, 5 * HD), F32)] * 4 + [((sub, 6 * HD), BF16), ((2, 2 * HD, sub), BF16)],
        [],
        ids,
        *weights,
        normed_sw,
        cot_sw,
    )
    got = [None] + [swap(theirs[s], "c") for s in range(1, NX)]
    got[0] = swap(theirs[0], "c")
    *mine, normed_t = call(
        mine_kernel,
        [((rows, 5 * HD), F32)] * 4 + [((sub, 512), BF16)],
        [],
        ids,
        normed_sw,
        cot_sw,
        w_all,
        w_heads,
    )
    split = ((rows, 8 * HD), BF16)
    chunks = [shift_x(call(chunk_kernel, [split], [], ids, mine[s], got[s])[0], -s) for s in range(1, NX)]
    (own,) = call(own_kernel, [((rows, 5 * HD), F32)], [], ids, mine[0], got[0])
    (partial,) = call(sum_kernel, [split], [], ids, own, *chunks)
    qa, kv = call(final_kernel, [((rows, 4 * HD), BF16), ((rows, HD), BF16)], [], ids, partial, swap(partial, "yl"))
    heads, row_sum = call(
        attend_kernel, [((rows, 6 * HD), BF16), ((1, rows), F32)], [], ids, qa, kv, swap(kv, "c")
    )
    row_sum = row_sum + swap(row_sum, "c")
    heads = [heads] + [shift_x(heads, s) for s in range(1, NX)]

    g, n = GROWS, BLOCK
    up, down, t4a, t4b, *back, gain_own, d_heads, attended_t, shared_terms = call(
        gradient_kernel,
        [((g + 4 * n, HD), BF16)] * 2
        + [((g + n, HD), BF16)] * 2
        + [((rows + g, sub), BF16)] * 4
        + [((g, HD), BF16), ((512, 6 * HD), BF16), ((4 * HD, 512), BF16), ((sub, 2 * HD), F32)],
        [],
        ids,
        *heads,
        *[swap(h, "c") for h in heads],
        normed_t,
        cot_sw,
        unit_sw,
        w_all,
    )
    t0, t2, m2 = call(
        near_kernel, [((2 * n, HD), BF16)] * 3, [], ids, normed_t, cot_sw, d_heads, attended_t, shared_terms
    )
    c4, d4 = shift_z(t4a, 2), shift_z(t4b, -2)
    a, b = shift_z(up, 1), shift_z(down, -1)
    a, row_sum = lax.optimization_barrier((a, row_sum))
    up, down, *back = call(
        relay_kernel,
        [((2 * n, HD), BF16)] * 2 + [((rows + g, sub), BF16)] * 4,
        [],
        ids,
        t2,
        m2,
        a,
        b,
        c4,
        d4,
        gain_own,
        *back,
        aliases={8 + s: 2 + s for s in range(NX)},
    )
    up, down = shift_z(up, 2), shift_z(down, -2)

    pieces = [back[0]] + [shift_x(back[s], -s) for s in range(1, NX)]
    to_same, to_other = call(finish_kernel, [((n, HD), BF16)] * 2, [], ids, t0, a, b, up, down)
    arrived = (lax.ppermute(to_same, AXES, inverse(owner_perm(0))), lax.ppermute(to_other, AXES, inverse(owner_perm(1))))
    (gain_z,) = call(gain_kernel, [((8 * NX, HD), F32)], [], ids, *pieces)
    gain_z = gain_z + swap(gain_z, "yh")
    (grad_input,) = call(
        input_kernel,
        [((rows, quarter), F32)],
        [],
        ids,
        *pieces,
        tokens,
        gain_f,
        total,
        row_sum,
        static=width,
    )
    *arrived, grad_input = lax.optimization_barrier((*arrived, grad_input))
    (shared_own,) = call(shared_kernel, [((2 * PIECE, HD), BF16)], [], ids, *arrived)
    grad_query, grad_out = call(owner_kernel, [((HD, HD), F32)] * 2, [], ids, *arrived, static=loss_scale)
    shared_yl = swap(shared_own, "yl")
    shared_yl, grad_query, grad_out = lax.optimization_barrier((shared_yl, grad_query, grad_out))
    gain_z = gain_z[: 4 * NX] + shift_z(gain_z[4 * NX :], 4)
    grad_key, grad_value, grad_gain = call(
        join_kernel,
        [((rows, HD), F32)] * 2 + [((4 * NX, 1, HD), F32)],
        [],
        ids,
        shared_own,
        swap(shared_own, "c"),
        shared_yl,
        swap(shared_yl, "c"),
        gain_z,
        static=loss_scale,
    )
    grad_gain = grad_gain.reshape(quarter)
    return (grad_input, grad_gain, grad_query, grad_key, grad_value, grad_out)


def solution(mesh):
    fine = Mesh(mesh.devices.reshape(2, NX, NZ, 2, 2), AXES)
    in_specs = (P(FSDP, TP), P(TP), P(FSDP, TP), P(FSDP, None), P(FSDP, None), P(TP, FSDP), P(FSDP, TP))
    out_specs = (P(FSDP, TP), P(TP), P(FSDP, TP), P(FSDP, None), P(FSDP, None), P(TP, FSDP))
    return jax.shard_map(local, mesh=fine, in_specs=in_specs, out_specs=out_specs, check_vma=False)
```

```python
import functools
import math

import jax
import jax.numpy as jnp
from jax import lax
from jax.experimental import pallas as pl
from jax.experimental.pallas import tpu as pltpu
from jax.sharding import Mesh, PartitionSpec as P

HD = 128
NX = 4
NZ = 8
AXES = ("yh", "x", "z", "yl", "c")
FSDP = ("yh", "x", "z")
TP = ("yl", "c")
F32 = jnp.float32
BF16 = jnp.bfloat16
PIECE = 32
BLOCK = 2 * HD + 2 * PIECE
GROWS = 16
VMEM = pl.BlockSpec(memory_space=pltpu.VMEM)
SMEM = pl.BlockSpec(memory_space=pltpu.SMEM)


def flat(yh, x, z, yl, c):
    return (((yh * NX + x) * NZ + z) * 2 + yl) * 2 + c


def owner_perm(flip):
    pairs = []
    for yh in range(2):
        for x in range(NX):
            for z in range(NZ):
                for yl in range(2):
                    for c in range(2):
                        dest_x = (z % 2) * 2 + 1 - x % 2
                        dest_z = (z // 2) * 2 + c
                        pairs.append((flat(yh, x, z, yl, c), flat(yl ^ flip, dest_x, dest_z, yh, x // 2)))
    return pairs


def inverse(pairs):
    return [(d, s) for s, d in pairs]


def shift_x(value, by):
    return lax.ppermute(value, "x", [(i, (i + by) % NX) for i in range(NX)])


def shift_z(value, by):
    return lax.ppermute(value, "z", [(i, (i + by) % NZ) for i in range(NZ)])


def swap(value, axis):
    return lax.ppermute(value, axis, [(0, 1), (1, 0)])


def dot(a, b, ca, cb):
    return lax.dot_general(a, b, (((ca,), (cb,)), ((), ())), preferred_element_type=F32)


def lanes(start, size=HD):
    return pl.ds(pl.multiple_of(start, HD), size)


def feature(at, j):
    return ((1 - at % 2) * 8 + 2 * j + at // 2) * HD


def call(body, outs, scratch, ids, *args, static=None, aliases={}):
    body = body if static is None else functools.partial(body, static)
    return pl.pallas_call(
        body,
        out_shape=[jax.ShapeDtypeStruct(s, d) for s, d in outs],
        in_specs=[SMEM] + [VMEM] * len(args),
        out_specs=[VMEM] * len(outs),
        input_output_aliases=aliases,
        scratch_shapes=[pltpu.VMEM(s, d) for s, d in scratch],
        compiler_params=pltpu.CompilerParams(vmem_limit_bytes=16 * 2**20),
    )(ids, *args)


def spread_kernel(ids, tokens, cot, total_out, *outs):
    rows = tokens.shape[0]
    squares = jnp.zeros((rows, HD), F32)
    for s in range(NX):
        at = (ids[4] + s) % NX

        def cut(j, squares, s=s, at=at):
            block, cols = lanes(feature(at, j)), lanes(j * HD)
            value = tokens[:, block]
            outs[s][:rows, cols] = value
            outs[s][rows : 2 * rows, cols] = cot[:, block]
            return squares + value.astype(F32) * value.astype(F32)

        squares = lax.fori_loop(0, 4, cut, squares)
    total_out[...] = jnp.sum(jnp.transpose(squares), axis=0, keepdims=True)


def stamp_kernel(ids, total, *refs):
    total = total[...]
    high = total.astype(BF16).astype(F32)
    middle = (total - high).astype(BF16).astype(F32)
    extra = jnp.concatenate([high, middle, total - high - middle, jnp.zeros((GROWS - 3, HD), F32)], axis=0)
    extra = jnp.concatenate([extra] * 4, axis=1).astype(BF16)
    for out in refs[NX:]:
        out[2 * HD :] = extra


def normalize_kernel(width, ids, *refs):
    parts, (gain, unit, normed, cot) = refs[:4], refs[4:]
    for s in range(NX):
        rows = slice(s * HD, (s + 1) * HD)
        terms = parts[s][2 * HD :, :HD].astype(F32)
        total = (terms[2:3] + terms[1:2]) + terms[0:1]
        column = jnp.transpose(jnp.broadcast_to(total, (HD, HD)))
        inv = lax.rsqrt(column / width + 1e-05)

        @pl.loop(0, 4)
        def scale(j, s=s, rows=rows, inv=inv):
            cols = lanes(j * HD)
            value = parts[s][:HD, cols].astype(F32) * inv
            unit[rows, cols] = value
            normed[rows, cols] = (value * gain[:, lanes(feature(ids[4], j))]).astype(BF16)

        cot[rows] = parts[s][HD : 2 * HD]


def forward_pack_kernel(ids, both, prev, after, up, down, far_first, far_second):
    for out, ref in ((up, prev), (down, after)):
        out[: 2 * BLOCK] = both[...]
        out[2 * BLOCK :] = ref[...]
    far_first[...] = prev[:BLOCK]
    far_second[...] = after[BLOCK:]


def product(outs, side, normed, cot, w_all, w_out):
    w_q = w_all[:, lanes(side * 2 * HD, 2 * HD)]
    w_kv = w_all[:, lanes((4 + side) * HD)]
    w_o = w_out[side]
    for r in range(0, 512, 256):
        rows = slice(r, r + 256)
        query = dot(normed[rows], w_q, 1, 0)
        attn_grad = dot(cot[rows], w_o, 1, 1)
        shared = dot(normed[rows], w_kv, 1, 0)
        for half in range(2):
            out, part = outs[r // HD + half], slice(half * HD, (half + 1) * HD)
            out[:, : 2 * HD] = query[part]
            out[:, 2 * HD : 4 * HD] = attn_grad[part]
            out[:, 4 * HD :] = shared[part]


def theirs_kernel(ids, both, prev1, next1, prev2, next2, far_first, far_second, normed, cot, *refs):
    outs, w_all, w_out = refs[:NX], refs[NX], refs[NX + 1]
    z, c = ids[0], ids[2]

    def place(ref, base, d, half):
        zt = (z + d + NZ) % NZ
        side, j = zt % 2, zt // 2

        def block(start, size, unit=PIECE):
            return pl.ds(pl.multiple_of(start, unit), size)

        w_all[block(j * HD, HD), lanes(side * 2 * HD + half * HD)] = ref[block(base, HD)]
        w_out[side, block(half * HD, HD, HD), lanes(j * HD)] = ref[block(base + HD, HD)]
        part = block(j * HD + (2 * half + side) * PIECE, PIECE)
        w_all[part, 4 * HD : 5 * HD] = ref[block(base + 2 * HD, PIECE)]
        w_all[part, 5 * HD : 6 * HD] = ref[block(base + 2 * HD + PIECE, PIECE)]

    for ref, base, d in (
        (both, 0, 0),
        (prev1, 0, -1),
        (prev1, 2 * BLOCK, -3),
        (next1, 0, 1),
        (next1, 2 * BLOCK, 3),
        (prev2, 0, -2),
        (next2, 0, 2),
    ):


        @pl.loop(0, 2)
        def both_halves(half, ref=ref, base=base, d=d):
            place(ref, base + half * BLOCK, d, half)

    place(far_first, 0, 4, 0)
    place(far_second, 0, 4, 1)
    product(outs, 1 - c, normed, cot, w_all, w_out)


def mine_kernel(ids, normed, cot, w_all, w_out, *refs):
    outs, normed_t = refs[:NX], refs[NX]
    product(outs, ids[2], normed, cot, w_all, w_out)
    for s in range(NX):
        for j in range(4):
            rows, cols = slice(s * HD, (s + 1) * HD), slice(j * HD, (j + 1) * HD)
            normed_t[cols, rows] = jnp.transpose(normed[rows, cols])


def split_store(ref, total):
    for start, size, at in ((0, 2 * HD, 0), (4 * HD, HD, 6 * HD)):
        value = total[:, start : start + size]
        high = value.astype(BF16)
        ref[:, at : at + size] = high
        ref[:, at + size : at + 2 * size] = (value - high.astype(F32)).astype(BF16)
    ref[:, 4 * HD : 6 * HD] = total[:, 2 * HD : 4 * HD].astype(BF16)


def joined(ref):
    value = ref[...].astype(F32)
    return jnp.concatenate(
        [
            value[:, : 2 * HD] + value[:, 2 * HD : 4 * HD],
            value[:, 4 * HD : 6 * HD],
            value[:, 6 * HD : 7 * HD] + value[:, 7 * HD :],
        ],
        axis=1,
    )


def chunk_kernel(ids, mine, got, out):
    split_store(out, mine[...] + got[...])


def own_kernel(ids, mine, got, out):
    out[...] = mine[...] + got[...]


def sum_kernel(ids, own, a, b, c, out):
    split_store(out, own[...] + joined(a) + joined(b) + joined(c))


def final_kernel(ids, mine, got, qa, kv):
    total = (joined(mine) + joined(got)).astype(BF16)
    qa[...] = total[:, : 4 * HD]
    kv[...] = total[:, 4 * HD :]


def attend_kernel(ids, qa, kv_mine, kv_theirs, out, row_out):
    first = ids[2] == 0
    mine, theirs = kv_mine[...].astype(F32), kv_theirs[...].astype(F32)
    key_rows = jnp.where(first, mine, theirs).astype(BF16)
    value_rows = jnp.where(first, theirs, mine).astype(BF16)
    causal = lax.broadcasted_iota(jnp.int32, (HD, HD), 0) >= lax.broadcasted_iota(jnp.int32, (HD, HD), 1)
    keys = jnp.zeros((HD, HD), F32)
    values = jnp.zeros((HD, HD), F32)
    row_terms = jnp.zeros((HD, HD), F32)
    for h in range(2):
        query = qa[:, h * HD : (h + 1) * HD]
        attn_grad = qa[:, (2 + h) * HD : (3 + h) * HD]
        scores = dot(query, key_rows, 1, 1) * HD ** (-0.5)
        scores = jnp.where(causal, scores, jnp.float32(-1e30))
        shifted = jnp.exp(scores - jnp.max(scores, axis=-1, keepdims=True))
        softmax_out = shifted / jnp.sum(shifted, axis=-1, keepdims=True)
        rounded = softmax_out.astype(BF16)
        dprob = dot(attn_grad, value_rows, 1, 1)
        dscore = softmax_out * (dprob - jnp.sum(dprob * softmax_out, axis=-1, keepdims=True)) * HD ** (-0.5)
        dscore = dscore.astype(BF16)
        d_query = dot(dscore, key_rows, 1, 0).astype(BF16)
        out[:, h * HD : (h + 1) * HD] = d_query
        row_terms = row_terms + d_query.astype(F32) * query.astype(F32)
        out[:, (2 + h) * HD : (3 + h) * HD] = dot(rounded, value_rows, 1, 0).astype(BF16)
        keys = keys + dot(dscore, query, 0, 0).astype(BF16).astype(F32)
        values = values + dot(rounded, attn_grad, 0, 0).astype(BF16).astype(F32)
    out[:, 4 * HD : 5 * HD] = keys.astype(BF16)
    out[:, 5 * HD :] = values.astype(BF16)
    row_terms = row_terms + keys * key_rows.astype(F32) + values * value_rows.astype(F32)
    row_out[...] = jnp.sum(jnp.transpose(row_terms), axis=0, keepdims=True)


def gradient_kernel(ids, *refs):
    mine, theirs, (normed_t, cot, unit, w_all) = refs[:4], refs[4:8], refs[8:12]
    (up, down, t4a, t4b), back, (gain_out, heads, attended, shared) = refs[12:16], refs[16:20], refs[20:]
    c = ids[2]
    for s in range(NX):
        rows = slice(s * HD, (s + 1) * HD)
        for ref, side in ((mine[s], c), (theirs[s], 1 - c)):
            heads[rows, lanes(side * 2 * HD, 2 * HD)] = ref[:, : 2 * HD]
            for half in range(2):
                at = pl.ds(pl.multiple_of((2 * side + half) * HD, HD), HD)
                attended[at, rows] = jnp.transpose(ref[:, (2 + half) * HD : (3 + half) * HD])
        total = mine[s][:, 4 * HD :].astype(F32) + theirs[s][:, 4 * HD :].astype(F32)
        heads[rows, 4 * HD :] = total.astype(BF16)

    gain_sum = jnp.zeros((1, 4 * HD), F32)
    for s in range(NX):
        rows = slice(s * HD, (s + 1) * HD)
        term = dot(heads[rows], w_all[...], 1, 1)
        back[s][:HD] = term.astype(BF16)
        gain_sum = gain_sum + jnp.sum(term * unit[rows], axis=0, keepdims=True)
    gain_rows = jnp.concatenate([gain_sum[:, j * HD : (j + 1) * HD] for j in range(4)], axis=0)
    high = gain_rows.astype(BF16).astype(F32)
    gain_rows = jnp.concatenate([high, gain_rows - high, jnp.zeros((8, HD), F32)], axis=0).astype(BF16)

    shared[...] = dot(normed_t[...], heads[:, 4 * HD :], 1, 0)
    g, n = GROWS, BLOCK
    for ref in (up, down, t4a, t4b):
        ref[:g] = gain_rows
    terms(
        ids,
        normed_t,
        cot,
        heads,
        attended,
        shared,
        (
            (1, up.at[g : g + n], up.at[g + n : g + 2 * n]),
            (3, up.at[g + 2 * n : g + 3 * n], up.at[g + 3 * n :]),
            (-1, down.at[g : g + n], down.at[g + n : g + 2 * n]),
            (-3, down.at[g + 2 * n : g + 3 * n], down.at[g + 3 * n :]),
            (4, t4a.at[g:], t4b.at[g:]),
        ),
    )
    gain_out[...] = gain_rows


def terms(ids, normed_t, cot, heads, attended, shared, places):
    z = ids[0]
    for d, out_first, out_second in places:
        zt = (z + d + NZ) % NZ
        side, j = zt % 2, zt // 2
        rows = pl.ds(pl.multiple_of(j * HD, HD), HD)
        g_q = dot(normed_t[rows], heads[:, lanes(side * 2 * HD, 2 * HD)], 1, 0).astype(BF16)
        rows = pl.ds(pl.multiple_of(side * 2 * HD, 2 * HD), 2 * HD)
        g_o = dot(attended[rows], cot[:, lanes(j * HD)], 1, 0).astype(BF16)
        for half, out in enumerate((out_first, out_second)):
            out[:HD] = g_q[:, half * HD : (half + 1) * HD]
            out[HD : 2 * HD] = g_o[half * HD : (half + 1) * HD]
            part = shared[pl.ds(pl.multiple_of(j * HD + (2 * half + side) * PIECE, PIECE), PIECE), :].astype(BF16)
            out[2 * HD : 2 * HD + PIECE] = part[:, :HD]
            out[2 * HD + PIECE :] = part[:, HD:]


def near_kernel(ids, normed_t, cot, heads, attended, shared, t0, t2, m2):
    n = BLOCK
    terms(ids, normed_t, cot, heads, attended, shared, [(d, r.at[:n], r.at[n:]) for d, r in ((0, t0), (2, t2), (-2, m2))])


def relay_kernel(ids, t2, m2, a, b, c, d, gain_own, *refs):
    up, down, *back = refs[NX:]
    g, n = GROWS, BLOCK
    total = t2[...].astype(F32) + a[g + 2 * n :].astype(F32)
    up[:n] = (total[:n] + c[g:].astype(F32)).astype(BF16)
    up[n:] = total[n:].astype(BF16)
    total = m2[...].astype(F32) + b[g + 2 * n :].astype(F32)
    down[:n] = total[:n].astype(BF16)
    down[n:] = (total[n:] + d[g:].astype(F32)).astype(BF16)
    three = gain_own[...].astype(F32) + a[:g].astype(F32) + b[:g].astype(F32)
    five = three + c[:g].astype(F32) + d[:g].astype(F32)
    terms = []
    for rows in (five, three):
        value = rows[:4] + rows[4:8]
        high = value.astype(BF16).astype(F32)
        terms += [high, value - high]
    for j in range(4):
        rows = jnp.concatenate([t[j : j + 1] for t in terms] + [jnp.zeros((g - 4, HD), F32)], axis=0).astype(BF16)
        for ref in back:
            ref[HD:, j * HD : (j + 1) * HD] = rows


def finish_kernel(ids, t0, a, b, up, down, same, other):
    g, n = GROWS, BLOCK
    flip = ids[3]
    near = slice(g, g + 2 * n)
    total = t0[...].astype(F32) + a[near].astype(F32) + b[near].astype(F32)
    total = total + up[...].astype(F32) + down[...].astype(F32)
    same[...] = jnp.where(flip == 0, total[:n], total[n:]).astype(BF16)
    other[...] = jnp.where(flip == 0, total[n:], total[:n]).astype(BF16)


def gain_kernel(ids, *refs):
    out = refs[NX]
    for s in range(NX):
        rows = refs[s][HD:].astype(F32)
        for at in (0, 2):
            value = rows[at : at + 1] + rows[at + 1 : at + 2]
            for j in range(4):
                row = 2 * NX * at + 4 * s + j
                out[row : row + 1] = value[:, j * HD : (j + 1) * HD]


def input_kernel(width, ids, a, b, c, d, tokens, gain, total, row_sum, out):
    inv = lax.rsqrt(jnp.transpose(jnp.broadcast_to(total[...], (HD, HD))) / width + 1e-05)
    row_mean = jnp.transpose(jnp.broadcast_to(row_sum[...], (HD, HD))) / width
    for s, ref in enumerate((a, b, c, d)):
        at = (ids[4] + s) % NX

        @pl.loop(0, 4)
        def place(j, ref=ref, at=at):
            cols = lanes(feature(at, j))
            unit = tokens[:, cols].astype(F32) * inv
            scaled = ref[:HD, lanes(j * HD)].astype(F32) * gain[:, cols]
            out[:, cols] = inv * (scaled - unit * row_mean)


def owner_kernel(scale, ids, same, other, grad_query, grad_out):
    for grad, at in ((grad_query, slice(0, HD)), (grad_out, slice(HD, 2 * HD))):
        grad[...] = (same[at].astype(F32) + other[at].astype(F32)) * scale


def shared_kernel(ids, a, b, shared):
    shared[...] = (a[2 * HD :].astype(F32) + b[2 * HD :].astype(F32)).astype(BF16)


def join_kernel(scale, ids, own, by_c, by_yl, by_both, gains, grad_key, grad_value, grad_gain):
    yl, c, x = ids[1], ids[2], ids[4]
    for ref, at in ((own, 2 * yl + c), (by_c, 2 * yl + 1 - c), (by_yl, 2 - 2 * yl + c), (by_both, 3 - 2 * yl - c)):
        rows = pl.ds(pl.multiple_of(at * PIECE, PIECE), PIECE)
        grad_key[rows] = ref[:PIECE].astype(F32) * scale
        grad_value[rows] = ref[PIECE:].astype(F32) * scale
    for s in range(NX):
        at = (x + s) % NX
        for j in range(4):
            grad_gain[(1 - at % 2) * 8 + 2 * j + at // 2] = gains[4 * s + j : 4 * s + j + 1] * scale


def local(tokens, gain, w_query, w_key, w_value, w_out, cotangent):
    rows, quarter = tokens.shape
    sub = quarter // NX
    width = quarter * 4
    yh, x, z, yl, c = (lax.axis_index(a) for a in AXES)
    ids = jnp.stack([z, yl, c, yh, x]).astype(jnp.int32)
    head = yl * 2 + c
    loss_scale = 1.0 / math.sqrt(rows * 64)

    pack = jnp.concatenate(
        [
            w_query,
            w_out,
            lax.dynamic_slice_in_dim(w_key, head * PIECE, PIECE, 0),
            lax.dynamic_slice_in_dim(w_value, head * PIECE, PIECE, 0),
        ],
        axis=0,
    )
    same = lax.ppermute(pack, AXES, owner_perm(0))
    other = lax.ppermute(pack, AXES, owner_perm(1))
    part_shape = ((2 * rows + GROWS, sub), BF16)
    total, *parts = call(spread_kernel, [((1, rows), F32)] + [part_shape] * 4, [], ids, tokens, cotangent)
    total = total + swap(total, "c")
    same, other, total = lax.optimization_barrier((same, other, total))
    total = total + swap(total, "yl")
    both = jnp.where(yh == 0, jnp.concatenate([same, other]), jnp.concatenate([other, same]))
    prev2, next2 = shift_z(both, 2), shift_z(both, -2)
    double, half_shape = ((4 * BLOCK, HD), BF16), ((BLOCK, HD), BF16)
    relays = call(forward_pack_kernel, [double] * 2 + [half_shape] * 2, [], ids, both, prev2, next2)
    prev1, next1 = shift_z(relays[0], 1), shift_z(relays[1], -1)
    far_first, far_second = shift_z(relays[2], 2), shift_z(relays[3], -2)
    weights = (both, prev1, next1, prev2, next2, far_first, far_second)

    parts = call(stamp_kernel, [part_shape] * 4, [], ids, total, *parts, aliases={2 + s: s for s in range(4)})
    parts = [parts[0]] + [shift_x(parts[s], s) for s in range(1, NX)]
    gain_f = gain.astype(F32).reshape(1, quarter)
    unit_sw, normed_sw, cot_sw = call(
        normalize_kernel,
        [((512, sub), F32), ((512, sub), BF16), ((512, sub), BF16)],
        [],
        ids,
        *parts,
        gain_f,
        static=width,
    )

    *theirs, w_all, w_heads = call(
        theirs_kernel,
        [((rows, 5 * HD), F32)] * 4 + [((sub, 6 * HD), BF16), ((2, 2 * HD, sub), BF16)],
        [],
        ids,
        *weights,
        normed_sw,
        cot_sw,
    )
    got = [None] + [swap(theirs[s], "c") for s in range(1, NX)]
    got[0] = swap(theirs[0], "c")
    *mine, normed_t = call(
        mine_kernel,
        [((rows, 5 * HD), F32)] * 4 + [((sub, 512), BF16)],
        [],
        ids,
        normed_sw,
        cot_sw,
        w_all,
        w_heads,
    )
    split = ((rows, 8 * HD), BF16)
    chunks = [shift_x(call(chunk_kernel, [split], [], ids, mine[s], got[s])[0], -s) for s in range(1, NX)]
    (own,) = call(own_kernel, [((rows, 5 * HD), F32)], [], ids, mine[0], got[0])
    (partial,) = call(sum_kernel, [split], [], ids, own, *chunks)
    qa, kv = call(final_kernel, [((rows, 4 * HD), BF16), ((rows, HD), BF16)], [], ids, partial, swap(partial, "yl"))
    heads, row_sum = call(
        attend_kernel, [((rows, 6 * HD), BF16), ((1, rows), F32)], [], ids, qa, kv, swap(kv, "c")
    )
    row_sum = row_sum + swap(row_sum, "c")
    heads = [heads] + [shift_x(heads, s) for s in range(1, NX)]

    g, n = GROWS, BLOCK
    up, down, t4a, t4b, *back, gain_own, d_heads, attended_t, shared_terms = call(
        gradient_kernel,
        [((g + 4 * n, HD), BF16)] * 2
        + [((g + n, HD), BF16)] * 2
        + [((rows + g, sub), BF16)] * 4
        + [((g, HD), BF16), ((512, 6 * HD), BF16), ((4 * HD, 512), BF16), ((sub, 2 * HD), F32)],
        [],
        ids,
        *heads,
        *[swap(h, "c") for h in heads],
        normed_t,
        cot_sw,
        unit_sw,
        w_all,
    )
    t0, t2, m2 = call(
        near_kernel, [((2 * n, HD), BF16)] * 3, [], ids, normed_t, cot_sw, d_heads, attended_t, shared_terms
    )
    c4, d4 = shift_z(t4a, 2), shift_z(t4b, -2)
    a, b = shift_z(up, 1), shift_z(down, -1)
    a, row_sum = lax.optimization_barrier((a, row_sum))
    up, down, *back = call(
        relay_kernel,
        [((2 * n, HD), BF16)] * 2 + [((rows + g, sub), BF16)] * 4,
        [],
        ids,
        t2,
        m2,
        a,
        b,
        c4,
        d4,
        gain_own,
        *back,
        aliases={8 + s: 2 + s for s in range(NX)},
    )
    up, down = shift_z(up, 2), shift_z(down, -2)

    pieces = [back[0]] + [shift_x(back[s], -s) for s in range(1, NX)]
    to_same, to_other = call(finish_kernel, [((n, HD), BF16)] * 2, [], ids, t0, a, b, up, down)
    arrived = (lax.ppermute(to_same, AXES, inverse(owner_perm(0))), lax.ppermute(to_other, AXES, inverse(owner_perm(1))))
    (gain_z,) = call(gain_kernel, [((8 * NX, HD), F32)], [], ids, *pieces)
    gain_z = gain_z + swap(gain_z, "yh")
    (grad_input,) = call(
        input_kernel,
        [((rows, quarter), F32)],
        [],
        ids,
        *pieces,
        tokens,
        gain_f,
        total,
        row_sum,
        static=width,
    )
    (shared_own,) = call(shared_kernel, [((2 * PIECE, HD), BF16)], [], ids, *arrived)
    grad_query, grad_out = call(owner_kernel, [((HD, HD), F32)] * 2, [], ids, *arrived, static=loss_scale)
    shared_yl = swap(shared_own, "yl")
    shared_yl, grad_input, grad_query, grad_out = lax.optimization_barrier(
        (shared_yl, grad_input, grad_query, grad_out)
    )
    gain_z = gain_z[: 4 * NX] + shift_z(gain_z[4 * NX :], 4)
    grad_key, grad_value, grad_gain = call(
        join_kernel,
        [((rows, HD), F32)] * 2 + [((4 * NX, 1, HD), F32)],
        [],
        ids,
        shared_own,
        swap(shared_own, "c"),
        shared_yl,
        swap(shared_yl, "c"),
        gain_z,
        static=loss_scale,
    )
    grad_gain = grad_gain.reshape(quarter)
    return (grad_input, grad_gain, grad_query, grad_key, grad_value, grad_out)


def solution(mesh):
    fine = Mesh(mesh.devices.reshape(2, NX, NZ, 2, 2), AXES)
    in_specs = (P(FSDP, TP), P(TP), P(FSDP, TP), P(FSDP, None), P(FSDP, None), P(TP, FSDP), P(FSDP, TP))
    out_specs = (P(FSDP, TP), P(TP), P(FSDP, TP), P(FSDP, None), P(FSDP, None), P(TP, FSDP))
    return jax.shard_map(local, mesh=fine, in_specs=in_specs, out_specs=out_specs, check_vma=False)
```
